256 devices in a mesh: row: 8 (over z), col: 32 (over x, y, core).
Axes of the slice: x: 4, y: 4, z: 8, core: 2. Of those that a mesh axis runs over, the one named last changes fastest.
Arguments:
- schur_blocks: bfloat16 [8, 32, 2048, 2048], P('row', 'col'), as said below
- rigid_modes: float32 [8, 32, 6, 2048], P('row', 'col'), may hold values from -0.125 to 0.125
- floating: int32 [8, 32], P('row', 'col'), may hold values 0 or 1
- block_order: int32 [8, 32, 16], P('row', 'col'), may hold values from 0 to 15, each once within a row
- coarse_inverse: float32 [6, 8, 32, 6, 8, 32], P(None, 'row', None, None, None, 'col'), may hold values from -4 to 4
- right_side: float32 [8, 32, 2, 128, 512], P('row', 'col')
Outputs:
- multipliers: float32 [8, 32, 2, 128, 512], P('row', 'col')
- residual: float32 [8, 32, 2, 128, 512], P('row', 'col')
The draws below stay inside these ranges and needn't reach their ends.
Inputs may be any that keep to these rules, and one draw needn't show every extreme that they name: `schur_blocks`: each subdomain's matrix is symmetric. `block_order`: each subdomain's 16 entries name every block of its face order once.
All inputs are finite; a program needn't handle non-finite values. No bound on the sum of `floating` on one device may be relied on, other than what follows from the above.
Results may differ from the reference program's by a relative error of at most 0.0003.
Values sent between devices are 32-bit elements; how exact they have to be, the bound alone decides.
No kernel may reach another device: no remote copies, remote signals or barrier semaphores. Data moves between devices by JAX's collectives and lax.ppermute only.
A program may use at most 128 MiB of HBM per device.

```python
import math
import jax
import jax.numpy as jnp
from jax import lax

M = 512
NS = 2048
BLK = 128
NB = 16
MODES = 6
RHS = 128
ITERS = 3
ROWS = 8
COLS = 32


def draw_schur_blocks(key, part):
    key = jax.random.fold_in(key, 11)
    key_pairs, key_diag = jax.random.split(key)
    full_shape = (ROWS, COLS, NS, NS)
    pairs_raw = jnp.clip(jax.random.normal(key_pairs, full_shape, jnp.float32), -4.0, 4.0)
    diagonal = jax.random.uniform(key_diag, (ROWS, COLS, NS), jnp.float32, 1.0, 2.5)
    coupled = (pairs_raw + jnp.swapaxes(pairs_raw, 2, 3)) * (0.35 / math.sqrt(2.0 * NS))
    labels = jnp.arange(NS)
    on_diag = labels[:, None] == labels[None, :]
    matrices = jnp.where(on_diag[None, None], diagonal[:, :, :, None], coupled)
    return matrices.astype(jnp.bfloat16)


def draw_right_side(key, part):
    key = jax.random.fold_in(key, 23)
    key_noise, key_cells = jax.random.split(key)
    full_shape = (ROWS, COLS, 2, RHS, M)
    position = (jnp.arange(ROWS)[:, None] * COLS + jnp.arange(COLS)[None, :]).astype(jnp.float32) / max(ROWS * COLS - 1, 1)
    columns = jnp.exp(math.log(10.0) * jnp.arange(RHS).astype(jnp.float32) / max(RHS - 1, 1)) / math.sqrt(10.0)
    cell_scale = jnp.exp(jax.random.uniform(key_cells, full_shape, jnp.float32, 0.0, math.log(10.0))) / math.sqrt(10.0)
    noise_part = jnp.clip(jax.random.normal(key_noise, full_shape, jnp.float32), -4.0, 4.0)
    device_ramp = 1.0 + 2.0 * position
    values = noise_part * cell_scale * device_ramp[:, :, None, None, None] * columns[None, None, None, :, None] * 0.5
    return values.astype(jnp.float32)


def set_ends(values, stream_key, least, largest):
    longest = values.shape.index(max(values.shape))
    spots = []
    for shift in (0, 1):
        where = [jax.random.randint(jax.random.fold_in(stream_key, axis), (), 0, length) for axis, length in enumerate(values.shape)]
        where[longest] = (where[longest] + shift) % values.shape[longest]
        spots.append(tuple(where))
    return values.at[spots[0]].set(least).at[spots[1]].set(largest)


def with_spikes(array, rng, source, target, blocks, factor):
    owner, partner = [(jnp.arange(array.shape[axis_at]) // (array.shape[axis_at] // blocks)).reshape([-1 if axis == axis_at else 1 for axis in range(array.ndim)]) for axis_at in (source, target)]
    chosen = jax.random.permutation(rng, blocks)[partner]
    strong = (owner == chosen) | (owner == (partner + blocks // 2) % blocks)
    return jnp.where(strong, factor * array, array)


def block_scale(key, extent, cuts, low, top_value):
    def one(axis_at, shards_of):
        draws = jax.random.uniform(jax.random.fold_in(jax.random.fold_in(key, 6), axis_at), (shards_of,), jnp.float32, low / len(cuts), top_value / len(cuts))
        return jnp.repeat(jnp.exp(draws), extent[axis_at] // shards_of).reshape((-1,) + (1,) * (len(extent) - axis_at - 1))

    factor_of = one(*cuts[0])
    for cut in cuts[1:]:
        factor_of = factor_of * one(*cut)
    return factor_of


def scatter_about(rng, extent, scale, most, cuts=(), kind=jnp.bfloat16):
    entries = scale * jax.random.normal(rng, extent, jnp.float32)
    if cuts:
        entries = entries * block_scale(rng, extent, cuts, -0.22, 0.18)
    return jnp.clip(entries, -most, most).astype(kind)


def gaussian_with(rng, extent, deviation, reach, cuts, heavy, kind=jnp.bfloat16):
    values = deviation * jax.random.normal(rng, extent, jnp.float32)
    if cuts:
        values = values * block_scale(rng, extent, cuts, -0.22, 0.18)
    return jnp.clip(with_spikes(values, jax.random.fold_in(rng, 3), *heavy), -reach, reach).astype(kind)


def setup_inputs(seed: int = 0) -> dict:
    arg_keys = jax.random.split(jax.random.key(seed), 7)
    schur_blocks = draw_schur_blocks(jax.random.fold_in(arg_keys[6], 71), 0)
    rigid_modes = scatter_about(arg_keys[1], (ROWS, COLS, MODES, NS), NS ** -0.5, 0.125, ((0, 8), (1, 32)), jnp.float32)
    floating = set_ends((jax.random.randint(arg_keys[2], (ROWS, COLS), 0, 4) < 3).astype(jnp.int32), jax.random.fold_in(arg_keys[2], 1), 0, 1)
    block_order = jax.vmap(lambda own: jax.random.permutation(own, NB))(jax.random.split(arg_keys[3], ROWS * COLS)).reshape((ROWS, COLS, NB)).astype(jnp.int32)
    coarse_inverse = gaussian_with(arg_keys[4], (MODES, ROWS, COLS, MODES, ROWS, COLS), 0.15, 4.0, ((1, 8), (5, 32)), (5, 2, 32, 2.75), jnp.float32)
    right_side = draw_right_side(jax.random.fold_in(arg_keys[6], 71), 0)
    return dict(schur_blocks=schur_blocks, rigid_modes=rigid_modes, floating=floating, block_order=block_order, coarse_inverse=coarse_inverse, right_side=right_side)


highest = lax.Precision.HIGHEST


def from_lower(values, along):
    zero_rim = jnp.zeros_like(lax.slice_in_dim(values, 0, 1, axis=along))
    kept_part = lax.slice_in_dim(values, 0, values.shape[along] - 1, axis=along)
    return jnp.concatenate([zero_rim, kept_part], axis=along)


def from_upper(values, along):
    zero_rim = jnp.zeros_like(lax.slice_in_dim(values, 0, 1, axis=along))
    kept_part = lax.slice_in_dim(values, 1, values.shape[along], axis=along)
    return jnp.concatenate([kept_part, zero_rim], axis=along)


def local_copy(vector):
    south_face = vector[:, :, 0]
    east_face = vector[:, :, 1]
    stacked = jnp.stack([-from_lower(south_face, 0), south_face, -from_lower(east_face, 1), east_face], axis=3)
    return stacked.reshape(ROWS, COLS, RHS, NS)


def assemble(spread):
    face_stack = spread.reshape(ROWS, COLS, RHS, 4, M)
    south_edge = face_stack[:, :, :, 1] - from_upper(face_stack[:, :, :, 0], 0)
    east_edge = face_stack[:, :, :, 3] - from_upper(face_stack[:, :, :, 2], 1)
    return jnp.stack([south_edge, east_edge], axis=2)


def per_domain(operands):
    local_vector, matrix, block_perm = operands
    labels = jnp.arange(NB, dtype=jnp.int32)
    inverse = jnp.sum(labels[:, None] * (block_perm[:, None] == labels[None, :]).astype(jnp.int32), axis=0).astype(jnp.int32)
    permuted = jnp.take(local_vector, block_perm, axis=1).reshape(RHS, NS)
    product = jnp.dot(permuted, matrix.astype(jnp.float32), precision=highest, preferred_element_type=jnp.float32).reshape(RHS, NB, BLK)
    return jnp.take(product, inverse, axis=1).reshape(RHS, NS)


def apply_schur(direction, schur_blocks, block_order):
    copies = local_copy(direction).reshape(ROWS * COLS, RHS, NB, BLK)
    matrices = schur_blocks.reshape(ROWS * COLS, NS, NS)
    orders = block_order.reshape(ROWS * COLS, NB)
    images = lax.map(per_domain, (copies, matrices, orders))
    return assemble(images.reshape(ROWS, COLS, RHS, NS))


def correction(vector, rigid_used, coarse_inverse):
    copies = local_copy(vector)
    coarse_rhs = jnp.einsum('rcan,rckn->rcak', rigid_used, copies, precision=highest)
    coarse_values = jnp.einsum('aijbuv,uvbk->ijak', coarse_inverse, coarse_rhs, precision=highest)
    spread = jnp.einsum('rcak,rcan->rckn', coarse_values, rigid_used, precision=highest)
    return assemble(spread)


def reference(schur_blocks, rigid_modes, floating, block_order, coarse_inverse, right_side):
    rigid_used = rigid_modes * floating.astype(jnp.float32)[:, :, None, None]
    residual = right_side - correction(right_side, rigid_used, coarse_inverse)
    multipliers = jnp.zeros_like(right_side)
    direction = residual
    norm_now = jnp.sum(residual * residual, axis=(0, 1, 2, 4))
    for iteration in range(ITERS):
        image = apply_schur(direction, schur_blocks, block_order)
        curvature = jnp.sum(direction * image, axis=(0, 1, 2, 4))
        projected = image - correction(image, rigid_used, coarse_inverse)
        step_size = (norm_now / curvature)[:, None]
        multipliers = multipliers + step_size * direction
        residual = residual - step_size * projected
        norm_next = jnp.sum(residual * residual, axis=(0, 1, 2, 4))
        direction = residual + (norm_next / norm_now)[:, None] * direction
        norm_now = norm_next
    return multipliers, residual
```

```python
import functools

import jax
import jax.numpy as jnp
from jax import lax
from jax.experimental import pallas as pl
from jax.experimental.pallas import tpu as pltpu
from jax.sharding import PartitionSpec as P

M = 512
NS = 2048
BLK = 128
NB = 16
K = 128
ROWS = 8
COLS = 32
MODES = 6
ITERS = 3
SLOT = 8
SLOTS = 5
PAY = 48
TERMS = ((0, 0), (0, 1), (1, 0), (1, 1), (0, 2), (2, 0))
TALL = 512

f32 = jnp.float32
bf16 = jnp.bfloat16
highest = lax.Precision.HIGHEST
VM = pl.BlockSpec(memory_space=pltpu.VMEM)
SM = pl.BlockSpec(memory_space=pltpu.SMEM)
LIMIT = pltpu.CompilerParams(vmem_limit_bytes=40 * 1024 * 1024)


def cyclic(value, axis, steps):
    count = lax.axis_size(axis)
    return lax.ppermute(value, axis, [(s, (s + steps) % count) for s in range(count)])


def shifted(value, axis, steps):
    count = lax.axis_size(axis)
    initial, last = (max(0, -steps), min(count, count - steps))
    return lax.ppermute(value, axis, [(s, s + steps) for s in range(initial, last)])


def swapped(value, partner):
    return lax.ppermute(value, "col", [(s, partner(s)) for s in range(COLS)])


def parts_of(value, count):
    pieces = []
    for _ in range(count):
        piece = value.astype(bf16)
        pieces.append(piece)
        value = value - piece.astype(f32)
    return pieces


def pay_from(bgt, halves, pay):
    d = jnp.dot(bgt[...], halves[...], preferred_element_type=f32)
    pay[...] = (
        d[0:PAY, :K] + d[0:PAY, K:] + d[PAY : 2 * PAY, :K] + d[PAY : 2 * PAY, K:] + d[2 * PAY :, :K]
    )


def modes_kernel(masks, own, near_n, near_s, near_w, near_e, side, bgt, south, east, pay, full, halves):
    full[...] = jnp.zeros_like(full)
    full[0:MODES, 0:M] = own[:, 0:M] * masks[0]
    full[0:MODES, M : 2 * M] = own[:, M : 2 * M]
    full[0:MODES, 2 * M : 3 * M] = own[:, 2 * M : 3 * M] * masks[2]
    full[0:MODES, 3 * M :] = own[:, 3 * M :]
    for slot, near in enumerate((near_n, near_s, near_w, near_e)):
        full[SLOT * (slot + 1) : SLOT * (slot + 1) + MODES, M * slot : M * (slot + 1)] = -near[...]
    for index, piece in enumerate(parts_of(full[...], 3)):
        bgt[PAY * index : PAY * (index + 1), :] = piece
    halves[...] = jnp.zeros_like(halves)
    for face, out, at in ((0, south, M), (1, east, 3 * M)):
        for block in range(M // BLK):
            turned = side[face, :, BLK * block : BLK * (block + 1)].T
            out[BLK * block : BLK * (block + 1), :] = turned
            high, low = parts_of(turned, 2)
            halves[at + BLK * block : at + BLK * (block + 1), :K] = high
            halves[at + BLK * block : at + BLK * (block + 1), K:] = low
    pay_from(bgt, halves, pay)


def spread_kernel(bgt, bgc, turned):
    for index, (left, _) in enumerate(TERMS):
        rows = bgt[PAY * left : PAY * (left + 1), :].astype(f32)
        turned[40 * index : 40 * (index + 1), :] = rows[0:40]
    turned[240:256, :] = jnp.zeros((16, NS), f32)
    for block in range(NB):
        for half in range(2):
            piece = turned[BLK * half : BLK * (half + 1), BLK * block : BLK * (block + 1)].T
            bgc[BLK * block : BLK * (block + 1), BLK * half : BLK * (half + 1)] = piece.astype(bf16)


def stack_weights(weights, stack):
    pieces = parts_of(weights[...], 3)
    for index, (_, right) in enumerate(TERMS):
        stack[40 * index : 40 * (index + 1), :] = pieces[right].astype(f32)
    stack[240:256, :] = jnp.zeros((16, K), f32)
    return stack[...].astype(bf16)


def schur_product(order, matrix, vector, halves, product):
    for block in range(NB):
        at = pl.multiple_of(order[block] * BLK, BLK)
        high, low = parts_of(vector[pl.ds(at, BLK), :], 2)
        halves[BLK * block : BLK * (block + 1), :K] = high
        halves[BLK * block : BLK * (block + 1), K:] = low

    @pl.loop(0, NS // TALL)
    def _(step):
        rows = matrix[pl.ds(pl.multiple_of(step * TALL, TALL), TALL), :]
        both = jnp.dot(rows, halves[...], preferred_element_type=f32)
        both = both[:, :K] + both[:, K:]
        for piece in range(TALL // BLK):
            at = pl.multiple_of(order[step * (TALL // BLK) + piece] * BLK, BLK)
            product[pl.ds(at, BLK), :] = both[BLK * piece : BLK * (piece + 1)]


def finish(order, matrix, bgt, residual, image, faces, pay, halves, product):
    schur_product(order, matrix, residual, halves, product)
    norm = jnp.zeros((1, K), f32)
    energy = jnp.zeros((1, K), f32)
    cross = jnp.zeros((1, K), f32)
    for face in range(4):
        for block in range(M // BLK):
            inside = slice(BLK * block, BLK * (block + 1))
            rows = slice(M * face + BLK * block, M * face + BLK * (block + 1))
            r = residual[rows, :]
            y = product[rows, :]
            faces[face][inside, :] = y
            high, low = parts_of(y, 2)
            halves[rows, :K] = high
            halves[rows, K:] = low
            energy = energy + jnp.sum(r * y, axis=0, keepdims=True)
            if face % 2:
                norm = norm + jnp.sum(r * r, axis=0, keepdims=True)
            if image is not None:
                cross = cross + jnp.sum(r * image[rows, :], axis=0, keepdims=True)
    pay_from(bgt, halves, pay)
    pay[40:41, :] = norm
    pay[41:42, :] = energy
    pay[42:43, :] = cross


def begin_kernel(
    order, masks, matrix, bgt, bgc, weights, south, east, from_n, from_w,
    residual, yn, ys, yw, ye, pay, stack, halves, product,
):
    stacked = stack_weights(weights, stack)
    for face in range(4):
        for block in range(M // BLK):
            inside = slice(BLK * block, BLK * (block + 1))
            rows = slice(M * face + BLK * block, M * face + BLK * (block + 1))
            spread = jnp.dot(bgc[rows, :], stacked, preferred_element_type=f32)
            if face == 0:
                value = -masks[0] * from_n[inside, :]
            elif face == 1:
                value = south[inside, :]
            elif face == 2:
                value = -masks[2] * from_w[inside, :]
            else:
                value = east[inside, :]
            residual[rows, :] = value - spread
    finish(order, matrix, bgt, residual, None, (yn, ys, yw, ye), pay, halves, product)


def local_image(face, masks, y, near):
    if face == 0:
        return masks[0] * (y - near)
    if face == 1:
        return y - masks[1] * near
    if face == 2:
        return masks[2] * (y - near)
    return y - masks[3] * near


def scalars(first, sums, past):
    norm, energy = sums[0:1, :], sums[1:2, :]
    if first:
        return norm, energy, None, norm / energy
    ratio = norm / past[0:1, :]
    curvature = energy + 2.0 * ratio * sums[2:3, :] + ratio * ratio * past[1:2, :]
    return norm, curvature, ratio, norm / curvature


def step_kernel(first, *refs):
    order, masks, matrix, bgt, bgc, weights, sums, residual = refs[:8]
    near, faces = refs[8:12], refs[12:16]
    refs = refs[16:]
    if first:
        past = along = moved = done = image = None
    else:
        past, along, moved, image, done = refs[:5]
        refs = refs[5:]
    new_residual, new_along, new_moved, new_image, new_done, new_past = refs[:6]
    new_faces, pay, (stack, halves, product) = refs[6:10], refs[10], refs[11:]

    norm, curvature, ratio, step = scalars(first, sums, past)
    new_past[...] = jnp.zeros_like(new_past)
    new_past[0:1, :] = norm
    new_past[1:2, :] = curvature
    stacked = stack_weights(weights, stack)
    for face in range(4):
        for block in range(M // BLK):
            inside = slice(BLK * block, BLK * (block + 1))
            rows = slice(M * face + BLK * block, M * face + BLK * (block + 1))
            y = faces[face][inside, :]
            q = local_image(face, masks, y, near[face][inside, :])
            q = q - jnp.dot(bgc[rows, :], stacked, preferred_element_type=f32)
            r = residual[rows, :]
            if not first:
                q = q + ratio * moved[rows, :]
                y = y + ratio * image[rows, :]
            new_moved[rows, :] = q
            new_image[rows, :] = y
            new_residual[rows, :] = r - step * q
            if face % 2:
                own = slice(M * (face // 2) + BLK * block, M * (face // 2) + BLK * (block + 1))
                if first:
                    new_along[own, :] = r
                    new_done[own, :] = step * r
                else:
                    d = r + ratio * along[own, :]
                    new_along[own, :] = d
                    new_done[own, :] = done[own, :] + step * d
    finish(order, matrix, bgt, new_residual, new_image, new_faces, pay, halves, product)


def end_kernel(
    masks, bgc, weights, sums, residual, ns, ne, ys, ye, past, along, moved, done,
    out_done, out_residual, stack,
):
    _, _, ratio, step = scalars(False, sums, past)
    stacked = stack_weights(weights, stack)
    for face, near, mine in ((1, ns, ys), (3, ne, ye)):
        for block in range(M // BLK):
            inside = slice(BLK * block, BLK * (block + 1))
            rows = slice(M * face + BLK * block, M * face + BLK * (block + 1))
            own = slice(M * (face // 2) + BLK * block, M * (face // 2) + BLK * (block + 1))
            q = local_image(face, masks, mine[inside, :], near[inside, :])
            q = q - jnp.dot(bgc[rows, :], stacked, preferred_element_type=f32)
            q = q + ratio * moved[rows, :]
            r = residual[rows, :]
            d = r + ratio * along[own, :]
            out_residual[face // 2, :, inside] = (r - step * q).T
            out_done[face // 2, :, inside] = (done[own, :] + step * d).T


def shape(*dims, kind=f32):
    return jax.ShapeDtypeStruct(dims, kind)


WORK = [
    pltpu.VMEM((256, K), f32),
    pltpu.VMEM((NS, 2 * K), bf16),
    pltpu.VMEM((NS, K), f32),
]
FACES = [shape(M, K)] * 4


def call(kernel, specs, outs, scratch, flops):
    return pl.pallas_call(
        kernel,
        in_specs=specs,
        out_specs=[VM] * len(outs),
        out_shape=outs,
        scratch_shapes=scratch,
        compiler_params=LIMIT,
        cost_estimate=pl.CostEstimate(flops=flops, bytes_accessed=1 << 20, transcendentals=0),
    )


def coarse_matrix(coarse_inverse, row):
    mine = jnp.transpose(coarse_inverse[:, 0, :, :, :, 0], (1, 0, 2, 3)).reshape(COLS * MODES, MODES * ROWS)
    wide = jnp.concatenate([mine, shifted(mine, "col", 1), shifted(mine, "col", -1)], axis=1)
    index = lax.broadcasted_iota(jnp.int32, (3 * MODES * ROWS, ROWS * PAY), 0)
    entry = lax.broadcasted_iota(jnp.int32, (3 * MODES * ROWS, ROWS * PAY), 1)
    which, mode, target = index // (MODES * ROWS), index // ROWS % MODES, index % ROWS
    holder = lax.rem(row + 4 + entry // PAY, ROWS)
    slot, place = entry % PAY // SLOT, entry % SLOT
    aimed = holder - (slot == 1).astype(jnp.int32) + (slot == 2).astype(jnp.int32)
    source = jnp.where(slot == 3, 1, jnp.where(slot == 4, 2, 0))
    chosen = (which == source) & (mode == place) & (target == aimed) & (slot < SLOTS)
    body = jnp.dot(wide, chosen.astype(f32), precision=highest, preferred_element_type=f32)
    body = jnp.pad(body.reshape(COLS, MODES, ROWS * PAY), ((1, 1), (0, SLOT - MODES), (0, 0)))
    line = lax.broadcasted_iota(jnp.int32, (SLOT, ROWS * PAY), 0)
    spot = lax.broadcasted_iota(jnp.int32, (SLOT, ROWS * PAY), 1) % PAY
    total = (spot == line + SLOT * SLOTS).astype(f32)
    return jnp.concatenate([body.reshape(-1, ROWS * PAY), total], axis=0)


def coarse_phase(pay, weights, bits):
    pay = pay.reshape(1, PAY, K)
    before = cyclic(pay, "row", 1)
    after = cyclic(pay, "row", -1)
    three = jnp.concatenate([before, pay, after], axis=0)
    low = cyclic(three, "row", 3)
    high = cyclic(three[:2], "row", -3)
    gathered = jnp.concatenate([low, three, high], axis=0).reshape(ROWS * PAY, K)
    value = jnp.dot(weights, gathered, precision=highest, preferred_element_type=f32)
    value = value.reshape(COLS + 3, SLOT, K)
    body, total = value[: COLS + 2], value[COLS + 2 :]
    partners = (
        lambda c: (3 - c // 8) * 8 + c % 8,
        lambda c: c ^ 8,
        lambda c: c // 8 * 8 + (3 - c // 2 % 4) * 2 + c % 2,
        lambda c: c ^ 2,
        lambda c: c ^ 1,
    )
    for bit, partner in zip(bits, partners):
        half = (body.shape[0] - 2) // 2
        lower, upper = body[: half + 2], body[half:]
        sent = jnp.concatenate([jnp.where(bit, lower, upper), total], axis=0)
        came = swapped(sent, partner)
        body = jnp.where(bit, upper, lower) + came[: half + 2]
        total = total + came[half + 2 :]
    centre = body[1]
    north = cyclic(centre, "row", 1)
    south = cyclic(centre, "row", -1)
    return jnp.concatenate([centre, north, south, body[0], body[2]], axis=0), total[0]


def per_device(schur_blocks, rigid_modes, floating, block_order, coarse_inverse, right_side):
    matrix = schur_blocks[0, 0]
    order = block_order[0, 0]
    row, col = lax.axis_index("row"), lax.axis_index("col")
    masks = jnp.stack([row > 0, row < ROWS - 1, col > 0, col < COLS - 1]).astype(f32)
    bits = [(col // 16) % 2 == 1, (col // 8) % 2 == 1, (col // 4) % 2 == 1, (col // 2) % 2 == 1, col % 2 == 1]

    used = rigid_modes[0, 0] * floating[0, 0].astype(f32)
    near_n = shifted(used[:, M : 2 * M], "row", 1)
    near_s = shifted(used[:, :M], "row", -1)
    near_w = shifted(used[:, 3 * M :], "col", 1)
    near_e = shifted(used[:, 2 * M : 3 * M], "col", -1)
    bgt, south, east, pay = call(
        modes_kernel,
        [SM] + [VM] * 6,
        [shape(3 * PAY, NS, kind=bf16), shape(M, K), shape(M, K), shape(PAY, K)],
        [pltpu.VMEM((PAY, NS), f32), pltpu.VMEM((NS, 2 * K), bf16)],
        10**8,
    )(masks, used, near_n, near_s, near_w, near_e, right_side[0, 0])
    weights = coarse_matrix(coarse_inverse, row)
    (bgc,) = call(
        spread_kernel, [VM], [shape(NS, 2 * K, kind=bf16)], [pltpu.VMEM((256, NS), f32)], 10**8
    )(bgt)
    from_n = cyclic(south, "row", 1)
    from_w = cyclic(east, "col", 1)
    values, _ = coarse_phase(pay, weights, bits)

    residual, *faces, pay = call(
        begin_kernel,
        [SM, SM] + [VM] * 8,
        [shape(NS, K)] + FACES + [shape(PAY, K)],
        WORK,
        2 * 10**9,
    )(order, masks, matrix, bgt, bgc, values, south, east, from_n, from_w)

    state = ()
    for iteration in range(ITERS):
        near = (
            cyclic(faces[1], "row", 1),
            cyclic(faces[0], "row", -1),
            cyclic(faces[3], "col", 1),
            cyclic(faces[2], "col", -1),
        )
        values, sums = coarse_phase(pay, weights, bits)
        if iteration + 1 == ITERS:
            break
        first = iteration == 0
        given = (order, masks, matrix, bgt, bgc, values, sums, residual, *near, *faces, *state)
        residual, along, moved, image, done, past, *faces, pay = call(
            functools.partial(step_kernel, first),
            [SM, SM] + [VM] * (len(given) - 2),
            [shape(NS, K), shape(2 * M, K), shape(NS, K), shape(NS, K), shape(2 * M, K), shape(SLOT, K)]
            + FACES
            + [shape(PAY, K)],
            WORK,
            2 * 10**9,
        )(*given)
        state = (past, along, moved, image, done)

    past, along, moved, image, done = state
    done, residual = call(
        end_kernel,
        [SM] + [VM] * 12,
        [shape(2, K, M)] * 2,
        [pltpu.VMEM((256, K), f32)],
        10**8,
    )(masks, bgc, values, sums, residual, near[1], near[3], faces[1], faces[3], past, along, moved, done)
    return (done[None, None], residual[None, None])


def solution(mesh):
    placed = (
        P("row", "col", None, None),
        P("row", "col", None, None),
        P("row", "col"),
        P("row", "col", None),
        P(None, "row", None, None, None, "col"),
        P("row", "col", None, None, None),
    )
    return jax.shard_map(
        per_device,
        mesh=mesh,
        in_specs=placed,
        out_specs=(P("row", "col", None, None, None), P("row", "col", None, None, None)),
        check_vma=False,
    )
```

```python
import functools

import jax
import jax.numpy as jnp
from jax import lax
from jax.experimental import pallas as pl
from jax.experimental.pallas import tpu as pltpu
from jax.sharding import PartitionSpec as P

M = 512
NS = 2048
BLK = 128
NB = 16
K = 128
ROWS = 8
COLS = 32
MODES = 6
ITERS = 3
SLOT = 8
SLOTS = 5
PAY = 48
TERMS = ((0, 0), (0, 1), (1, 0), (1, 1), (0, 2), (2, 0))
TALL = 512
CHIPS = 16

f32 = jnp.float32
bf16 = jnp.bfloat16
VM = pl.BlockSpec(memory_space=pltpu.VMEM)
SM = pl.BlockSpec(memory_space=pltpu.SMEM)
LIMIT = pltpu.CompilerParams(vmem_limit_bytes=40 * 1024 * 1024)


def cyclic(value, axis, steps):
    count = lax.axis_size(axis)
    return lax.ppermute(value, axis, [(s, (s + steps) % count) for s in range(count)])


def shifted(value, axis, steps):
    count = lax.axis_size(axis)
    initial, last = (max(0, -steps), min(count, count - steps))
    return lax.ppermute(value, axis, [(s, s + steps) for s in range(initial, last)])


def swapped(value, partner):
    return lax.ppermute(value, "col", [(s, partner(s)) for s in range(COLS)])


def parts_of(value, count):
    pieces = []
    for _ in range(count):
        piece = value.astype(bf16)
        pieces.append(piece)
        value = value - piece.astype(f32)
    return pieces


def pay_from(bgt, halves):
    d = jnp.dot(bgt[...], halves[...], preferred_element_type=f32)
    return d[0:PAY, :K] + d[0:PAY, K:] + d[PAY : 2 * PAY, :K] + d[PAY : 2 * PAY, K:] + d[2 * PAY :, :K]


def hand_in(value, pay):
    for index in range(ROWS):
        pay[index] = value


def start_kernel(masks, own, side, from_n, from_w, local, pay, full, halves):
    full[...] = jnp.zeros_like(full)
    full[0:MODES, 0:M] = own[:, 0:M] * masks[0]
    full[0:MODES, M : 2 * M] = own[:, M : 2 * M]
    full[0:MODES, 2 * M : 3 * M] = own[:, 2 * M : 3 * M] * masks[2]
    full[0:MODES, 3 * M :] = own[:, 3 * M :]
    for face in range(4):
        for block in range(M // BLK):
            inside = slice(BLK * block, BLK * (block + 1))
            rows = slice(M * face + BLK * block, M * face + BLK * (block + 1))
            if face == 0:
                turned = from_n[:, inside].T * -masks[0]
            elif face == 2:
                turned = from_w[:, inside].T * -masks[2]
            else:
                turned = side[face // 2, :, inside].T
            local[rows, :] = turned
            high, low = parts_of(turned, 2)
            halves[rows, :K] = high
            halves[rows, K:] = low
    pieces = jnp.concatenate(parts_of(full[...], 3), axis=0)
    d = jnp.dot(pieces, halves[...], preferred_element_type=f32)
    value = d[0:16, :K] + d[0:16, K:] + d[16:32, :K] + d[16:32, K:] + d[32:48, :K]
    pay[...] = jnp.zeros_like(pay)
    for index in range(ROWS):
        pay[index, 0:SLOT, :] = value[0:SLOT]


def modes_kernel(masks, own, near_n, near_s, near_w, near_e, bgt, full):
    full[...] = jnp.zeros_like(full)
    full[0:MODES, 0:M] = own[:, 0:M] * masks[0]
    full[0:MODES, M : 2 * M] = own[:, M : 2 * M]
    full[0:MODES, 2 * M : 3 * M] = own[:, 2 * M : 3 * M] * masks[2]
    full[0:MODES, 3 * M :] = own[:, 3 * M :]
    for slot, near in enumerate((near_n, near_s, near_w, near_e)):
        full[SLOT * (slot + 1) : SLOT * (slot + 1) + MODES, M * slot : M * (slot + 1)] = -near[...]
    for index, piece in enumerate(parts_of(full[...], 3)):
        bgt[PAY * index : PAY * (index + 1), :] = piece


def table_kernel(core, west, mine, east, far, parts, full):
    first = core[0] == 0
    left = lax.broadcasted_iota(jnp.int32, (SLOT, BLK), 1) < SLOT * ROWS
    for target in range(CHIPS):
        at = 2 * target + core[0]
        picks = ((0, at), (1, at), (2, at), (0, jnp.maximum(at - 1, 0)), (0, jnp.minimum(at + 1, COLS - 1)))
        for slot, (line, column) in enumerate(picks):
            w, m, e, f = west[line, column], mine[line, column], east[line, column], far[line, column]
            inner = jnp.where(left, jnp.where(first, w, f), jnp.where(first, m, w))
            outer = jnp.where(left, jnp.where(first, e, m), jnp.where(first, f, e))
            rows = slice((target * SLOTS + slot) * SLOT, (target * SLOTS + slot + 1) * SLOT)
            full[rows, :K] = inner
            full[rows, K:] = outer
    for index, piece in enumerate(parts_of(full[...], 3)):
        parts[index] = piece


def coarse_kernel(core, parts, own, other, out, entries):
    first = core[0] == 0

    def tile(which, line, slot):
        here = slice(SLOT * slot, SLOT * (slot + 1))
        a, b = own[line, here, :], other[line, here, :]
        return jnp.where(first, a, b) if which == 0 else jnp.where(first, b, a)

    total = jnp.zeros((SLOT, K), f32)
    for line in range(ROWS):
        for which in range(2):
            value = tile(which, line, 0)
            if line > 0:
                value = value + tile(which, line - 1, 2)
            if line < ROWS - 1:
                value = value + tile(which, line + 1, 1)
            value = value + tile(1 - which, line, 3 + which)
            at = SLOT * (ROWS * (which + 1) + line)
            entries[at : at + SLOT, :] = value
        entries[SLOT * line : SLOT * (line + 1), :] = tile(0, line, 3)
        at = SLOT * (ROWS * 3 + line)
        entries[at : at + SLOT, :] = tile(1, line, 4)
        total = total + own[line, SLOT * SLOTS :, :] + other[line, SLOT * SLOTS :, :]
    z1, z2, z3 = parts_of(entries[...], 3)
    both = jnp.concatenate([z1, z2], axis=1)
    d = jnp.dot(parts[0], both, preferred_element_type=f32)
    e = jnp.dot(parts[1], both, preferred_element_type=f32)
    value = jnp.dot(parts[0], z3, preferred_element_type=f32) + jnp.dot(parts[2], z1, preferred_element_type=f32)
    value = value + e[:, K:] + e[:, :K] + d[:, K:] + d[:, :K]
    for target in range(CHIPS):
        out[target] = value[SLOTS * SLOT * target : SLOTS * SLOT * (target + 1)]
        out[target, 6:8, :] = total[0:2]
        out[target, 14:15, :] = total[2:3]


def spread_kernel(bgt, bgc, turned):
    for index, (left, _) in enumerate(TERMS):
        rows = bgt[PAY * left : PAY * (left + 1), :].astype(f32)
        turned[40 * index : 40 * (index + 1), :] = rows[0:40]
    turned[240:256, :] = jnp.zeros((16, NS), f32)
    for block in range(NB):
        for half in range(2):
            piece = turned[BLK * half : BLK * (half + 1), BLK * block : BLK * (block + 1)].T
            bgc[BLK * block : BLK * (block + 1), BLK * half : BLK * (half + 1)] = piece.astype(bf16)


def take_values(came, stack):
    value = came[0]
    for index in range(1, CHIPS):
        value = value + came[index]
    spare = lax.broadcasted_iota(jnp.int32, (SLOT * SLOTS, K), 0) % SLOT >= MODES
    pieces = parts_of(jnp.where(spare, 0.0, value), 3)
    for index, (_, right) in enumerate(TERMS):
        stack[40 * index : 40 * (index + 1), :] = pieces[right].astype(f32)
    stack[240:256, :] = jnp.zeros((16, K), f32)
    return stack[...].astype(bf16), (value[6:7], value[7:8], value[14:15])


def schur_product(order, matrix, vector, halves, product, copies):
    for block in range(NB):
        at = pl.multiple_of(order[block] * BLK, BLK)
        high, low = parts_of(vector[pl.ds(at, BLK), :], 2)
        halves[BLK * block : BLK * (block + 1), :K] = high
        halves[BLK * block : BLK * (block + 1), K:] = low

    def tall(step):
        rows = matrix[pl.ds(pl.multiple_of(step * TALL, TALL), TALL), :]
        both = jnp.dot(rows, halves[...], preferred_element_type=f32)
        both = both[:, :K] + both[:, K:]
        for piece in range(TALL // BLK):
            at = pl.multiple_of(order[step * (TALL // BLK) + piece] * BLK, BLK)
            product[pl.ds(at, BLK), :] = both[BLK * piece : BLK * (piece + 1)]

    if copies:
        for step, copy in enumerate(copies):
            copy.wait()
            tall(step)
    else:
        pl.loop(0, NS // TALL)(tall)


def finish(order, matrix, bgt, residual, image, faces, pay, halves, product, copies=()):
    schur_product(order, matrix, residual, halves, product, copies)
    norm = jnp.zeros((1, K), f32)
    energy = jnp.zeros((1, K), f32)
    cross = jnp.zeros((1, K), f32)
    for face in range(4):
        for block in range(M // BLK):
            inside = slice(BLK * block, BLK * (block + 1))
            rows = slice(M * face + BLK * block, M * face + BLK * (block + 1))
            r = residual[rows, :]
            y = product[rows, :]
            faces[face][inside, :] = y
            high, low = parts_of(y, 2)
            halves[rows, :K] = high
            halves[rows, K:] = low
            energy = energy + jnp.sum(r * y, axis=0, keepdims=True)
            if face % 2:
                norm = norm + jnp.sum(r * r, axis=0, keepdims=True)
            if image is not None:
                cross = cross + jnp.sum(r * image[rows, :], axis=0, keepdims=True)
    hand_in(pay_from(bgt, halves), pay)
    for index in range(ROWS):
        pay[index, 40:41, :] = norm
        pay[index, 41:42, :] = energy
        pay[index, 42:43, :] = cross


def begin_kernel(
    order, source, bgt, bgc, came, local,
    residual, yn, ys, yw, ye, pay, matrix, stack, halves, product, sems,
):
    copies = []
    for index in range(NS // TALL):
        rows = pl.ds(TALL * index, TALL)
        copies.append(pltpu.make_async_copy(source.at[rows], matrix.at[rows], sems.at[index]))
        copies[-1].start()
    stacked, _ = take_values(came, stack)
    for block in range(NB):
        rows = slice(BLK * block, BLK * (block + 1))
        residual[rows, :] = local[rows, :] - jnp.dot(bgc[rows, :], stacked, preferred_element_type=f32)
    finish(order, matrix, bgt, residual, None, (yn, ys, yw, ye), pay, halves, product, copies)


def local_image(face, masks, y, near):
    if face == 0:
        return masks[0] * (y - near)
    if face == 1:
        return y - masks[1] * near
    if face == 2:
        return masks[2] * (y - near)
    return y - masks[3] * near


def scalars(first, sums, past):
    norm, energy, cross = sums
    if first:
        return norm, energy, None, norm / energy
    ratio = norm / past[0:1, :]
    curvature = energy + 2.0 * ratio * cross + ratio * ratio * past[1:2, :]
    return norm, curvature, ratio, norm / curvature


def step_kernel(first, *refs):
    order, masks, matrix, bgt, bgc, came, residual = refs[:7]
    near, faces = refs[7:11], refs[11:15]
    refs = refs[15:]
    if first:
        past = along = moved = done = image = None
    else:
        past, along, moved, image, done = refs[:5]
        refs = refs[5:]
    new_residual, new_along, new_moved, new_image, new_done, new_past = refs[:6]
    new_faces, pay, (stack, halves, product) = refs[6:10], refs[10], refs[11:]

    stacked, sums = take_values(came, stack)
    norm, curvature, ratio, step = scalars(first, sums, past)
    new_past[...] = jnp.zeros_like(new_past)
    new_past[0:1, :] = norm
    new_past[1:2, :] = curvature
    for face in range(4):
        for block in range(M // BLK):
            inside = slice(BLK * block, BLK * (block + 1))
            rows = slice(M * face + BLK * block, M * face + BLK * (block + 1))
            y = faces[face][inside, :]
            q = local_image(face, masks, y, near[face][inside, :])
            q = q - jnp.dot(bgc[rows, :], stacked, preferred_element_type=f32)
            r = residual[rows, :]
            if not first:
                q = q + ratio * moved[rows, :]
                y = y + ratio * image[rows, :]
            new_moved[rows, :] = q
            new_image[rows, :] = y
            new_residual[rows, :] = r - step * q
            if face % 2:
                own = slice(M * (face // 2) + BLK * block, M * (face // 2) + BLK * (block + 1))
                if first:
                    new_along[own, :] = r
                    new_done[own, :] = step * r
                else:
                    d = r + ratio * along[own, :]
                    new_along[own, :] = d
                    new_done[own, :] = done[own, :] + step * d
    finish(order, matrix, bgt, new_residual, new_image, new_faces, pay, halves, product)


def end_kernel(
    masks, bgc, came, residual, ns, ne, ys, ye, past, along, moved, done,
    out_done, out_residual, stack,
):
    stacked, sums = take_values(came, stack)
    _, _, ratio, step = scalars(False, sums, past)
    for face, near, mine in ((1, ns, ys), (3, ne, ye)):
        for block in range(M // BLK):
            inside = slice(BLK * block, BLK * (block + 1))
            rows = slice(M * face + BLK * block, M * face + BLK * (block + 1))
            own = slice(M * (face // 2) + BLK * block, M * (face // 2) + BLK * (block + 1))
            q = local_image(face, masks, mine[inside, :], near[inside, :])
            q = q - jnp.dot(bgc[rows, :], stacked, preferred_element_type=f32)
            q = q + ratio * moved[rows, :]
            r = residual[rows, :]
            d = r + ratio * along[own, :]
            out_residual[face // 2, :, inside] = (r - step * q).T
            out_done[face // 2, :, inside] = (done[own, :] + step * d).T


def shape(*dims, kind=f32):
    return jax.ShapeDtypeStruct(dims, kind)


WORK = [
    pltpu.VMEM((256, K), f32),
    pltpu.VMEM((NS, 2 * K), bf16),
    pltpu.VMEM((NS, K), f32),
]
FACES = [shape(M, K)] * 4


def call(kernel, specs, outs, scratch, flops):
    return pl.pallas_call(
        kernel,
        in_specs=specs,
        out_specs=[VM] * len(outs),
        out_shape=outs,
        scratch_shapes=scratch,
        compiler_params=LIMIT,
        cost_estimate=pl.CostEstimate(flops=flops, bytes_accessed=1 << 20, transcendentals=0),
    )


def coarse_table(coarse_inverse, core):
    mine = jnp.transpose(coarse_inverse[:, 0, :, :, :, 0], (1, 0, 3, 2))
    mine = jnp.pad(mine, ((0, 0), (0, SLOT - MODES), (0, 0), (0, SLOT - MODES))).reshape(COLS, SLOT, SLOT * ROWS)
    mine = jnp.concatenate([mine, mine], axis=2)
    lines = jnp.stack([mine, cyclic(mine, "row", 1), cyclic(mine, "row", -1)])
    west = cyclic(lines, "col", 1)
    east = cyclic(lines, "col", -1)
    far = swapped(jnp.where(core[0] == 0, west, east), lambda c: c ^ 1)
    (parts,) = call(
        table_kernel,
        [SM] + [VM] * 4,
        [shape(3, CHIPS * SLOTS * SLOT, 2 * K, kind=bf16)],
        [pltpu.VMEM((CHIPS * SLOTS * SLOT, 2 * K), f32)],
        10**7,
    )(core, west, lines, east, far)
    return parts


def coarse_phase(pay, parts, core):
    own = lax.all_to_all(pay, "row", 0, 0, tiled=True)
    other = swapped(own, lambda c: c ^ 1)
    (terms,) = call(
        coarse_kernel,
        [SM] + [VM] * 3,
        [shape(CHIPS, SLOTS * SLOT, K)],
        [pltpu.VMEM((2 * K, K), f32)],
        10**8,
    )(core, parts, own, other)
    groups = [[2 * chip + which for chip in range(CHIPS)] for which in range(2)]
    return lax.all_to_all(terms, "col", 0, 0, axis_index_groups=groups, tiled=True)


def per_device(schur_blocks, rigid_modes, floating, block_order, coarse_inverse, right_side):
    order = block_order[0, 0]
    row, col = lax.axis_index("row"), lax.axis_index("col")
    core = (col % 2).astype(jnp.int32).reshape(1)
    masks = jnp.stack([row > 0, row < ROWS - 1, col > 0, col < COLS - 1]).astype(f32)
    side = right_side[0, 0]

    from_n = cyclic(side[0], "row", 1)
    from_w = cyclic(side[1], "col", 1)
    used = rigid_modes[0, 0] * floating[0, 0].astype(f32)
    near_n = shifted(used[:, M : 2 * M], "row", 1)
    near_s = shifted(used[:, :M], "row", -1)
    near_w = shifted(used[:, 3 * M :], "col", 1)
    near_e = shifted(used[:, 2 * M : 3 * M], "col", -1)
    local, pay = call(
        start_kernel,
        [SM] + [VM] * 4,
        [shape(NS, K), shape(ROWS, PAY, K)],
        [pltpu.VMEM((16, NS), f32), pltpu.VMEM((NS, 2 * K), bf16)],
        10**8,
    )(masks, used, side, from_n, from_w)
    parts = coarse_table(coarse_inverse, core)
    (bgt,) = call(
        modes_kernel, [SM] + [VM] * 5, [shape(3 * PAY, NS, kind=bf16)], [pltpu.VMEM((PAY, NS), f32)], 10**8
    )(masks, used, near_n, near_s, near_w, near_e)
    (bgc,) = call(
        spread_kernel, [VM], [shape(NS, 2 * K, kind=bf16)], [pltpu.VMEM((256, NS), f32)], 10**8
    )(bgt)
    came = coarse_phase(pay, parts, core)

    residual, *faces, pay, matrix = call(
        begin_kernel,
        [SM, pl.BlockSpec(memory_space=pl.ANY)] + [VM] * 4,
        [shape(NS, K)] + FACES + [shape(ROWS, PAY, K), shape(NS, NS, kind=bf16)],
        WORK + [pltpu.SemaphoreType.DMA((NS // TALL,))],
        2 * 10**9,
    )(order, schur_blocks[0, 0], bgt, bgc, came, local)

    state = ()
    for iteration in range(ITERS):
        near = (
            cyclic(faces[1], "row", 1),
            cyclic(faces[0], "row", -1),
            cyclic(faces[3], "col", 1),
            cyclic(faces[2], "col", -1),
        )
        came = coarse_phase(pay, parts, core)
        if iteration + 1 == ITERS:
            break
        first = iteration == 0
        given = (order, masks, matrix, bgt, bgc, came, residual, *near, *faces, *state)
        residual, along, moved, image, done, past, *faces, pay = call(
            functools.partial(step_kernel, first),
            [SM, SM] + [VM] * (len(given) - 2),
            [shape(NS, K), shape(2 * M, K), shape(NS, K), shape(NS, K), shape(2 * M, K), shape(SLOT, K)]
            + FACES
            + [shape(ROWS, PAY, K)],
            WORK,
            2 * 10**9,
        )(*given)
        state = (past, along, moved, image, done)

    past, along, moved, image, done = state
    done, residual = call(
        end_kernel,
        [SM] + [VM] * 11,
        [shape(2, K, M)] * 2,
        [pltpu.VMEM((256, K), f32)],
        10**8,
    )(masks, bgc, came, residual, near[1], near[3], faces[1], faces[3], past, along, moved, done)
    return (done[None, None], residual[None, None])


def solution(mesh):
    placed = (
        P("row", "col", None, None),
        P("row", "col", None, None),
        P("row", "col"),
        P("row", "col", None),
        P(None, "row", None, None, None, "col"),
        P("row", "col", None, None, None),
    )
    return jax.shard_map(
        per_device,
        mesh=mesh,
        in_specs=placed,
        out_specs=(P("row", "col", None, None, None), P("row", "col", None, None, None)),
        check_vma=False,
    )
```

```python
import functools

import jax
import jax.numpy as jnp
from jax import lax
from jax.experimental import pallas as pl
from jax.experimental.pallas import tpu as pltpu
from jax.sharding import PartitionSpec as P

M = 512
NS = 2048
BLK = 128
NB = 16
K = 128
ROWS = 8
COLS = 32
MODES = 6
ITERS = 3
SLOT = 8
SLOTS = 5
PAY = 48
TERMS = ((0, 0), (0, 1), (1, 0), (1, 1), (0, 2), (2, 0))
TALL = 512
CHIPS = 16

f32 = jnp.float32
bf16 = jnp.bfloat16
VM = pl.BlockSpec(memory_space=pltpu.VMEM)
SM = pl.BlockSpec(memory_space=pltpu.SMEM)
LIMIT = pltpu.CompilerParams(vmem_limit_bytes=12 * 1024 * 1024)


def cyclic(value, axis, steps):
    count = lax.axis_size(axis)
    return lax.ppermute(value, axis, [(s, (s + steps) % count) for s in range(count)])


def shifted(value, axis, steps):
    count = lax.axis_size(axis)
    initial, last = (max(0, -steps), min(count, count - steps))
    return lax.ppermute(value, axis, [(s, s + steps) for s in range(initial, last)])


def swapped(value, partner):
    return lax.ppermute(value, "col", [(s, partner(s)) for s in range(COLS)])


def parts_of(value, count):
    pieces = []
    for _ in range(count):
        piece = value.astype(bf16)
        pieces.append(piece)
        value = value - piece.astype(f32)
    return pieces


def pay_from(bgt, halves):
    d = jnp.dot(bgt[...], halves[...], preferred_element_type=f32)
    return d[0:PAY, :K] + d[0:PAY, K:] + d[PAY : 2 * PAY, :K] + d[PAY : 2 * PAY, K:] + d[2 * PAY :, :K]


def hand_in(value, pay):
    for index in range(ROWS):
        pay[index] = value


def start_kernel(masks, own, side, from_n, from_w, local, pay, full, halves):
    full[...] = jnp.zeros_like(full)
    full[0:MODES, 0:M] = own[:, 0:M] * masks[0]
    full[0:MODES, M : 2 * M] = own[:, M : 2 * M]
    full[0:MODES, 2 * M : 3 * M] = own[:, 2 * M : 3 * M] * masks[2]
    full[0:MODES, 3 * M :] = own[:, 3 * M :]
    for face in range(4):
        for block in range(M // BLK):
            inside = slice(BLK * block, BLK * (block + 1))
            rows = slice(M * face + BLK * block, M * face + BLK * (block + 1))
            if face == 0:
                turned = from_n[:, inside].T * -masks[0]
            elif face == 2:
                turned = from_w[:, inside].T * -masks[2]
            else:
                turned = side[face // 2, :, inside].T
            local[rows, :] = turned
            high, low = parts_of(turned, 2)
            halves[rows, :K] = high
            halves[rows, K:] = low
    pieces = jnp.concatenate(parts_of(full[...], 3), axis=0)
    d = jnp.dot(pieces, halves[...], preferred_element_type=f32)
    value = d[0:16, :K] + d[0:16, K:] + d[16:32, :K] + d[16:32, K:] + d[32:48, :K]
    pay[...] = jnp.zeros_like(pay)
    for index in range(ROWS):
        pay[index, 0:SLOT, :] = value[0:SLOT]


def modes_kernel(masks, own, near_n, near_s, near_w, near_e, bgt, full):
    full[...] = jnp.zeros_like(full)
    full[0:MODES, 0:M] = own[:, 0:M] * masks[0]
    full[0:MODES, M : 2 * M] = own[:, M : 2 * M]
    full[0:MODES, 2 * M : 3 * M] = own[:, 2 * M : 3 * M] * masks[2]
    full[0:MODES, 3 * M :] = own[:, 3 * M :]
    for slot, near in enumerate((near_n, near_s, near_w, near_e)):
        full[SLOT * (slot + 1) : SLOT * (slot + 1) + MODES, M * slot : M * (slot + 1)] = -near[...]
    for index, piece in enumerate(parts_of(full[...], 3)):
        bgt[PAY * index : PAY * (index + 1), :] = piece


def table_kernel(core, west, mine, east, far, parts, full):
    first = core[0] == 0
    left = lax.broadcasted_iota(jnp.int32, (SLOT, BLK), 1) < SLOT * ROWS
    for target in range(CHIPS):
        at = 2 * target + core[0]
        picks = ((0, at), (1, at), (2, at), (0, jnp.maximum(at - 1, 0)), (0, jnp.minimum(at + 1, COLS - 1)))
        for slot, (line, column) in enumerate(picks):
            w, m, e, f = west[line, column], mine[line, column], east[line, column], far[line, column]
            inner = jnp.where(left, jnp.where(first, w, f), jnp.where(first, m, w))
            outer = jnp.where(left, jnp.where(first, e, m), jnp.where(first, f, e))
            rows = slice((target * SLOTS + slot) * SLOT, (target * SLOTS + slot + 1) * SLOT)
            full[rows, :K] = inner
            full[rows, K:] = outer
    for index, piece in enumerate(parts_of(full[...], 3)):
        parts[index] = piece


def coarse_kernel(core, parts, own, other, out, entries):
    first = core[0] == 0

    def tile(which, line, slot):
        here = slice(SLOT * slot, SLOT * (slot + 1))
        a, b = own[line, here, :], other[line, here, :]
        return jnp.where(first, a, b) if which == 0 else jnp.where(first, b, a)

    total = jnp.zeros((SLOT, K), f32)
    for line in range(ROWS):
        for which in range(2):
            value = tile(which, line, 0)
            if line > 0:
                value = value + tile(which, line - 1, 2)
            if line < ROWS - 1:
                value = value + tile(which, line + 1, 1)
            value = value + tile(1 - which, line, 3 + which)
            at = SLOT * (ROWS * (which + 1) + line)
            entries[at : at + SLOT, :] = value
        entries[SLOT * line : SLOT * (line + 1), :] = tile(0, line, 3)
        at = SLOT * (ROWS * 3 + line)
        entries[at : at + SLOT, :] = tile(1, line, 4)
        total = total + own[line, SLOT * SLOTS :, :] + other[line, SLOT * SLOTS :, :]
    z1, z2, z3 = parts_of(entries[...], 3)
    both = jnp.concatenate([z1, z2], axis=1)
    d = jnp.dot(parts[0], both, preferred_element_type=f32)
    e = jnp.dot(parts[1], both, preferred_element_type=f32)
    value = jnp.dot(parts[0], z3, preferred_element_type=f32) + jnp.dot(parts[2], z1, preferred_element_type=f32)
    value = value + e[:, K:] + e[:, :K] + d[:, K:] + d[:, :K]
    for target in range(CHIPS):
        out[target] = value[SLOTS * SLOT * target : SLOTS * SLOT * (target + 1)]
        out[target, 6:8, :] = total[0:2]
        out[target, 14:15, :] = total[2:3]


def spread_kernel(bgt, bgc, turned):
    for index, (left, _) in enumerate(TERMS):
        rows = bgt[PAY * left : PAY * (left + 1), :].astype(f32)
        turned[40 * index : 40 * (index + 1), :] = rows[0:40]
    turned[240:256, :] = jnp.zeros((16, NS), f32)
    for block in range(NB):
        for half in range(2):
            piece = turned[BLK * half : BLK * (half + 1), BLK * block : BLK * (block + 1)].T
            bgc[BLK * block : BLK * (block + 1), BLK * half : BLK * (half + 1)] = piece.astype(bf16)


def take_values(came, stack):
    value = came[0]
    for index in range(1, CHIPS):
        value = value + came[index]
    spare = lax.broadcasted_iota(jnp.int32, (SLOT * SLOTS, K), 0) % SLOT >= MODES
    pieces = parts_of(jnp.where(spare, 0.0, value), 3)
    for index, (_, right) in enumerate(TERMS):
        stack[40 * index : 40 * (index + 1), :] = pieces[right].astype(f32)
    stack[240:256, :] = jnp.zeros((16, K), f32)
    return stack[...].astype(bf16), (value[6:7], value[7:8], value[14:15])


def schur_product(order, matrix, vector, halves, product, copies):
    for block in range(NB):
        at = pl.multiple_of(order[block] * BLK, BLK)
        high, low = parts_of(vector[pl.ds(at, BLK), :], 2)
        halves[BLK * block : BLK * (block + 1), :K] = high
        halves[BLK * block : BLK * (block + 1), K:] = low

    def tall(step):
        rows = matrix[pl.ds(pl.multiple_of(step * TALL, TALL), TALL), :]
        both = jnp.dot(rows, halves[...], preferred_element_type=f32)
        both = both[:, :K] + both[:, K:]
        for piece in range(TALL // BLK):
            at = pl.multiple_of(order[step * (TALL // BLK) + piece] * BLK, BLK)
            product[pl.ds(at, BLK), :] = both[BLK * piece : BLK * (piece + 1)]

    if copies:
        for step, copy in enumerate(copies):
            copy.wait()
            tall(step)
    else:
        pl.loop(0, NS // TALL)(tall)


def finish(order, matrix, bgt, residual, image, faces, pay, halves, product, copies=()):
    schur_product(order, matrix, residual, halves, product, copies)
    norm = jnp.zeros((1, K), f32)
    energy = jnp.zeros((1, K), f32)
    cross = jnp.zeros((1, K), f32)
    for face in range(4):
        for block in range(M // BLK):
            inside = slice(BLK * block, BLK * (block + 1))
            rows = slice(M * face + BLK * block, M * face + BLK * (block + 1))
            r = residual[rows, :]
            y = product[rows, :]
            faces[face][inside, :] = y
            high, low = parts_of(y, 2)
            halves[rows, :K] = high
            halves[rows, K:] = low
            energy = energy + jnp.sum(r * y, axis=0, keepdims=True)
            if face % 2:
                norm = norm + jnp.sum(r * r, axis=0, keepdims=True)
            if image is not None:
                cross = cross + jnp.sum(r * image[rows, :], axis=0, keepdims=True)
    hand_in(pay_from(bgt, halves), pay)
    for index in range(ROWS):
        pay[index, 40:41, :] = norm
        pay[index, 41:42, :] = energy
        pay[index, 42:43, :] = cross


def begin_kernel(
    order, source, bgt, bgc, came, local,
    residual, yn, ys, yw, ye, pay, matrix, stack, halves, product, sems,
):
    copies = []
    for index in range(NS // TALL):
        rows = pl.ds(TALL * index, TALL)
        copies.append(pltpu.make_async_copy(source.at[rows], matrix.at[rows], sems.at[index]))
        copies[-1].start()
    stacked, _ = take_values(came, stack)
    for block in range(NB):
        rows = slice(BLK * block, BLK * (block + 1))
        residual[rows, :] = local[rows, :] - jnp.dot(bgc[rows, :], stacked, preferred_element_type=f32)
    finish(order, matrix, bgt, residual, None, (yn, ys, yw, ye), pay, halves, product, copies)


def local_image(face, masks, y, near):
    if face == 0:
        return masks[0] * (y - near)
    if face == 1:
        return y - masks[1] * near
    if face == 2:
        return masks[2] * (y - near)
    return y - masks[3] * near


def scalars(first, sums, past):
    norm, energy, cross = sums
    if first:
        return norm, energy, None, norm / energy
    ratio = norm / past[0:1, :]
    curvature = energy + 2.0 * ratio * cross + ratio * ratio * past[1:2, :]
    return norm, curvature, ratio, norm / curvature


def step_kernel(first, *refs):
    order, masks, matrix, bgt, bgc, came, residual = refs[:7]
    near, faces = refs[7:11], refs[11:15]
    refs = refs[15:]
    if first:
        past = along = moved = done = image = None
    else:
        past, along, moved, image, done = refs[:5]
        refs = refs[5:]
    new_residual, new_along, new_moved, new_image, new_done, new_past = refs[:6]
    new_faces, pay, (stack, halves, product) = refs[6:10], refs[10], refs[11:]

    stacked, sums = take_values(came, stack)
    norm, curvature, ratio, step = scalars(first, sums, past)
    new_past[...] = jnp.zeros_like(new_past)
    new_past[0:1, :] = norm
    new_past[1:2, :] = curvature
    for face in range(4):
        for block in range(M // BLK):
            inside = slice(BLK * block, BLK * (block + 1))
            rows = slice(M * face + BLK * block, M * face + BLK * (block + 1))
            y = faces[face][inside, :]
            q = local_image(face, masks, y, near[face][inside, :])
            q = q - jnp.dot(bgc[rows, :], stacked, preferred_element_type=f32)
            r = residual[rows, :]
            if not first:
                q = q + ratio * moved[rows, :]
                y = y + ratio * image[rows, :]
            new_moved[rows, :] = q
            new_image[rows, :] = y
            new_residual[rows, :] = r - step * q
            if face % 2:
                own = slice(M * (face // 2) + BLK * block, M * (face // 2) + BLK * (block + 1))
                if first:
                    new_along[own, :] = r
                    new_done[own, :] = step * r
                else:
                    d = r + ratio * along[own, :]
                    new_along[own, :] = d
                    new_done[own, :] = done[own, :] + step * d
    finish(order, matrix, bgt, new_residual, new_image, new_faces, pay, halves, product)


def end_kernel(
    masks, bgc, came, residual, ns, ne, ys, ye, past, along, moved, done,
    out_done, out_residual, stack,
):
    stacked, sums = take_values(came, stack)
    _, _, ratio, step = scalars(False, sums, past)
    for face, near, mine in ((1, ns, ys), (3, ne, ye)):
        for block in range(M // BLK):
            inside = slice(BLK * block, BLK * (block + 1))
            rows = slice(M * face + BLK * block, M * face + BLK * (block + 1))
            own = slice(M * (face // 2) + BLK * block, M * (face // 2) + BLK * (block + 1))
            q = local_image(face, masks, mine[inside, :], near[inside, :])
            q = q - jnp.dot(bgc[rows, :], stacked, preferred_element_type=f32)
            q = q + ratio * moved[rows, :]
            r = residual[rows, :]
            d = r + ratio * along[own, :]
            out_residual[face // 2, :, inside] = (r - step * q).T
            out_done[face // 2, :, inside] = (done[own, :] + step * d).T


def shape(*dims, kind=f32):
    return jax.ShapeDtypeStruct(dims, kind)


WORK = [
    pltpu.VMEM((256, K), f32),
    pltpu.VMEM((NS, 2 * K), bf16),
    pltpu.VMEM((NS, K), f32),
]
FACES = [shape(M, K)] * 4


def call(kernel, specs, outs, scratch, flops):
    return pl.pallas_call(
        kernel,
        in_specs=specs,
        out_specs=[VM] * len(outs),
        out_shape=outs,
        scratch_shapes=scratch,
        compiler_params=LIMIT,
        cost_estimate=pl.CostEstimate(flops=flops, bytes_accessed=1 << 20, transcendentals=0),
    )


def coarse_table(coarse_inverse, core):
    mine = jnp.transpose(coarse_inverse[:, 0, :, :, :, 0], (1, 0, 3, 2))
    mine = jnp.pad(mine, ((0, 0), (0, SLOT - MODES), (0, 0), (0, SLOT - MODES))).reshape(COLS, SLOT, SLOT * ROWS)
    mine = jnp.concatenate([mine, mine], axis=2)
    lines = jnp.stack([mine, cyclic(mine, "row", 1), cyclic(mine, "row", -1)])
    west = cyclic(lines, "col", 1)
    east = cyclic(lines, "col", -1)
    far = swapped(jnp.where(core[0] == 0, west, east), lambda c: c ^ 1)
    (parts,) = call(
        table_kernel,
        [SM] + [VM] * 4,
        [shape(3, CHIPS * SLOTS * SLOT, 2 * K, kind=bf16)],
        [pltpu.VMEM((CHIPS * SLOTS * SLOT, 2 * K), f32)],
        10**7,
    )(core, west, lines, east, far)
    return parts


def coarse_phase(pay, parts, core):
    own = lax.all_to_all(pay, "row", 0, 0, tiled=True)
    other = swapped(own, lambda c: c ^ 1)
    (terms,) = call(
        coarse_kernel,
        [SM] + [VM] * 3,
        [shape(CHIPS, SLOTS * SLOT, K)],
        [pltpu.VMEM((2 * K, K), f32)],
        10**8,
    )(core, parts, own, other)
    groups = [[2 * chip + which for chip in range(CHIPS)] for which in range(2)]
    return lax.all_to_all(terms, "col", 0, 0, axis_index_groups=groups, tiled=True)


def per_device(schur_blocks, rigid_modes, floating, block_order, coarse_inverse, right_side):
    order = block_order[0, 0]
    row, col = lax.axis_index("row"), lax.axis_index("col")
    core = (col % 2).astype(jnp.int32).reshape(1)
    masks = jnp.stack([row > 0, row < ROWS - 1, col > 0, col < COLS - 1]).astype(f32)
    side = right_side[0, 0]

    from_n = cyclic(side[0], "row", 1)
    from_w = cyclic(side[1], "col", 1)
    used = rigid_modes[0, 0] * floating[0, 0].astype(f32)
    near_n = shifted(used[:, M : 2 * M], "row", 1)
    near_s = shifted(used[:, :M], "row", -1)
    near_w = shifted(used[:, 3 * M :], "col", 1)
    near_e = shifted(used[:, 2 * M : 3 * M], "col", -1)
    local, pay = call(
        start_kernel,
        [SM] + [VM] * 4,
        [shape(NS, K), shape(ROWS, PAY, K)],
        [pltpu.VMEM((16, NS), f32), pltpu.VMEM((NS, 2 * K), bf16)],
        10**8,
    )(masks, used, side, from_n, from_w)
    parts = coarse_table(coarse_inverse, core)
    (bgt,) = call(
        modes_kernel, [SM] + [VM] * 5, [shape(3 * PAY, NS, kind=bf16)], [pltpu.VMEM((PAY, NS), f32)], 10**8
    )(masks, used, near_n, near_s, near_w, near_e)
    (bgc,) = call(
        spread_kernel, [VM], [shape(NS, 2 * K, kind=bf16)], [pltpu.VMEM((256, NS), f32)], 10**8
    )(bgt)
    came = coarse_phase(pay, parts, core)

    residual, *faces, pay, matrix = call(
        begin_kernel,
        [SM, pl.BlockSpec(memory_space=pl.ANY)] + [VM] * 4,
        [shape(NS, K)] + FACES + [shape(ROWS, PAY, K), shape(NS, NS, kind=bf16)],
        WORK + [pltpu.SemaphoreType.DMA((NS // TALL,))],
        2 * 10**9,
    )(order, schur_blocks[0, 0], bgt, bgc, came, local)

    state = ()
    for iteration in range(ITERS):
        near = (
            cyclic(faces[1], "row", 1),
            cyclic(faces[0], "row", -1),
            cyclic(faces[3], "col", 1),
            cyclic(faces[2], "col", -1),
        )
        came = coarse_phase(pay, parts, core)
        if iteration + 1 == ITERS:
            break
        first = iteration == 0
        given = (order, masks, matrix, bgt, bgc, came, residual, *near, *faces, *state)
        residual, along, moved, image, done, past, *faces, pay = call(
            functools.partial(step_kernel, first),
            [SM, SM] + [VM] * (len(given) - 2),
            [shape(NS, K), shape(2 * M, K), shape(NS, K), shape(NS, K), shape(2 * M, K), shape(SLOT, K)]
            + FACES
            + [shape(ROWS, PAY, K)],
            WORK,
            2 * 10**9,
        )(*given)
        state = (past, along, moved, image, done)

    past, along, moved, image, done = state
    done, residual = call(
        end_kernel,
        [SM] + [VM] * 11,
        [shape(2, K, M)] * 2,
        [pltpu.VMEM((256, K), f32)],
        10**8,
    )(masks, bgc, came, residual, near[1], near[3], faces[1], faces[3], past, along, moved, done)
    return (done[None, None], residual[None, None])


def solution(mesh):
    placed = (
        P("row", "col", None, None),
        P("row", "col", None, None),
        P("row", "col"),
        P("row", "col", None),
        P(None, "row", None, None, None, "col"),
        P("row", "col", None, None, None),
    )
    return jax.shard_map(
        per_device,
        mesh=mesh,
        in_specs=placed,
        out_specs=(P("row", "col", None, None, None), P("row", "col", None, None, None)),
        check_vma=False,
    )
```

```python
import functools

import jax
import jax.numpy as jnp
from jax import lax
from jax.experimental import pallas as pl
from jax.experimental.pallas import tpu as pltpu
from jax.sharding import PartitionSpec as P

M = 512
NS = 2048
BLK = 128
NB = 16
K = 128
ROWS = 8
COLS = 32
MODES = 6
ITERS = 3
SLOT = 8
SLOTS = 5
PAY = 48
TERMS = ((0, 0), (0, 1), (1, 0), (1, 1), (0, 2), (2, 0))
TALL = 1024
CHIPS = 16

f32 = jnp.float32
bf16 = jnp.bfloat16
VM = pl.BlockSpec(memory_space=pltpu.VMEM)
SM = pl.BlockSpec(memory_space=pltpu.SMEM)
HB = pl.BlockSpec(memory_space=pltpu.HBM)
LIMIT = pltpu.CompilerParams(vmem_limit_bytes=56 * 1024 * 1024)
SMALL = pltpu.CompilerParams(vmem_limit_bytes=8 * 1024 * 1024)


def cyclic(value, axis, steps):
    count = lax.axis_size(axis)
    return lax.ppermute(value, axis, [(s, (s + steps) % count) for s in range(count)])


def shifted(value, axis, steps):
    count = lax.axis_size(axis)
    initial, last = (max(0, -steps), min(count, count - steps))
    return lax.ppermute(value, axis, [(s, s + steps) for s in range(initial, last)])


def swapped(value, partner):
    return lax.ppermute(value, "col", [(s, partner(s)) for s in range(COLS)])


def parts_of(value, count):
    pieces = []
    for _ in range(count):
        piece = value.astype(bf16)
        pieces.append(piece)
        value = value - piece.astype(f32)
    return pieces


class Copies:
    def __init__(self, sems):
        self.sems, self.used, self.open = sems, 0, []

    def start(self, source, target):
        copy = pltpu.make_async_copy(source, target, self.sems.at[self.used])
        copy.start()
        self.used += 1
        return copy

    def out(self, source, target):
        self.open.append(self.start(source, target))

    def close(self):
        for copy in self.open:
            copy.wait()


def wait(copies):
    for copy in copies:
        copy.wait()


def own_modes(full, own, masks):
    for block in range(NB):
        face = block // (M // BLK)
        value = own[block] * masks[face] if face % 2 == 0 else own[block]
        full[0:SLOT, BLK * block : BLK * (block + 1)] = value


def start_kernel(
    masks, own, side, from_n, from_w, local, pay,
    own_v, side_v, near_v, local_v, full, halves, pay_v, sems,
):
    copies = Copies(sems)
    ready = [copies.start(own, own_v), copies.start(side.at[0], side_v.at[0]), copies.start(side.at[1], side_v.at[1])]
    near = [copies.start(from_n, near_v.at[0]), copies.start(from_w, near_v.at[1])]
    full[...] = jnp.zeros_like(full)
    wait(ready)
    own_modes(full, own_v, masks)
    for pair in range(2):
        wait(near[pair : pair + 1])
        for kind in range(2):
            face = 2 * pair + kind
            for block in range(M // BLK):
                inside = slice(BLK * block, BLK * (block + 1))
                rows = slice(M * face + BLK * block, M * face + BLK * (block + 1))
                if kind:
                    turned = side_v[pair, :, inside].T
                else:
                    turned = near_v[pair, :, inside].T * -masks[face]
                local_v[rows, :] = turned
                high, low = parts_of(turned, 2)
                halves[rows, :K] = high
                halves[rows, K:] = low
        wide = pl.ds(2 * M * pair, 2 * M)
        copies.out(local_v.at[wide], local.at[wide])
    pieces = jnp.concatenate(parts_of(full[...], 2), axis=0)
    d = jnp.dot(pieces, halves[...], preferred_element_type=f32)
    value = d[0:16, :K] + d[0:16, K:] + d[16:32, :K] + d[16:32, K:]
    pay_v[...] = jnp.zeros_like(pay_v)
    pay_v[0:SLOT, :] = value[0:SLOT]
    for index in range(ROWS):
        copies.out(pay_v, pay.at[index])
    copies.close()


def setup_kernel(
    order, masks, core, own, mine, down, up, right, left, far, bgt, bgc, parts,
    own_v, mine_v, down_v, up_v, right_v, left_v, far_v, full, turned, table, bgt_v, bgc_v, parts_v, sems,
):
    copies = Copies(sems)
    pairs = ((own, own_v), (mine, mine_v), (down, down_v), (up, up_v), (right, right_v), (left, left_v), (far, far_v))
    ready = [copies.start(source, target) for source, target in pairs]
    full[...] = jnp.zeros_like(full)
    wait(ready)
    own_modes(full, own_v, masks)
    for slot, (near, at) in enumerate(((down_v, COLS), (up_v, COLS), (right_v, 3 * COLS), (left_v, 3 * COLS))):
        rows = slice(SLOT * (slot + 1), SLOT * (slot + 2))
        for block in range(M // BLK):
            lanes = slice(M * slot + BLK * block, M * slot + BLK * (block + 1))
            full[rows, lanes] = near[at + block] * -masks[slot]
    pieces = parts_of(full[...], 3)
    for index, (which, _) in enumerate(TERMS):
        turned[40 * index : 40 * (index + 1), :] = pieces[which][0:40].astype(f32)
    turned[240:256, :] = jnp.zeros((16, NS), f32)
    for block in range(NB):
        for half in range(2):
            piece = turned[BLK * half : BLK * (half + 1), BLK * block : BLK * (block + 1)].T
            bgc_v[BLK * block : BLK * (block + 1), BLK * half : BLK * (half + 1)] = piece.astype(bf16)
    copies.out(bgc_v, bgc)
    for block in range(NB):
        at = pl.multiple_of(order[block] * BLK, BLK)
        for index, piece in enumerate(parts_of(full[:, pl.ds(at, BLK)], 2)):
            bgt_v[PAY * index : PAY * (index + 1), BLK * block : BLK * (block + 1)] = piece
    copies.out(bgt_v, bgt)

    first = core[0] == 0
    half = lax.broadcasted_iota(jnp.int32, (SLOT, BLK), 1) < SLOT * ROWS

    @pl.loop(0, CHIPS)
    def _(target):
        at = 2 * target + core[0]
        picks = ((0, at), (1, at), (2, at), (0, jnp.maximum(at - 1, 0)), (0, jnp.minimum(at + 1, COLS - 1)))
        for slot, (line, column) in enumerate(picks):
            w, e, f = (ref[COLS * line + column] for ref in (right_v, left_v, far_v))
            m = (mine_v[column], down_v[column], up_v[column])[line]
            inner = jnp.where(half, jnp.where(first, w, f), jnp.where(first, m, w))
            outer = jnp.where(half, jnp.where(first, e, m), jnp.where(first, f, e))
            rows = pl.ds(pl.multiple_of((target * SLOTS + slot) * SLOT, SLOT), SLOT)
            table[rows, :K] = inner
            table[rows, K:] = outer

    for index, piece in enumerate(parts_of(table[...], 2)):
        parts_v[index] = piece
        copies.out(parts_v.at[index], parts.at[index])
    copies.close()


def coarse_kernel(core, parts, own_v, other_v, out, parts_v, entries, out_v, sems):
    copies = Copies(sems)
    table = [copies.start(parts.at[index], parts_v.at[index]) for index in range(2)]
    first = core[0] == 0

    def tile(which, line, slot):
        here = slice(SLOT * slot, SLOT * (slot + 1))
        a, b = own_v[line, here, :], other_v[line, here, :]
        return jnp.where(first, a, b) if which == 0 else jnp.where(first, b, a)

    total = jnp.zeros((SLOT, K), f32)
    for line in range(ROWS):
        for which in range(2):
            value = tile(which, line, 0)
            if line > 0:
                value = value + tile(which, line - 1, 2)
            if line < ROWS - 1:
                value = value + tile(which, line + 1, 1)
            value = value + tile(1 - which, line, 3 + which)
            at = SLOT * (ROWS * (which + 1) + line)
            entries[at : at + SLOT, :] = value
        entries[SLOT * line : SLOT * (line + 1), :] = tile(0, line, 3)
        at = SLOT * (ROWS * 3 + line)
        entries[at : at + SLOT, :] = tile(1, line, 4)
        total = total + own_v[line, SLOT * SLOTS :, :] + other_v[line, SLOT * SLOTS :, :]
    both = jnp.concatenate(parts_of(entries[...], 2), axis=1)
    wait(table)
    d = jnp.dot(parts_v[0], both, preferred_element_type=f32)
    e = jnp.dot(parts_v[1], both, preferred_element_type=f32)
    value = e[:, K:] + e[:, :K] + d[:, K:] + d[:, :K]
    for target in range(CHIPS):
        out_v[target] = value[SLOTS * SLOT * target : SLOTS * SLOT * (target + 1)]
        out_v[target, 6:8, :] = total[0:2]
        out_v[target, 14:15, :] = total[2:3]
    copies.out(out_v, out)
    copies.close()


def take_values(came, stack):
    value = came[0]
    for index in range(1, CHIPS):
        value = value + came[index]
    spare = lax.broadcasted_iota(jnp.int32, (SLOT * SLOTS, K), 0) % SLOT >= MODES
    pieces = parts_of(jnp.where(spare, 0.0, value), 3)
    for index, (_, right) in enumerate(TERMS):
        stack[40 * index : 40 * (index + 1), :] = pieces[right].astype(f32)
    stack[240:256, :] = jnp.zeros((16, K), f32)
    return stack[...].astype(bf16), (value[6:7], value[7:8], value[14:15])


def folded(value):
    return jnp.sum(value.reshape(-1, SLOT, K), axis=0)


def schur_product(order, copies, matrix, turn, bgt, residual, halves, product):
    wait(turn)

    def tall(step, carry):
        value, energy = carry
        matrix.wait(step)
        rows = matrix.held[pl.ds(pl.multiple_of(step * TALL, TALL), TALL), :]
        both = jnp.dot(rows, halves[...], preferred_element_type=f32)
        both = both[:, :K] + both[:, K:]
        d = jnp.dot(
            bgt[:, pl.ds(pl.multiple_of(step * TALL, TALL), TALL)],
            jnp.concatenate(parts_of(both, 2), axis=1),
            preferred_element_type=f32,
        )
        value = value + d[:PAY, :K] + d[:PAY, K:] + d[PAY:, :K] + d[PAY:, K:]
        for piece in range(TALL // BLK):
            at = pl.multiple_of(order[step * (TALL // BLK) + piece] * BLK, BLK)
            y = both[BLK * piece : BLK * (piece + 1)]
            product[pl.ds(at, BLK), :] = y
            energy = energy + folded(residual[pl.ds(at, BLK), :] * y)
        return value, energy

    return lax.fori_loop(0, NS // TALL, tall, (jnp.zeros((PAY, K), f32), jnp.zeros((SLOT, K), f32)))


class Matrix:
    def __init__(self, source, held, sems):
        self.source, self.held, self.sems = source, held, sems

    def copy(self, step):
        rows = pl.ds(TALL * step if isinstance(step, int) else pl.multiple_of(step * TALL, TALL), TALL)
        return pltpu.make_async_copy(self.source.at[rows], self.held.at[rows], self.sems.at[step])

    def start(self, step):
        self.copy(step).start()

    def wait(self, step):
        self.copy(step).wait()


def put_halves(value, halves, at):
    high, low = parts_of(value, 2)
    halves[pl.ds(pl.multiple_of(at * BLK, BLK), BLK), :K] = high
    halves[pl.ds(pl.multiple_of(at * BLK, BLK), BLK), K:] = low


def invert(order, inverse):
    for block in range(NB):
        inverse[order[block]] = block


def close_product(value, norm, energy, cross, product, pay, faces, copies, pay_held):
    for face in range(4):
        copies.out(product.at[pl.ds(M * face, M)], faces[face])
    pay_held[0:PAY, :] = value
    pay_held[40:41, :] = jnp.sum(norm, axis=0, keepdims=True)
    pay_held[41:42, :] = jnp.sum(energy, axis=0, keepdims=True)
    pay_held[42:43, :] = jnp.sum(cross, axis=0, keepdims=True)
    for index in range(ROWS):
        copies.out(pay_held, pay.at[index])
    copies.close()


def begin_kernel(
    order, matrix, bgt, bgc, came, local, residual, yn, ys, yw, ye, pay,
    inverse, held, bgt_v, bgc_v, came_v, r_v, halves, product, spread, stack, pay_v, sems, tall_sems,
):
    copies, matrix = Copies(sems), Matrix(matrix, held, tall_sems)
    head = [copies.start(came, came_v), copies.start(bgc, bgc_v)]
    body = [copies.start(local.at[pl.ds(M * face, M)], r_v.at[pl.ds(M * face, M)]) for face in range(4)]
    matrix.start(0)
    turn = [copies.start(bgt, bgt_v)]
    invert(order, inverse)
    wait(head)
    matrix.start(1)
    stacked, _ = take_values(came_v, stack)
    norm = jnp.zeros((SLOT, K), f32)
    for face in range(4):
        inner = slice(M * face, M * (face + 1))
        spread[0:M, :] = jnp.dot(bgc_v[inner, :], stacked, preferred_element_type=f32)
        wait(body[face : face + 1])

        def block(index, norm, face=face):
            rows = pl.ds(pl.multiple_of(M * face + BLK * index, BLK), BLK)
            r = r_v[rows, :] - spread[pl.ds(pl.multiple_of(BLK * index, BLK), BLK), :]
            r_v[rows, :] = r
            put_halves(r, halves, inverse[M // BLK * face + index])
            return norm + folded(r * r) if face % 2 else norm

        norm = lax.fori_loop(0, M // BLK, block, norm)
        copies.out(r_v.at[inner], residual.at[inner])
    value, energy = schur_product(order, copies, matrix, turn, bgt_v, r_v, halves, product)
    close_product(value, norm, energy, jnp.zeros_like(norm), product, pay, (yn, ys, yw, ye), copies, pay_v)


def scalars(first, sums, past):
    norm, energy, cross = sums
    if first:
        return norm, energy, None, norm / energy
    ratio = norm / past[0:1, :]
    curvature = energy + 2.0 * ratio * cross + ratio * ratio * past[1:2, :]
    return norm, curvature, ratio, norm / curvature


def step_kernel(first, *refs):
    order, masks, matrix, bgt, bgc, came, residual = refs[:7]
    near, faces = refs[7:11], refs[11:15]
    refs = refs[15:]
    if not first:
        past, along, moved, image, done = refs[:5]
        refs = refs[5:]
    new_residual, new_along, new_moved, new_image, new_done, new_past = refs[:6]
    new_faces, pay, refs = refs[6:10], refs[10], refs[11:]
    (inverse, held, bgt_v, bgc_v, came_v, r_v, halves, product, spread, stack, pay_v, sems, tall_sems,
     y_v, near_v, moved_v, image_v, along_v, done_v, past_v, new_past_v) = refs

    copies, matrix = Copies(sems), Matrix(matrix, held, tall_sems)
    head = [copies.start(came, came_v)]
    if not first:
        head.append(copies.start(past, past_v))
    head.append(copies.start(bgc, bgc_v))
    def fetch(pair):
        wide, own = pl.ds(2 * M * pair, 2 * M), pl.ds(M * pair, M)
        part = [copies.start(residual.at[wide], r_v.at[wide])]
        for face in (2 * pair, 2 * pair + 1):
            rows = pl.ds(M * face, M)
            part += [copies.start(faces[face], y_v.at[rows]), copies.start(near[face], near_v.at[rows])]
        if not first:
            part.append(copies.start(moved.at[wide], moved_v.at[wide]))
            for source, target in ((image, image_v), (along, along_v), (done, done_v)):
                part.append(copies.start(source.at[own], target.at[own]))
        return part

    body = [fetch(0)]
    matrix.start(0)
    invert(order, inverse)

    wait(head)
    stacked, sums = take_values(came_v, stack)
    norm, curvature, ratio, step = scalars(first, sums, past_v)
    new_past_v[...] = jnp.zeros_like(new_past_v)
    new_past_v[0:1, :] = norm
    new_past_v[1:2, :] = curvature
    copies.out(new_past_v, new_past)
    carry = (jnp.zeros((SLOT, K), f32), jnp.zeros((SLOT, K), f32))
    for pair in range(2):
        wide, own = pl.ds(2 * M * pair, 2 * M), pl.ds(M * pair, M)
        spread[...] = jnp.dot(bgc_v[2 * M * pair : 2 * M * (pair + 1), :], stacked, preferred_element_type=f32)
        wait(body[pair])
        if pair == 0:
            body.append(fetch(1))
            turn = [copies.start(bgt, bgt_v)]

        def block(index, carry, pair=pair):
            norm, cross = carry
            for kind in range(2):
                face = 2 * pair + kind
                rows = pl.ds(pl.multiple_of(M * face + BLK * index, BLK), BLK)
                mine = pl.ds(pl.multiple_of(M * pair + BLK * index, BLK), BLK)
                if kind:
                    q = y_v[rows, :] - masks[face] * near_v[rows, :]
                    f = q if first else q + ratio * image_v[mine, :]
                    image_v[mine, :] = f
                else:
                    q = masks[face] * (y_v[rows, :] - near_v[rows, :])
                q = q - spread[pl.ds(pl.multiple_of(M * kind + BLK * index, BLK), BLK), :]
                if not first:
                    q = q + ratio * moved_v[rows, :]
                moved_v[rows, :] = q
                r = r_v[rows, :]
                if kind:
                    if first:
                        along_v[mine, :] = r
                        done_v[mine, :] = step * r
                    else:
                        d = r + ratio * along_v[mine, :]
                        along_v[mine, :] = d
                        done_v[mine, :] = done_v[mine, :] + step * d
                r = r - step * q
                r_v[rows, :] = r
                put_halves(r, halves, inverse[M // BLK * face + index])
                if kind:
                    norm = norm + folded(r * r)
                    cross = cross + folded(r * f)
            return norm, cross

        carry = lax.fori_loop(0, M // BLK, block, carry)
        if pair == 0:
            matrix.start(1)
        for source, target in ((r_v, new_residual), (moved_v, new_moved)):
            copies.out(source.at[wide], target.at[wide])
        for source, target in ((image_v, new_image), (along_v, new_along), (done_v, new_done)):
            copies.out(source.at[own], target.at[own])
    value, energy = schur_product(order, copies, matrix, turn, bgt_v, r_v, halves, product)
    close_product(value, carry[0], energy, carry[1], product, pay, new_faces, copies, pay_v)


def end_kernel(
    masks, bgc, came, residual, ns, ne, ys, ye, past, along, moved, done, out_done, out_residual,
    stack, bgc_v, came_v, past_v, r_v, near_v, y_v, along_v, moved_v, done_v, x_v, s_v, sems,
):
    copies = Copies(sems)
    head = [copies.start(came, came_v), copies.start(past, past_v)]
    body = []
    for pair, near, mine in ((0, ns, ys), (1, ne, ye)):
        rows, own = pl.ds(M * (2 * pair + 1), M), pl.ds(M * pair, M)
        part = [copies.start(bgc.at[rows], bgc_v.at[own]), copies.start(near, near_v.at[own])]
        part += [copies.start(mine, y_v.at[own]), copies.start(residual.at[rows], r_v.at[own])]
        part += [copies.start(moved.at[rows], moved_v.at[own]), copies.start(along.at[own], along_v.at[own])]
        body.append(part + [copies.start(done.at[own], done_v.at[own])])
    wait(head)
    stacked, sums = take_values(came_v, stack)
    _, _, ratio, step = scalars(False, sums, past_v)
    for pair in range(2):
        wait(body[pair])
        for block in range(M // BLK):
            inside = slice(BLK * block, BLK * (block + 1))
            own = slice(M * pair + BLK * block, M * pair + BLK * (block + 1))
            q = y_v[own, :] - masks[2 * pair + 1] * near_v[own, :]
            q = q - jnp.dot(bgc_v[own, :], stacked, preferred_element_type=f32)
            q = q + ratio * moved_v[own, :]
            r = r_v[own, :]
            d = r + ratio * along_v[own, :]
            s_v[pair, :, inside] = (r - step * q).T
            x_v[pair, :, inside] = (done_v[own, :] + step * d).T
        copies.out(s_v.at[pair], out_residual.at[pair])
        copies.out(x_v.at[pair], out_done.at[pair])
    copies.close()


def shape(*dims, kind=f32):
    return jax.ShapeDtypeStruct(dims, kind)


WORK = [
    pltpu.SMEM((NB,), jnp.int32),
    pltpu.VMEM((NS, NS), bf16),
    pltpu.VMEM((2 * PAY, NS), bf16),
    pltpu.VMEM((NS, 2 * K), bf16),
    pltpu.VMEM((CHIPS, SLOTS * SLOT, K), f32),
    pltpu.VMEM((NS, K), f32),
    pltpu.VMEM((NS, 2 * K), bf16),
    pltpu.VMEM((NS, K), f32),
    pltpu.VMEM((2 * M, K), f32),
    pltpu.VMEM((256, K), f32),
    pltpu.VMEM((PAY, K), f32),
    pltpu.SemaphoreType.DMA((64,)),
    pltpu.SemaphoreType.DMA((NS // TALL,)),
]
MORE = [pltpu.VMEM((NS, K), f32)] * 3 + [pltpu.VMEM((2 * M, K), f32)] * 3 + [pltpu.VMEM((SLOT, K), f32)] * 2
LAST = (
    [pltpu.VMEM((256, K), f32), pltpu.VMEM((2 * M, 2 * K), bf16), pltpu.VMEM((CHIPS, SLOTS * SLOT, K), f32)]
    + [pltpu.VMEM((SLOT, K), f32)]
    + [pltpu.VMEM((2 * M, K), f32)] * 6
    + [pltpu.VMEM((2, K, M), f32)] * 2
    + [pltpu.SemaphoreType.DMA((32,))]
)
FACES = [shape(M, K)] * 4


def call(kernel, specs, outs, scratch, flops, place, limit=LIMIT):
    return pl.pallas_call(
        kernel,
        in_specs=specs,
        out_specs=[place] * len(outs),
        out_shape=outs,
        scratch_shapes=scratch,
        compiler_params=limit,
        cost_estimate=pl.CostEstimate(flops=flops, bytes_accessed=1 << 20, transcendentals=0),
    )


def coarse_phase(pay, parts, core):
    own = lax.all_to_all(pay, "row", 0, 0, tiled=True)
    other = swapped(own, lambda c: c ^ 1)
    (terms,) = call(
        coarse_kernel,
        [SM, HB, VM, VM],
        [shape(CHIPS, SLOTS * SLOT, K)],
        [
            pltpu.VMEM((2, CHIPS * SLOTS * SLOT, 2 * K), bf16),
            pltpu.VMEM((2 * K, K), f32),
            pltpu.VMEM((CHIPS, SLOTS * SLOT, K), f32),
            pltpu.SemaphoreType.DMA((8,)),
        ],
        10**8,
        HB,
        SMALL,
    )(core, parts, own, other)
    groups = [[2 * chip + which for chip in range(CHIPS)] for which in range(2)]
    return lax.all_to_all(terms, "col", 0, 0, axis_index_groups=groups, tiled=True)


def per_device(schur_blocks, rigid_modes, floating, block_order, coarse_inverse, right_side):
    order = block_order[0, 0]
    row, col = lax.axis_index("row"), lax.axis_index("col")
    core = (col % 2).astype(jnp.int32).reshape(1)
    masks = jnp.stack([row > 0, row < ROWS - 1, col > 0, col < COLS - 1]).astype(f32)
    side = right_side[0, 0]

    from_n = cyclic(side[0], "row", 1)
    from_w = cyclic(side[1], "col", 1)
    modes = (rigid_modes[0, 0] * floating[0, 0].astype(f32)).reshape(MODES, NB, BLK)
    modes = jnp.pad(jnp.transpose(modes, (1, 0, 2)), ((0, 0), (0, SLOT - MODES), (0, 0)))
    local, pay = call(
        start_kernel,
        [SM] + [HB] * 4,
        [shape(NS, K), shape(ROWS, PAY, K)],
        [
            pltpu.VMEM((NB, SLOT, BLK), f32),
            pltpu.VMEM((2, K, M), f32),
            pltpu.VMEM((2, K, M), f32),
            pltpu.VMEM((NS, K), f32),
            pltpu.VMEM((16, NS), f32),
            pltpu.VMEM((NS, 2 * K), bf16),
            pltpu.VMEM((PAY, K), f32),
            pltpu.SemaphoreType.DMA((16,)),
        ],
        10**8,
        HB,
    )(masks, modes, side, from_n, from_w)

    mine = jnp.transpose(coarse_inverse[:, 0, :, :, :, 0], (1, 0, 3, 2))
    mine = jnp.pad(mine, ((0, 0), (0, SLOT - MODES), (0, 0), (0, SLOT - MODES))).reshape(COLS, SLOT, SLOT * ROWS)
    mine = jnp.concatenate([mine, mine], axis=2)
    down = cyclic(jnp.concatenate([mine, modes[4:8]], axis=0), "row", 1)
    up = cyclic(jnp.concatenate([mine, modes[0:4]], axis=0), "row", -1)
    down, up, pay = lax.optimization_barrier((down, up, pay))
    lines = jnp.concatenate([mine, down[:COLS], up[:COLS]], axis=0)
    right = cyclic(jnp.concatenate([lines, modes[12:16]], axis=0), "col", 1)
    left = cyclic(jnp.concatenate([lines, modes[8:12]], axis=0), "col", -1)
    far = swapped(jnp.where(core[0] == 0, right[: 3 * COLS], left[: 3 * COLS]), lambda c: c ^ 1)
    bgt, bgc, parts = call(
        setup_kernel,
        [SM] * 3 + [HB] * 7,
        [shape(2 * PAY, NS, kind=bf16), shape(NS, 2 * K, kind=bf16), shape(2, CHIPS * SLOTS * SLOT, 2 * K, kind=bf16)],
        [pltpu.VMEM((tiles, SLOT, BLK), f32) for tiles in (NB, COLS, COLS + 4, COLS + 4, 3 * COLS + 4, 3 * COLS + 4, 3 * COLS)]
        + [
            pltpu.VMEM((PAY, NS), f32),
            pltpu.VMEM((256, NS), f32),
            pltpu.VMEM((CHIPS * SLOTS * SLOT, 2 * K), f32),
            pltpu.VMEM((2 * PAY, NS), bf16),
            pltpu.VMEM((NS, 2 * K), bf16),
            pltpu.VMEM((2, CHIPS * SLOTS * SLOT, 2 * K), bf16),
            pltpu.SemaphoreType.DMA((16,)),
        ],
        10**8,
        HB,
    )(order, masks, core, modes, mine, down, up, right, left, far)
    came = coarse_phase(pay, parts, core)

    matrix = schur_blocks[0, 0]
    residual, *faces, pay = call(
        begin_kernel,
        [SM] + [HB] * 5,
        [shape(NS, K)] + FACES + [shape(ROWS, PAY, K)],
        WORK,
        2 * 10**9,
        HB,
    )(order, matrix, bgt, bgc, came, local)

    state = ()
    for iteration in range(ITERS):
        north, south = cyclic(faces[1], "row", 1), cyclic(faces[0], "row", -1)
        west, east = cyclic(faces[3], "col", 1), cyclic(faces[2], "col", -1)
        near = (north, south, west, east)
        came = coarse_phase(pay, parts, core)
        if iteration + 1 == ITERS:
            break
        first = iteration == 0
        given = (order, masks, matrix, bgt, bgc, came, residual, *near, *faces, *state)
        residual, along, moved, image, done, past, *faces, pay = call(
            functools.partial(step_kernel, first),
            [SM, SM] + [HB] * (len(given) - 2),
            [shape(NS, K), shape(2 * M, K), shape(NS, K), shape(2 * M, K), shape(2 * M, K), shape(SLOT, K)]
            + FACES
            + [shape(ROWS, PAY, K)],
            WORK + MORE,
            2 * 10**9,
            HB,
        )(*given)
        state = (past, along, moved, image, done)

    past, along, moved, image, done = state
    done, residual = call(
        end_kernel,
        [SM] + [HB] * 11,
        [shape(2, K, M)] * 2,
        LAST,
        10**8,
        HB,
    )(masks, bgc, came, residual, near[1], near[3], faces[1], faces[3], past, along, moved, done)
    return (done[None, None], residual[None, None])


def solution(mesh):
    placed = (
        P("row", "col", None, None),
        P("row", "col", None, None),
        P("row", "col"),
        P("row", "col", None),
        P(None, "row", None, None, None, "col"),
        P("row", "col", None, None, None),
    )
    return jax.shard_map(
        per_device,
        mesh=mesh,
        in_specs=placed,
        out_specs=(P("row", "col", None, None, None), P("row", "col", None, None, None)),
        check_vma=False,
    )
```

```python
import functools

import jax
import jax.numpy as jnp
from jax import lax
from jax.experimental import pallas as pl
from jax.experimental.pallas import tpu as pltpu
from jax.sharding import PartitionSpec as P

M = 512
NS = 2048
BLK = 128
NB = 16
K = 128
ROWS = 8
COLS = 32
MODES = 6
ITERS = 3
SLOT = 8
SLOTS = 5
PAY = 40
ROWS16 = 48
TERMS = ((0, 0), (0, 1), (1, 0), (1, 1), (0, 2), (2, 0))
TALL = 1024
CHIPS = 16
COST = 2 * 10**10

f32 = jnp.float32
bf16 = jnp.bfloat16
VM = pl.BlockSpec(memory_space=pltpu.VMEM)
SM = pl.BlockSpec(memory_space=pltpu.SMEM)
HB = pl.BlockSpec(memory_space=pltpu.HBM)
LIMIT = pltpu.CompilerParams(vmem_limit_bytes=56 * 1024 * 1024)
SMALL = pltpu.CompilerParams(vmem_limit_bytes=8 * 1024 * 1024)


def cyclic(value, axis, steps):
    count = lax.axis_size(axis)
    return lax.ppermute(value, axis, [(s, (s + steps) % count) for s in range(count)])


def shifted(value, axis, steps):
    count = lax.axis_size(axis)
    initial, last = (max(0, -steps), min(count, count - steps))
    return lax.ppermute(value, axis, [(s, s + steps) for s in range(initial, last)])


def swapped(value, partner):
    return lax.ppermute(value, "col", [(s, partner(s)) for s in range(COLS)])


def parts_of(value, count):
    pieces = []
    for _ in range(count):
        piece = value.astype(bf16)
        pieces.append(piece)
        value = value - piece.astype(f32)
    return pieces


class Copies:
    def __init__(self, sems):
        self.sems, self.used, self.open = sems, 0, []

    def start(self, source, target):
        copy = pltpu.make_async_copy(source, target, self.sems.at[self.used])
        copy.start()
        self.used += 1
        return copy

    def out(self, source, target):
        self.open.append(self.start(source, target))

    def close(self):
        for copy in self.open:
            copy.wait()


def wait(copies):
    for copy in copies:
        copy.wait()


def own_modes(full, own, masks):
    for block in range(NB):
        face = block // (M // BLK)
        value = own[block] * masks[face] if face % 2 == 0 else own[block]
        full[0:SLOT, BLK * block : BLK * (block + 1)] = value


def start_kernel(
    masks, own, side, from_n, from_w, local, pay,
    own_v, side_v, near_v, local_v, full, halves, pay_v, sems,
):
    copies = Copies(sems)
    ready = [copies.start(own, own_v), copies.start(side.at[0], side_v.at[0]), copies.start(side.at[1], side_v.at[1])]
    near = [copies.start(from_n, near_v.at[0]), copies.start(from_w, near_v.at[1])]
    full[...] = jnp.zeros_like(full)
    wait(ready)
    own_modes(full, own_v, masks)
    for pair in range(2):
        wait(near[pair : pair + 1])
        for kind in range(2):
            face = 2 * pair + kind
            for block in range(M // BLK):
                inside = slice(BLK * block, BLK * (block + 1))
                rows = slice(M * face + BLK * block, M * face + BLK * (block + 1))
                if kind:
                    turned = side_v[pair, :, inside].T
                else:
                    turned = near_v[pair, :, inside].T * -masks[face]
                local_v[rows, :] = turned
                high, low = parts_of(turned, 2)
                halves[rows, :K] = high
                halves[rows, K:] = low
        wide = pl.ds(2 * M * pair, 2 * M)
        copies.out(local_v.at[wide], local.at[wide])
    pieces = jnp.concatenate(parts_of(full[...], 2), axis=0)
    d = jnp.dot(pieces, halves[...], preferred_element_type=f32)
    value = d[0:16, :K] + d[0:16, K:] + d[16:32, :K] + d[16:32, K:]
    pay_v[...] = jnp.zeros_like(pay_v)
    pay_v[0:SLOT, :] = value[0:SLOT]
    for index in range(ROWS):
        copies.out(pay_v, pay.at[index])
    copies.close()


def modes_kernel(
    order, masks, own, down, up, right, left, bgt, bgc,
    own_v, down_v, up_v, right_v, left_v, full, turned, bgt_v, bgc_v, sems,
):
    copies = Copies(sems)
    ready = [copies.start(own, own_v)]
    for source, target in ((down, down_v), (up, up_v)):
        ready.append(copies.start(source.at[pl.ds(COLS, 4)], target))
    for source, target in ((right, right_v), (left, left_v)):
        ready.append(copies.start(source.at[pl.ds(3 * COLS, 4)], target))
    full[...] = jnp.zeros_like(full)
    wait(ready)
    own_modes(full, own_v, masks)
    for slot, near in enumerate((down_v, up_v, right_v, left_v)):
        rows = slice(SLOT * (slot + 1), SLOT * (slot + 2))
        for block in range(M // BLK):
            lanes = slice(M * slot + BLK * block, M * slot + BLK * (block + 1))
            full[rows, lanes] = near[block] * -masks[slot]
    pieces = parts_of(full[...], 3)
    for index, (which, _) in enumerate(TERMS):
        turned[40 * index : 40 * (index + 1), :] = pieces[which][0:40].astype(f32)
    turned[240:256, :] = jnp.zeros((16, NS), f32)
    for block in range(NB):
        for half in range(2):
            piece = turned[BLK * half : BLK * (half + 1), BLK * block : BLK * (block + 1)].T
            bgc_v[BLK * block : BLK * (block + 1), BLK * half : BLK * (half + 1)] = piece.astype(bf16)
    copies.out(bgc_v, bgc)
    for block in range(NB):
        at = pl.multiple_of(order[block] * BLK, BLK)
        for index, piece in enumerate(parts_of(full[:, pl.ds(at, BLK)], 2)):
            bgt_v[ROWS16 * index : ROWS16 * (index + 1), BLK * block : BLK * (block + 1)] = piece
    copies.out(bgt_v, bgt)
    copies.close()


def table_kernel(
    core, mine, down, up, right, left, far, parts,
    mine_v, down_v, up_v, right_v, left_v, far_v, table, parts_v, sems,
):
    copies = Copies(sems)
    pairs = ((mine, mine_v), (down, down_v), (up, up_v), (right, right_v), (left, left_v), (far, far_v))
    wait([copies.start(source, target) for source, target in pairs])
    first = core[0] == 0
    half = lax.broadcasted_iota(jnp.int32, (SLOT, BLK), 1) < SLOT * ROWS

    @pl.loop(0, CHIPS)
    def _(target):
        at = 2 * target + core[0]
        picks = ((0, at), (1, at), (2, at), (0, jnp.maximum(at - 1, 0)), (0, jnp.minimum(at + 1, COLS - 1)))
        for slot, (line, column) in enumerate(picks):
            w, e, f = (ref[COLS * line + column] for ref in (right_v, left_v, far_v))
            m = (mine_v[column], down_v[column], up_v[column])[line]
            inner = jnp.where(half, jnp.where(first, w, f), jnp.where(first, m, w))
            outer = jnp.where(half, jnp.where(first, e, m), jnp.where(first, f, e))
            rows = pl.ds(pl.multiple_of((target * SLOTS + slot) * SLOT, SLOT), SLOT)
            table[rows, :K] = inner
            table[rows, K:] = outer

    for index, piece in enumerate(parts_of(table[...], 2)):
        parts_v[index] = piece
        copies.out(parts_v.at[index], parts.at[index])
    copies.close()


def coarse_kernel(core, parts, own_v, other_v, out, parts_v, entries, out_v, sems):
    copies = Copies(sems)
    table = [copies.start(parts.at[index], parts_v.at[index]) for index in range(2)]
    first = core[0] == 0

    def tile(which, line, slot):
        here = slice(SLOT * slot, SLOT * (slot + 1))
        a, b = own_v[line, here, :], other_v[line, here, :]
        return jnp.where(first, a, b) if which == 0 else jnp.where(first, b, a)

    total = jnp.zeros((2 * SLOT, K), f32)
    for line in range(ROWS):
        for which in range(2):
            value = tile(which, line, 0)
            if line > 0:
                value = value + tile(which, line - 1, 2)
            if line < ROWS - 1:
                value = value + tile(which, line + 1, 1)
            value = value + tile(1 - which, line, 3 + which)
            at = SLOT * (ROWS * (which + 1) + line)
            entries[at : at + SLOT, :] = value
        entries[SLOT * line : SLOT * (line + 1), :] = tile(0, line, 3)
        at = SLOT * (ROWS * 3 + line)
        entries[at : at + SLOT, :] = tile(1, line, 4)
        total = total + own_v[line, : 2 * SLOT, :] + other_v[line, : 2 * SLOT, :]
    both = jnp.concatenate(parts_of(entries[...], 2), axis=1)
    wait(table)
    d = jnp.dot(parts_v[0], both, preferred_element_type=f32)
    e = jnp.dot(parts_v[1], both, preferred_element_type=f32)
    value = e[:, K:] + e[:, :K] + d[:, K:] + d[:, :K]
    for target in range(CHIPS):
        out_v[target] = value[SLOTS * SLOT * target : SLOTS * SLOT * (target + 1)]
        out_v[target, 6:8, :] = total[6:8]
        out_v[target, 14:15, :] = total[14:15]
    copies.out(out_v, out)
    copies.close()


def take_values(came, stack):
    value = came[0]
    for index in range(1, CHIPS):
        value = value + came[index]
    spare = lax.broadcasted_iota(jnp.int32, (SLOT * SLOTS, K), 0) % SLOT >= MODES
    pieces = parts_of(jnp.where(spare, 0.0, value), 3)
    for index, (_, right) in enumerate(TERMS):
        stack[40 * index : 40 * (index + 1), :] = pieces[right].astype(f32)
    stack[240:256, :] = jnp.zeros((16, K), f32)
    return stack[...].astype(bf16), (value[6:7], value[7:8], value[14:15])


def folded(value):
    return jnp.sum(value.reshape(-1, SLOT, K), axis=0)


def schur_product(order, copies, matrix, turn, bgt, residual, halves, product):
    wait(turn)

    def tall(step, carry):
        value, energy = carry
        matrix.wait(step)
        rows = matrix.held[pl.ds(pl.multiple_of(step * TALL, TALL), TALL), :]
        both = jnp.dot(rows, halves[...], preferred_element_type=f32)
        both = both[:, :K] + both[:, K:]
        d = jnp.dot(
            bgt[:, pl.ds(pl.multiple_of(step * TALL, TALL), TALL)],
            jnp.concatenate(parts_of(both, 2), axis=1),
            preferred_element_type=f32,
        )
        value = value + d[:ROWS16, :K] + d[:ROWS16, K:] + d[ROWS16:, :K] + d[ROWS16:, K:]
        for piece in range(TALL // BLK):
            at = pl.multiple_of(order[step * (TALL // BLK) + piece] * BLK, BLK)
            y = both[BLK * piece : BLK * (piece + 1)]
            product[pl.ds(at, BLK), :] = y
            energy = energy + folded(residual[pl.ds(at, BLK), :] * y)
        return value, energy

    return lax.fori_loop(0, NS // TALL, tall, (jnp.zeros((ROWS16, K), f32), jnp.zeros((SLOT, K), f32)))


class Matrix:
    def __init__(self, source, held, sems):
        self.source, self.held, self.sems = source, held, sems

    def copy(self, step):
        rows = pl.ds(TALL * step if isinstance(step, int) else pl.multiple_of(step * TALL, TALL), TALL)
        return pltpu.make_async_copy(self.source.at[rows], self.held.at[rows], self.sems.at[step])

    def start(self, step):
        self.copy(step).start()

    def wait(self, step):
        self.copy(step).wait()


def put_halves(value, halves, at):
    high, low = parts_of(value, 2)
    halves[pl.ds(pl.multiple_of(at * BLK, BLK), BLK), :K] = high
    halves[pl.ds(pl.multiple_of(at * BLK, BLK), BLK), K:] = low


def invert(order, inverse):
    for block in range(NB):
        inverse[order[block]] = block


def close_product(value, norm, energy, cross, product, pay, faces, copies, pay_held):
    for face in range(4):
        copies.out(product.at[pl.ds(M * face, M)], faces[face])
    pay_held[...] = value[0:PAY]
    pay_held[6:7, :] = jnp.sum(norm, axis=0, keepdims=True)
    pay_held[7:8, :] = jnp.sum(energy, axis=0, keepdims=True)
    pay_held[14:15, :] = jnp.sum(cross, axis=0, keepdims=True)
    for index in range(ROWS):
        copies.out(pay_held, pay.at[index])
    copies.close()


def begin_kernel(
    order, matrix, bgt, bgc, came, local, residual, yn, ys, yw, ye, pay,
    inverse, held, bgt_v, bgc_v, came_v, r_v, halves, product, spread, stack, pay_v, sems, tall_sems,
):
    copies, matrix = Copies(sems), Matrix(matrix, held, tall_sems)
    head = [copies.start(came, came_v), copies.start(bgc, bgc_v)]
    body = [copies.start(local.at[pl.ds(M * face, M)], r_v.at[pl.ds(M * face, M)]) for face in range(4)]
    matrix.start(0)
    turn = [copies.start(bgt, bgt_v)]
    invert(order, inverse)
    wait(head)
    matrix.start(1)
    stacked, _ = take_values(came_v, stack)
    norm = jnp.zeros((SLOT, K), f32)
    for face in range(4):
        inner = slice(M * face, M * (face + 1))
        spread[0:M, :] = jnp.dot(bgc_v[inner, :], stacked, preferred_element_type=f32)
        wait(body[face : face + 1])

        def block(index, norm, face=face):
            rows = pl.ds(pl.multiple_of(M * face + BLK * index, BLK), BLK)
            r = r_v[rows, :] - spread[pl.ds(pl.multiple_of(BLK * index, BLK), BLK), :]
            r_v[rows, :] = r
            put_halves(r, halves, inverse[M // BLK * face + index])
            return norm + folded(r * r) if face % 2 else norm

        norm = lax.fori_loop(0, M // BLK, block, norm)
        copies.out(r_v.at[inner], residual.at[inner])
    value, energy = schur_product(order, copies, matrix, turn, bgt_v, r_v, halves, product)
    close_product(value, norm, energy, jnp.zeros_like(norm), product, pay, (yn, ys, yw, ye), copies, pay_v)


def image_kernel(which, *refs):
    masks, refs = refs[0], refs[1:]
    count = len(which)
    faces, near, image, (y_v, near_v, sems) = refs[:count], refs[count : 2 * count], refs[2 * count], refs[2 * count + 1 :]
    copies = Copies(sems)
    ready = []
    for index in range(count):
        ready.append([copies.start(faces[index], y_v.at[index]), copies.start(near[index], near_v.at[index])])
    for index, face in enumerate(which):
        wait(ready[index])
        if face % 2:
            y_v[index] = y_v[index] - masks[face] * near_v[index]
        else:
            y_v[index] = masks[face] * (y_v[index] - near_v[index])
        copies.out(y_v.at[index], image.at[index])
    copies.close()


def scalars(first, sums, past):
    norm, energy, cross = sums
    if first:
        return norm, energy, None, norm / energy
    ratio = norm / past[0:1, :]
    curvature = energy + 2.0 * ratio * cross + ratio * ratio * past[1:2, :]
    return norm, curvature, ratio, norm / curvature


def step_kernel(first, *refs):
    order, matrix, bgt, bgc, came, residual, local = refs[:7]
    refs = refs[7:]
    if not first:
        past, along, moved, image, done = refs[:5]
        refs = refs[5:]
    new_residual, new_along, new_moved, new_image, new_done, new_past = refs[:6]
    new_faces, pay, refs = refs[6:10], refs[10], refs[11:]
    (inverse, held, bgt_v, bgc_v, came_v, r_v, halves, product, spread, stack, pay_v, sems, tall_sems,
     local_v, moved_v, image_v, along_v, done_v, past_v, new_past_v) = refs

    copies, matrix = Copies(sems), Matrix(matrix, held, tall_sems)
    head = [copies.start(came, came_v)]
    if not first:
        head.append(copies.start(past, past_v))
    head.append(copies.start(bgc, bgc_v))
    def fetch(pair):
        wide, own = pl.ds(2 * M * pair, 2 * M), pl.ds(M * pair, M)
        part = [copies.start(residual.at[wide], r_v.at[wide])]
        part.append(copies.start(local.at[pl.ds(2 * pair, 2)], local_v.at[pl.ds(2 * pair, 2)]))
        if not first:
            part.append(copies.start(moved.at[wide], moved_v.at[wide]))
            for source, target in ((image, image_v), (along, along_v), (done, done_v)):
                part.append(copies.start(source.at[own], target.at[own]))
        return part

    body = [fetch(0)]
    matrix.start(0)
    invert(order, inverse)

    wait(head)
    stacked, sums = take_values(came_v, stack)
    norm, curvature, ratio, step = scalars(first, sums, past_v)
    new_past_v[...] = jnp.zeros_like(new_past_v)
    new_past_v[0:1, :] = norm
    new_past_v[1:2, :] = curvature
    copies.out(new_past_v, new_past)
    carry = (jnp.zeros((SLOT, K), f32), jnp.zeros((SLOT, K), f32))
    for pair in range(2):
        wide, own = pl.ds(2 * M * pair, 2 * M), pl.ds(M * pair, M)
        spread[...] = jnp.dot(bgc_v[2 * M * pair : 2 * M * (pair + 1), :], stacked, preferred_element_type=f32)
        wait(body[pair])
        if pair == 0:
            body.append(fetch(1))
            turn = [copies.start(bgt, bgt_v)]

        def block(index, carry, pair=pair):
            norm, cross = carry
            for kind in range(2):
                face = 2 * pair + kind
                rows = pl.ds(pl.multiple_of(M * face + BLK * index, BLK), BLK)
                mine = pl.ds(pl.multiple_of(M * pair + BLK * index, BLK), BLK)
                q = local_v[face, pl.ds(pl.multiple_of(BLK * index, BLK), BLK), :]
                if kind:
                    f = q if first else q + ratio * image_v[mine, :]
                    image_v[mine, :] = f
                q = q - spread[pl.ds(pl.multiple_of(M * kind + BLK * index, BLK), BLK), :]
                if not first:
                    q = q + ratio * moved_v[rows, :]
                moved_v[rows, :] = q
                r = r_v[rows, :]
                if kind:
                    if first:
                        along_v[mine, :] = r
                        done_v[mine, :] = step * r
                    else:
                        d = r + ratio * along_v[mine, :]
                        along_v[mine, :] = d
                        done_v[mine, :] = done_v[mine, :] + step * d
                r = r - step * q
                r_v[rows, :] = r
                put_halves(r, halves, inverse[M // BLK * face + index])
                if kind:
                    norm = norm + folded(r * r)
                    cross = cross + folded(r * f)
            return norm, cross

        carry = lax.fori_loop(0, M // BLK, block, carry)
        if pair == 0:
            matrix.start(1)
        for source, target in ((r_v, new_residual), (moved_v, new_moved)):
            copies.out(source.at[wide], target.at[wide])
        for source, target in ((image_v, new_image), (along_v, new_along), (done_v, new_done)):
            copies.out(source.at[own], target.at[own])
    value, energy = schur_product(order, copies, matrix, turn, bgt_v, r_v, halves, product)
    close_product(value, carry[0], energy, carry[1], product, pay, new_faces, copies, pay_v)


def end_kernel(
    bgc, came, residual, local, past, along, moved, done, out_done, out_residual,
    stack, bgc_v, came_v, past_v, r_v, local_v, along_v, moved_v, done_v, x_v, s_v, sems,
):
    copies = Copies(sems)
    head = [copies.start(came, came_v), copies.start(past, past_v)]
    body = []
    for pair in range(2):
        rows, own = pl.ds(M * (2 * pair + 1), M), pl.ds(M * pair, M)
        part = [copies.start(bgc.at[rows], bgc_v.at[own]), copies.start(local.at[pair], local_v.at[own])]
        part.append(copies.start(residual.at[rows], r_v.at[own]))
        part += [copies.start(moved.at[rows], moved_v.at[own]), copies.start(along.at[own], along_v.at[own])]
        body.append(part + [copies.start(done.at[own], done_v.at[own])])
    wait(head)
    stacked, sums = take_values(came_v, stack)
    _, _, ratio, step = scalars(False, sums, past_v)
    for pair in range(2):
        wait(body[pair])
        for block in range(M // BLK):
            inside = slice(BLK * block, BLK * (block + 1))
            own = slice(M * pair + BLK * block, M * pair + BLK * (block + 1))
            q = local_v[own, :] - jnp.dot(bgc_v[own, :], stacked, preferred_element_type=f32)
            q = q + ratio * moved_v[own, :]
            r = r_v[own, :]
            d = r + ratio * along_v[own, :]
            s_v[pair, :, inside] = (r - step * q).T
            x_v[pair, :, inside] = (done_v[own, :] + step * d).T
        copies.out(s_v.at[pair], out_residual.at[pair])
        copies.out(x_v.at[pair], out_done.at[pair])
    copies.close()


def shape(*dims, kind=f32):
    return jax.ShapeDtypeStruct(dims, kind)


WORK = [
    pltpu.SMEM((NB,), jnp.int32),
    pltpu.VMEM((NS, NS), bf16),
    pltpu.VMEM((2 * ROWS16, NS), bf16),
    pltpu.VMEM((NS, 2 * K), bf16),
    pltpu.VMEM((CHIPS, SLOTS * SLOT, K), f32),
    pltpu.VMEM((NS, K), f32),
    pltpu.VMEM((NS, 2 * K), bf16),
    pltpu.VMEM((NS, K), f32),
    pltpu.VMEM((2 * M, K), f32),
    pltpu.VMEM((256, K), f32),
    pltpu.VMEM((PAY, K), f32),
    pltpu.SemaphoreType.DMA((64,)),
    pltpu.SemaphoreType.DMA((NS // TALL,)),
]
MORE = [pltpu.VMEM((4, M, K), f32), pltpu.VMEM((NS, K), f32)] + [pltpu.VMEM((2 * M, K), f32)] * 3 + [pltpu.VMEM((SLOT, K), f32)] * 2
LAST = (
    [pltpu.VMEM((256, K), f32), pltpu.VMEM((2 * M, 2 * K), bf16), pltpu.VMEM((CHIPS, SLOTS * SLOT, K), f32)]
    + [pltpu.VMEM((SLOT, K), f32)]
    + [pltpu.VMEM((2 * M, K), f32)] * 5
    + [pltpu.VMEM((2, K, M), f32)] * 2
    + [pltpu.SemaphoreType.DMA((32,))]
)
FACES = [shape(M, K)] * 4


def call(kernel, specs, outs, scratch, flops, place, limit=LIMIT):
    return pl.pallas_call(
        kernel,
        in_specs=specs,
        out_specs=[place] * len(outs),
        out_shape=outs,
        scratch_shapes=scratch,
        compiler_params=limit,
        cost_estimate=pl.CostEstimate(flops=flops, bytes_accessed=1 << 20, transcendentals=0),
    )


def coarse_phase(pay, parts, core, *beside):
    own = lax.all_to_all(pay, "row", 0, 0, tiled=True)
    own, *beside = lax.optimization_barrier((own, *beside))
    other = swapped(own, lambda c: c ^ 1)
    (terms,) = call(
        coarse_kernel,
        [SM, HB, VM, VM],
        [shape(CHIPS, SLOTS * SLOT, K)],
        [
            pltpu.VMEM((2, CHIPS * SLOTS * SLOT, 2 * K), bf16),
            pltpu.VMEM((2 * K, K), f32),
            pltpu.VMEM((CHIPS, SLOTS * SLOT, K), f32),
            pltpu.SemaphoreType.DMA((8,)),
        ],
        10**8,
        HB,
        SMALL,
    )(core, parts, own, other)
    groups = [[2 * chip + which for chip in range(CHIPS)] for which in range(2)]
    return lax.all_to_all(terms, "col", 0, 0, axis_index_groups=groups, tiled=True), *beside


def per_device(schur_blocks, rigid_modes, floating, block_order, coarse_inverse, right_side):
    order = block_order[0, 0]
    row, col = lax.axis_index("row"), lax.axis_index("col")
    core = (col % 2).astype(jnp.int32).reshape(1)
    masks = jnp.stack([row > 0, row < ROWS - 1, col > 0, col < COLS - 1]).astype(f32)
    side = right_side[0, 0]

    from_n = cyclic(side[0], "row", 1)
    from_w = cyclic(side[1], "col", 1)
    modes = (rigid_modes[0, 0] * floating[0, 0].astype(f32)).reshape(MODES, NB, BLK)
    modes = jnp.pad(jnp.transpose(modes, (1, 0, 2)), ((0, 0), (0, SLOT - MODES), (0, 0)))
    local, pay = call(
        start_kernel,
        [SM] + [HB] * 4,
        [shape(NS, K), shape(ROWS, PAY, K)],
        [
            pltpu.VMEM((NB, SLOT, BLK), f32),
            pltpu.VMEM((2, K, M), f32),
            pltpu.VMEM((2, K, M), f32),
            pltpu.VMEM((NS, K), f32),
            pltpu.VMEM((16, NS), f32),
            pltpu.VMEM((NS, 2 * K), bf16),
            pltpu.VMEM((PAY, K), f32),
            pltpu.SemaphoreType.DMA((16,)),
        ],
        10**8,
        HB,
    )(masks, modes, side, from_n, from_w)

    mine = jnp.transpose(coarse_inverse[:, 0, :, :, :, 0], (1, 0, 3, 2))
    mine = jnp.pad(mine, ((0, 0), (0, SLOT - MODES), (0, 0), (0, SLOT - MODES))).reshape(COLS, SLOT, SLOT * ROWS)
    mine = jnp.concatenate([mine, mine], axis=2)
    down = cyclic(jnp.concatenate([mine, modes[4:8]], axis=0), "row", 1)
    up = cyclic(jnp.concatenate([mine, modes[0:4]], axis=0), "row", -1)
    down, up, pay = lax.optimization_barrier((down, up, pay))
    lines = jnp.concatenate([mine, down[:COLS], up[:COLS]], axis=0)
    right = cyclic(jnp.concatenate([lines, modes[12:16]], axis=0), "col", 1)
    left = cyclic(jnp.concatenate([lines, modes[8:12]], axis=0), "col", -1)
    far = swapped(jnp.where(core[0] == 0, right[: 3 * COLS], left[: 3 * COLS]), lambda c: c ^ 1)
    (parts,) = call(
        table_kernel,
        [SM] + [HB] * 6,
        [shape(2, CHIPS * SLOTS * SLOT, 2 * K, kind=bf16)],
        [pltpu.VMEM((tiles, SLOT, BLK), f32) for tiles in (COLS, COLS + 4, COLS + 4, 3 * COLS + 4, 3 * COLS + 4, 3 * COLS)]
        + [
            pltpu.VMEM((CHIPS * SLOTS * SLOT, 2 * K), f32),
            pltpu.VMEM((2, CHIPS * SLOTS * SLOT, 2 * K), bf16),
            pltpu.SemaphoreType.DMA((16,)),
        ],
        10**7,
        HB,
    )(core, mine, down, up, right, left, far)
    bgt, bgc = call(
        modes_kernel,
        [SM] * 2 + [HB] * 5,
        [shape(2 * ROWS16, NS, kind=bf16), shape(NS, 2 * K, kind=bf16)],
        [pltpu.VMEM((tiles, SLOT, BLK), f32) for tiles in (NB, 4, 4, 4, 4)]
        + [
            pltpu.VMEM((ROWS16, NS), f32),
            pltpu.VMEM((256, NS), f32),
            pltpu.VMEM((2 * ROWS16, NS), bf16),
            pltpu.VMEM((NS, 2 * K), bf16),
            pltpu.SemaphoreType.DMA((16,)),
        ],
        10**8,
        HB,
    )(order, masks, modes, down, up, right, left)
    (came,) = coarse_phase(pay, parts, core)

    matrix = schur_blocks[0, 0]
    residual, *faces, pay = call(
        begin_kernel,
        [SM] + [HB] * 5,
        [shape(NS, K)] + FACES + [shape(ROWS, PAY, K)],
        WORK,
        2 * 10**9,
        HB,
    )(order, matrix, bgt, bgc, came, local)

    state = ()
    for iteration in range(ITERS):
        which = (1, 3) if iteration + 1 == ITERS else (0, 1, 2, 3)
        moves = (("row", 1), ("row", -1), ("col", 1), ("col", -1))
        near = [cyclic(faces[face ^ 1], *moves[face]) for face in which]
        mine = [faces[face] for face in which]
        (local,) = call(
            functools.partial(image_kernel, which),
            [SM] + [HB] * (2 * len(which)),
            [shape(len(which), M, K)],
            [pltpu.VMEM((len(which), M, K), f32)] * 2 + [pltpu.SemaphoreType.DMA((16,))],
            COST,
            HB,
        )(masks, *mine, *near)
        came, local = coarse_phase(pay, parts, core, local)
        if iteration + 1 == ITERS:
            break
        first = iteration == 0
        given = (order, matrix, bgt, bgc, came, residual, local, *state)
        residual, along, moved, image, done, past, *faces, pay = call(
            functools.partial(step_kernel, first),
            [SM] + [HB] * (len(given) - 1),
            [shape(NS, K), shape(2 * M, K), shape(NS, K), shape(2 * M, K), shape(2 * M, K), shape(SLOT, K)]
            + FACES
            + [shape(ROWS, PAY, K)],
            WORK + MORE,
            2 * 10**9,
            HB,
        )(*given)
        state = (past, along, moved, image, done)

    past, along, moved, image, done = state
    done, residual = call(
        end_kernel,
        [HB] * 8,
        [shape(2, K, M)] * 2,
        LAST,
        10**8,
        HB,
    )(bgc, came, residual, local, past, along, moved, done)
    return (done[None, None], residual[None, None])


def solution(mesh):
    placed = (
        P("row", "col", None, None),
        P("row", "col", None, None),
        P("row", "col"),
        P("row", "col", None),
        P(None, "row", None, None, None, "col"),
        P("row", "col", None, None, None),
    )
    return jax.shard_map(
        per_device,
        mesh=mesh,
        in_specs=placed,
        out_specs=(P("row", "col", None, None, None), P("row", "col", None, None, None)),
        check_vma=False,
    )
```

```python
import functools

import jax
import jax.numpy as jnp
from jax import lax
from jax.experimental import pallas as pl
from jax.experimental.pallas import tpu as pltpu
from jax.sharding import PartitionSpec as P

M = 512
NS = 2048
BLK = 128
NB = 16
K = 128
ROWS = 8
COLS = 32
MODES = 6
ITERS = 3
SLOT = 8
SLOTS = 5
PAY = 40
ROWS16 = 48
TERMS = ((0, 0), (0, 1), (1, 0), (1, 1), (0, 2), (2, 0))
TALL = 1024
CHIPS = 16
HALF = COLS // 2
COST = 2 * 10**10

f32 = jnp.float32
bf16 = jnp.bfloat16
VM = pl.BlockSpec(memory_space=pltpu.VMEM)
SM = pl.BlockSpec(memory_space=pltpu.SMEM)
HB = pl.BlockSpec(memory_space=pltpu.HBM)
LIMIT = pltpu.CompilerParams(vmem_limit_bytes=56 * 1024 * 1024)
SMALL = pltpu.CompilerParams(vmem_limit_bytes=8 * 1024 * 1024)


def cyclic(value, axis, steps):
    count = lax.axis_size(axis)
    return lax.ppermute(value, axis, [(s, (s + steps) % count) for s in range(count)])


def shifted(value, axis, steps):
    count = lax.axis_size(axis)
    initial, last = (max(0, -steps), min(count, count - steps))
    return lax.ppermute(value, axis, [(s, s + steps) for s in range(initial, last)])


def swapped(value, partner):
    return lax.ppermute(value, "col", [(s, partner(s)) for s in range(COLS)])


def parts_of(value, count):
    pieces = []
    for _ in range(count):
        piece = value.astype(bf16)
        pieces.append(piece)
        value = value - piece.astype(f32)
    return pieces


class Copies:
    def __init__(self, sems):
        self.sems, self.used, self.open = sems, 0, []

    def start(self, source, target):
        copy = pltpu.make_async_copy(source, target, self.sems.at[self.used])
        copy.start()
        self.used += 1
        return copy

    def out(self, source, target):
        self.open.append(self.start(source, target))

    def close(self):
        for copy in self.open:
            copy.wait()


def wait(copies):
    for copy in copies:
        copy.wait()


def own_modes(full, own, masks):
    for block in range(NB):
        face = block // (M // BLK)
        value = own[block] * masks[face] if face % 2 == 0 else own[block]
        full[0:SLOT, BLK * block : BLK * (block + 1)] = value


def start_kernel(
    masks, own, near_s, near_e, side, turned, pay,
    own_v, near_v, side_v, turned_v, full, halves, pay_v, sems,
):
    copies = Copies(sems)
    ready = [copies.start(own, own_v), copies.start(near_s, near_v.at[0]), copies.start(near_e, near_v.at[1])]
    faces = [copies.start(side.at[index], side_v.at[index]) for index in range(2)]
    full[...] = jnp.zeros_like(full)
    for index in range(2):
        wait(faces[index : index + 1])
        for block in range(M // BLK):
            rows = slice(M * index + BLK * block, M * index + BLK * (block + 1))
            value = side_v[index, :, BLK * block : BLK * (block + 1)].T
            turned_v[index, BLK * block : BLK * (block + 1), :] = value
            high, low = parts_of(value, 2)
            halves[rows, :K] = high
            halves[rows, K:] = low
        copies.out(turned_v.at[index], turned.at[index])
    wait(ready)
    for index in range(2):
        rows = slice(SLOT * 2 * (index + 1), SLOT * (2 * index + 3))
        for block in range(M // BLK):
            lanes = slice(M * index + BLK * block, M * index + BLK * (block + 1))
            full[0:SLOT, lanes] = own_v[M // BLK * (2 * index + 1) + block]
            full[rows, lanes] = near_v[index, block] * -masks[2 * index + 1]
    pieces = jnp.concatenate(parts_of(full[...], 2), axis=0)
    d = jnp.dot(pieces, halves[...], preferred_element_type=f32)
    pay_v[...] = (d[:ROWS16, :K] + d[:ROWS16, K:] + d[ROWS16:, :K] + d[ROWS16:, K:])[0:PAY]
    for index in range(ROWS):
        copies.out(pay_v, pay.at[index])
    copies.close()


def modes_kernel(
    order, masks, own, down, up, right, left, from_n, from_w, bgt, bgc, other,
    own_v, down_v, up_v, right_v, left_v, full, turned, bgt_v, bgc_v, near_v, other_v, sems,
):
    copies = Copies(sems)
    ready = [copies.start(own, own_v)]
    for source, target in ((up, up_v), (left, left_v)):
        ready.append(copies.start(source, target))
    ready.append(copies.start(down.at[pl.ds(HALF, 4)], down_v))
    ready.append(copies.start(right.at[pl.ds(3 * HALF, 4)], right_v))
    sides = [copies.start(from_n, near_v.at[0]), copies.start(from_w, near_v.at[1])]
    full[...] = jnp.zeros_like(full)
    wait(ready)
    own_modes(full, own_v, masks)
    for slot, near in enumerate((down_v, up_v, right_v, left_v)):
        rows = slice(SLOT * (slot + 1), SLOT * (slot + 2))
        for block in range(M // BLK):
            lanes = slice(M * slot + BLK * block, M * slot + BLK * (block + 1))
            full[rows, lanes] = near[block] * -masks[slot]
    pieces = parts_of(full[...], 3)
    for index, (which, _) in enumerate(TERMS):
        turned[40 * index : 40 * (index + 1), :] = pieces[which][0:40].astype(f32)
    turned[240:256, :] = jnp.zeros((16, NS), f32)
    for block in range(NB):
        for half in range(2):
            piece = turned[BLK * half : BLK * (half + 1), BLK * block : BLK * (block + 1)].T
            bgc_v[BLK * block : BLK * (block + 1), BLK * half : BLK * (half + 1)] = piece.astype(bf16)
    copies.out(bgc_v, bgc)
    for block in range(NB):
        at = pl.multiple_of(order[block] * BLK, BLK)
        for index, piece in enumerate(parts_of(full[:, pl.ds(at, BLK)], 2)):
            bgt_v[ROWS16 * index : ROWS16 * (index + 1), BLK * block : BLK * (block + 1)] = piece
    copies.out(bgt_v, bgt)
    for index in range(2):
        wait(sides[index : index + 1])
        for block in range(M // BLK):
            inside = slice(BLK * block, BLK * (block + 1))
            other_v[index, inside, :] = near_v[index, :, inside].T * -masks[2 * index]
        copies.out(other_v.at[index], other.at[index])
    copies.close()


def table_kernel(
    core, mine, down, up, right, left, far, parts,
    mine_v, down_v, up_v, right_v, left_v, far_v, table, parts_v, sems,
):
    copies = Copies(sems)
    pairs = ((mine, mine_v), (down, down_v), (up, up_v), (right, right_v), (left, left_v), (far, far_v))
    wait([copies.start(source, target) for source, target in pairs])
    first = core[0] == 0
    half = lax.broadcasted_iota(jnp.int32, (SLOT, BLK), 1) < SLOT * ROWS

    @pl.loop(0, CHIPS)
    def _(target):
        at = 2 * target + core[0]
        picks = ((0, at), (1, at), (2, at), (0, jnp.maximum(at - 1, 0)), (0, jnp.minimum(at + 1, COLS - 1)))
        for slot, (line, column) in enumerate(picks):
            two = lax.div(column, 2)
            w, e, f = (ref[HALF * line + two] for ref in (right_v, left_v, far_v))
            m = (mine_v[two], down_v[two], up_v[two])[line]
            on_left = (core[0] == 0) == (slot < 3)
            pairs = ((jnp.where(first, w, f), jnp.where(first, m, w)), (jnp.where(first, e, m), jnp.where(first, f, e)))
            turned = [
                jnp.where(
                    half,
                    jnp.where(on_left, a, pltpu.roll(a, SLOT * ROWS, 1)),
                    jnp.where(on_left, pltpu.roll(b, SLOT * ROWS, 1), b),
                )
                for a, b in pairs
            ]
            rows = pl.ds(pl.multiple_of((target * SLOTS + slot) * SLOT, SLOT), SLOT)
            table[rows, :K] = turned[0]
            table[rows, K:] = turned[1]

    for index, piece in enumerate(parts_of(table[...], 2)):
        parts_v[index] = piece
        copies.out(parts_v.at[index], parts.at[index])
    copies.close()


def coarse_kernel(core, parts, own_v, other_v, out, parts_v, entries, out_v, sems):
    copies = Copies(sems)
    table = [copies.start(parts.at[index], parts_v.at[index]) for index in range(2)]
    first = core[0] == 0

    def tile(which, line, slot):
        here = slice(SLOT * slot, SLOT * (slot + 1))
        a, b = own_v[line, here, :], other_v[line, here, :]
        return jnp.where(first, a, b) if which == 0 else jnp.where(first, b, a)

    total = jnp.zeros((2 * SLOT, K), f32)
    for line in range(ROWS):
        for which in range(2):
            value = tile(which, line, 0)
            if line > 0:
                value = value + tile(which, line - 1, 2)
            if line < ROWS - 1:
                value = value + tile(which, line + 1, 1)
            value = value + tile(1 - which, line, 3 + which)
            at = SLOT * (ROWS * (which + 1) + line)
            entries[at : at + SLOT, :] = value
        entries[SLOT * line : SLOT * (line + 1), :] = tile(0, line, 3)
        at = SLOT * (ROWS * 3 + line)
        entries[at : at + SLOT, :] = tile(1, line, 4)
        total = total + own_v[line, : 2 * SLOT, :] + other_v[line, : 2 * SLOT, :]
    both = jnp.concatenate(parts_of(entries[...], 2), axis=1)
    wait(table)
    d = jnp.dot(parts_v[0], both, preferred_element_type=f32)
    e = jnp.dot(parts_v[1], both, preferred_element_type=f32)
    value = e[:, K:] + e[:, :K] + d[:, K:] + d[:, :K]
    for target in range(CHIPS):
        out_v[target] = value[SLOTS * SLOT * target : SLOTS * SLOT * (target + 1)]
        out_v[target, 6:8, :] = total[6:8]
        out_v[target, 14:15, :] = total[14:15]
    copies.out(out_v, out)
    copies.close()


def take_values(came, stack):
    value = came[0]
    for index in range(1, CHIPS):
        value = value + came[index]
    spare = lax.broadcasted_iota(jnp.int32, (SLOT * SLOTS, K), 0) % SLOT >= MODES
    pieces = parts_of(jnp.where(spare, 0.0, value), 3)
    for index, (_, right) in enumerate(TERMS):
        stack[40 * index : 40 * (index + 1), :] = pieces[right].astype(f32)
    stack[240:256, :] = jnp.zeros((16, K), f32)
    return stack[...].astype(bf16), (value[6:7], value[7:8], value[14:15])


def folded(value):
    return jnp.sum(value.reshape(-1, SLOT, K), axis=0)


def schur_product(order, copies, matrix, turn, bgt, residual, halves, product):
    wait(turn)

    def tall(step, carry):
        value, energy = carry
        matrix.wait(step)
        rows = matrix.held[pl.ds(pl.multiple_of(step * TALL, TALL), TALL), :]
        both = jnp.dot(rows, halves[...], preferred_element_type=f32)
        both = both[:, :K] + both[:, K:]
        d = jnp.dot(
            bgt[:, pl.ds(pl.multiple_of(step * TALL, TALL), TALL)],
            jnp.concatenate(parts_of(both, 2), axis=1),
            preferred_element_type=f32,
        )
        value = value + d[:ROWS16, :K] + d[:ROWS16, K:] + d[ROWS16:, :K] + d[ROWS16:, K:]
        for piece in range(TALL // BLK):
            at = pl.multiple_of(order[step * (TALL // BLK) + piece] * BLK, BLK)
            y = both[BLK * piece : BLK * (piece + 1)]
            product[pl.ds(at, BLK), :] = y
            energy = energy + folded(residual[pl.ds(at, BLK), :] * y)
        return value, energy

    return lax.fori_loop(0, NS // TALL, tall, (jnp.zeros((ROWS16, K), f32), jnp.zeros((SLOT, K), f32)))


class Matrix:
    def __init__(self, source, held, sems):
        self.source, self.held, self.sems = source, held, sems

    def copy(self, step):
        rows = pl.ds(TALL * step if isinstance(step, int) else pl.multiple_of(step * TALL, TALL), TALL)
        return pltpu.make_async_copy(self.source.at[rows], self.held.at[rows], self.sems.at[step])

    def start(self, step):
        self.copy(step).start()

    def wait(self, step):
        self.copy(step).wait()


def put_halves(value, halves, at):
    high, low = parts_of(value, 2)
    halves[pl.ds(pl.multiple_of(at * BLK, BLK), BLK), :K] = high
    halves[pl.ds(pl.multiple_of(at * BLK, BLK), BLK), K:] = low


def invert(order, inverse):
    for block in range(NB):
        inverse[order[block]] = block


def close_product(value, norm, energy, cross, product, pay, faces, copies, pay_held):
    for face in range(4):
        copies.out(product.at[pl.ds(M * face, M)], faces[face])
    pay_held[...] = value[0:PAY]
    pay_held[6:7, :] = jnp.sum(norm, axis=0, keepdims=True)
    pay_held[7:8, :] = jnp.sum(energy, axis=0, keepdims=True)
    pay_held[14:15, :] = jnp.sum(cross, axis=0, keepdims=True)
    for index in range(ROWS):
        copies.out(pay_held, pay.at[index])
    copies.close()


def begin_kernel(
    order, matrix, bgt, bgc, came_v, own, other, residual, yn, ys, yw, ye, pay,
    inverse, held, bgt_v, bgc_v, _, r_v, halves, product, spread, stack, pay_v, sems, tall_sems,
):
    copies, matrix = Copies(sems), Matrix(matrix, held, tall_sems)
    head = [copies.start(bgc, bgc_v)]
    body = [copies.start((other, own)[face % 2].at[face // 2], r_v.at[pl.ds(M * face, M)]) for face in range(4)]
    matrix.start(0)
    turn = [copies.start(bgt, bgt_v)]
    invert(order, inverse)
    wait(head)
    matrix.start(1)
    stacked, _ = take_values(came_v, stack)
    norm = jnp.zeros((SLOT, K), f32)
    for face in range(4):
        inner = slice(M * face, M * (face + 1))
        spread[0:M, :] = jnp.dot(bgc_v[inner, :], stacked, preferred_element_type=f32)
        wait(body[face : face + 1])

        def block(index, norm, face=face):
            rows = pl.ds(pl.multiple_of(M * face + BLK * index, BLK), BLK)
            r = r_v[rows, :] - spread[pl.ds(pl.multiple_of(BLK * index, BLK), BLK), :]
            r_v[rows, :] = r
            put_halves(r, halves, inverse[M // BLK * face + index])
            return norm + folded(r * r) if face % 2 else norm

        norm = lax.fori_loop(0, M // BLK, block, norm)
        copies.out(r_v.at[inner], residual.at[inner])
    value, energy = schur_product(order, copies, matrix, turn, bgt_v, r_v, halves, product)
    close_product(value, norm, energy, jnp.zeros_like(norm), product, pay, (yn, ys, yw, ye), copies, pay_v)


def image_kernel(which, *refs):
    masks, refs = refs[0], refs[1:]
    count = len(which)
    faces, near, image, (y_v, near_v, sems) = refs[:count], refs[count : 2 * count], refs[2 * count], refs[2 * count + 1 :]
    copies = Copies(sems)
    ready = []
    for index in range(count):
        ready.append([copies.start(faces[index], y_v.at[index]), copies.start(near[index], near_v.at[index])])
    for index, face in enumerate(which):
        wait(ready[index])
        if face % 2:
            y_v[index] = y_v[index] - masks[face] * near_v[index]
        else:
            y_v[index] = masks[face] * (y_v[index] - near_v[index])
        copies.out(y_v.at[index], image.at[index])
    copies.close()


def scalars(first, sums, past):
    norm, energy, cross = sums
    if first:
        return norm, energy, None, norm / energy
    ratio = norm / past[0:1, :]
    curvature = energy + 2.0 * ratio * cross + ratio * ratio * past[1:2, :]
    return norm, curvature, ratio, norm / curvature


def step_kernel(first, *refs):
    order, matrix, bgt, bgc, came, residual, local = refs[:7]
    refs = refs[7:]
    if not first:
        past, moved, image = refs[:3]
        refs = refs[3:]
    new_residual, new_moved, new_past = refs[:3]
    new_faces, pay, refs = refs[3:7], refs[7], refs[8:]
    (inverse, held, bgt_v, bgc_v, came_v, r_v, halves, product, spread, stack, pay_v, sems, tall_sems,
     local_v, moved_v, image_v, past_v, new_past_v) = refs

    copies, matrix = Copies(sems), Matrix(matrix, held, tall_sems)
    head = [copies.start(came, came_v)]
    if not first:
        head.append(copies.start(past, past_v))
    head.append(copies.start(bgc, bgc_v))

    def fetch(pair):
        wide = pl.ds(2 * M * pair, 2 * M)
        part = [copies.start(residual.at[wide], r_v.at[wide])]
        part.append(copies.start(local.at[pl.ds(2 * pair, 2)], local_v.at[pl.ds(2 * pair, 2)]))
        if not first:
            part.append(copies.start(moved.at[wide], moved_v.at[wide]))
            part.append(copies.start(image.at[2 * pair + 1], image_v.at[pl.ds(M * pair, M)]))
        return part

    body = [fetch(0)]
    matrix.start(0)
    invert(order, inverse)

    wait(head)
    stacked, sums = take_values(came_v, stack)
    norm, curvature, ratio, step = scalars(first, sums, past_v)
    new_past_v[...] = jnp.zeros_like(new_past_v)
    new_past_v[0:1, :] = norm
    new_past_v[1:2, :] = curvature
    if first:
        new_past_v[2:3, :] = step
    else:
        new_past_v[2:3, :] = past_v[2:3, :] + step * ratio
        new_past_v[3:4, :] = step
        new_past_v[4:5, :] = ratio
    copies.out(new_past_v, new_past)
    carry = (jnp.zeros((SLOT, K), f32), jnp.zeros((SLOT, K), f32))
    for pair in range(2):
        wide = pl.ds(2 * M * pair, 2 * M)
        spread[...] = jnp.dot(bgc_v[2 * M * pair : 2 * M * (pair + 1), :], stacked, preferred_element_type=f32)
        wait(body[pair])
        if pair == 0:
            body.append(fetch(1))
            turn = [copies.start(bgt, bgt_v)]

        def block(index, carry, pair=pair):
            norm, cross = carry
            for kind in range(2):
                face = 2 * pair + kind
                rows = pl.ds(pl.multiple_of(M * face + BLK * index, BLK), BLK)
                q = local_v[face, pl.ds(pl.multiple_of(BLK * index, BLK), BLK), :]
                f = q
                if kind and not first:
                    f = q + ratio * image_v[pl.ds(pl.multiple_of(M * pair + BLK * index, BLK), BLK), :]
                q = q - spread[pl.ds(pl.multiple_of(M * kind + BLK * index, BLK), BLK), :]
                if not first:
                    q = q + ratio * moved_v[rows, :]
                moved_v[rows, :] = q
                r = r_v[rows, :] - step * q
                r_v[rows, :] = r
                put_halves(r, halves, inverse[M // BLK * face + index])
                if kind:
                    norm = norm + folded(r * r)
                    cross = cross + folded(r * f)
            return norm, cross

        carry = lax.fori_loop(0, M // BLK, block, carry)
        if pair == 0:
            matrix.start(1)
        for source, target in ((r_v, new_residual), (moved_v, new_moved)):
            copies.out(source.at[wide], target.at[wide])
    value, energy = schur_product(order, copies, matrix, turn, bgt_v, r_v, halves, product)
    close_product(value, carry[0], energy, carry[1], product, pay, new_faces, copies, pay_v)


def end_kernel(
    bgc, came, residual, first, second, local, past, moved, out_done, out_residual,
    stack, bgc_v, came_v, past_v, r_v, first_v, second_v, local_v, moved_v, x_v, s_v, sems,
):
    copies = Copies(sems)
    head = [copies.start(came, came_v), copies.start(past, past_v)]
    body = []
    for pair in range(2):
        rows, own = pl.ds(M * (2 * pair + 1), M), pl.ds(M * pair, M)
        part = [copies.start(bgc.at[rows], bgc_v.at[own]), copies.start(local.at[pair], local_v.at[own])]
        for source, target in ((residual, r_v), (moved, moved_v), (first, first_v), (second, second_v)):
            part.append(copies.start(source.at[rows], target.at[own]))
        body.append(part)
    wait(head)
    stacked, sums = take_values(came_v, stack)
    _, _, ratio, step = scalars(False, sums, past_v)
    along = step * ratio
    of_second = past_v[3:4, :] + along
    of_first = past_v[2:3, :] + along * past_v[4:5, :]
    for pair in range(2):
        wait(body[pair])
        for block in range(M // BLK):
            inside = slice(BLK * block, BLK * (block + 1))
            own = slice(M * pair + BLK * block, M * pair + BLK * (block + 1))
            q = local_v[own, :] - jnp.dot(bgc_v[own, :], stacked, preferred_element_type=f32)
            q = q + ratio * moved_v[own, :]
            r = r_v[own, :]
            s_v[pair, :, inside] = (r - step * q).T
            x_v[pair, :, inside] = (of_first * first_v[own, :] + of_second * second_v[own, :] + step * r).T
        copies.out(s_v.at[pair], out_residual.at[pair])
        copies.out(x_v.at[pair], out_done.at[pair])
    copies.close()


def shape(*dims, kind=f32):
    return jax.ShapeDtypeStruct(dims, kind)


WORK = [
    pltpu.SMEM((NB,), jnp.int32),
    pltpu.VMEM((NS, NS), bf16),
    pltpu.VMEM((2 * ROWS16, NS), bf16),
    pltpu.VMEM((NS, 2 * K), bf16),
    pltpu.VMEM((CHIPS, SLOTS * SLOT, K), f32),
    pltpu.VMEM((NS, K), f32),
    pltpu.VMEM((NS, 2 * K), bf16),
    pltpu.VMEM((NS, K), f32),
    pltpu.VMEM((2 * M, K), f32),
    pltpu.VMEM((256, K), f32),
    pltpu.VMEM((PAY, K), f32),
    pltpu.SemaphoreType.DMA((64,)),
    pltpu.SemaphoreType.DMA((NS // TALL,)),
]
MORE = [pltpu.VMEM((4, M, K), f32), pltpu.VMEM((NS, K), f32), pltpu.VMEM((2 * M, K), f32)]
MORE += [pltpu.VMEM((SLOT, K), f32)] * 2
LAST = (
    [pltpu.VMEM((256, K), f32), pltpu.VMEM((2 * M, 2 * K), bf16), pltpu.VMEM((CHIPS, SLOTS * SLOT, K), f32)]
    + [pltpu.VMEM((SLOT, K), f32)]
    + [pltpu.VMEM((2 * M, K), f32)] * 5
    + [pltpu.VMEM((2, K, M), f32)] * 2
    + [pltpu.SemaphoreType.DMA((32,))]
)
FACES = [shape(M, K)] * 4


def call(kernel, specs, outs, scratch, flops, place, limit=LIMIT):
    return pl.pallas_call(
        kernel,
        in_specs=specs,
        out_specs=[place] * len(outs),
        out_shape=outs,
        scratch_shapes=scratch,
        compiler_params=limit,
        cost_estimate=pl.CostEstimate(flops=flops, bytes_accessed=1 << 20, transcendentals=0),
    )


def coarse_phase(pay, parts, core, *beside):
    own = lax.all_to_all(pay, "row", 0, 0, tiled=True)
    own, parts, *beside = lax.optimization_barrier((own, parts, *beside))
    other = swapped(own, lambda c: c ^ 1)
    (terms,) = call(
        coarse_kernel,
        [SM, HB, VM, VM],
        [shape(CHIPS, SLOTS * SLOT, K)],
        [
            pltpu.VMEM((2, CHIPS * SLOTS * SLOT, 2 * K), bf16),
            pltpu.VMEM((2 * K, K), f32),
            pltpu.VMEM((CHIPS, SLOTS * SLOT, K), f32),
            pltpu.SemaphoreType.DMA((8,)),
        ],
        10**8,
        HB,
        SMALL,
    )(core, parts, own, other)
    groups = [[2 * chip + which for chip in range(CHIPS)] for which in range(2)]
    return lax.all_to_all(terms, "col", 0, 0, axis_index_groups=groups, tiled=True), *beside


def per_device(schur_blocks, rigid_modes, floating, block_order, coarse_inverse, right_side):
    order = block_order[0, 0]
    row, col = lax.axis_index("row"), lax.axis_index("col")
    core = (col % 2).astype(jnp.int32).reshape(1)
    masks = jnp.stack([row > 0, row < ROWS - 1, col > 0, col < COLS - 1]).astype(f32)
    side = right_side[0, 0]

    modes = (rigid_modes[0, 0] * floating[0, 0].astype(f32)).reshape(MODES, NB, BLK)
    modes = jnp.pad(jnp.transpose(modes, (1, 0, 2)), ((0, 0), (0, SLOT - MODES), (0, 0)))
    near_s = cyclic(modes[0:4], "row", -1)
    near_e = cyclic(modes[8:12], "col", -1)
    own, pay = call(
        start_kernel,
        [SM] + [HB] * 4,
        [shape(2, M, K), shape(ROWS, PAY, K)],
        [
            pltpu.VMEM((NB, SLOT, BLK), f32),
            pltpu.VMEM((2, 4, SLOT, BLK), f32),
            pltpu.VMEM((2, K, M), f32),
            pltpu.VMEM((2, M, K), f32),
            pltpu.VMEM((ROWS16, 2 * M), f32),
            pltpu.VMEM((2 * M, 2 * K), bf16),
            pltpu.VMEM((PAY, K), f32),
            pltpu.SemaphoreType.DMA((16,)),
        ],
        10**8,
        HB,
    )(masks, modes, near_s, near_e, side)
    from_n = cyclic(side[0], "row", 1)
    from_w = cyclic(side[1], "col", 1)
    mine = jnp.transpose(coarse_inverse[:, 0, :, :, :, 0], (1, 0, 3, 2))
    mine = jnp.pad(mine, ((0, 0), (0, SLOT - MODES), (0, 0), (0, SLOT - MODES))).reshape(HALF, 2, SLOT, SLOT * ROWS)
    mine = jnp.concatenate([mine[:, 0], mine[:, 1]], axis=2)
    down = cyclic(jnp.concatenate([mine, modes[4:8]], axis=0), "row", 1)
    up = cyclic(mine, "row", -1)
    down, up, pay = lax.optimization_barrier((down, up, pay))
    lines = jnp.concatenate([mine, down[:HALF], up], axis=0)
    right = cyclic(jnp.concatenate([lines, modes[12:16]], axis=0), "col", 1)
    left = cyclic(lines, "col", -1)
    right, left, from_n, from_w = lax.optimization_barrier((right, left, from_n, from_w))
    far = swapped(jnp.where(core[0] == 0, right[: 3 * HALF], left), lambda c: c ^ 1)
    (parts,) = call(
        table_kernel,
        [SM] + [HB] * 6,
        [shape(2, CHIPS * SLOTS * SLOT, 2 * K, kind=bf16)],
        [pltpu.VMEM((tiles, SLOT, BLK), f32) for tiles in (HALF, HALF + 4, HALF, 3 * HALF + 4, 3 * HALF, 3 * HALF)]
        + [
            pltpu.VMEM((CHIPS * SLOTS * SLOT, 2 * K), f32),
            pltpu.VMEM((2, CHIPS * SLOTS * SLOT, 2 * K), bf16),
            pltpu.SemaphoreType.DMA((16,)),
        ],
        10**6,
        HB,
    )(core, mine, down, up, right, left, far)
    bgt, bgc, other = call(
        modes_kernel,
        [SM] * 2 + [HB] * 7,
        [shape(2 * ROWS16, NS, kind=bf16), shape(NS, 2 * K, kind=bf16), shape(2, M, K)],
        [pltpu.VMEM((tiles, SLOT, BLK), f32) for tiles in (NB, 4, 4, 4, 4)]
        + [
            pltpu.VMEM((ROWS16, NS), f32),
            pltpu.VMEM((256, NS), f32),
            pltpu.VMEM((2 * ROWS16, NS), bf16),
            pltpu.VMEM((NS, 2 * K), bf16),
            pltpu.VMEM((2, K, M), f32),
            pltpu.VMEM((2, M, K), f32),
            pltpu.SemaphoreType.DMA((16,)),
        ],
        COST,
        HB,
    )(order, masks, modes, down, near_s, right, near_e, from_n, from_w)
    (came,) = coarse_phase(pay, parts, core)

    matrix = schur_blocks[0, 0]
    residual, *faces, pay = call(
        begin_kernel,
        [SM] + [HB] * 3 + [VM] + [HB] * 2,
        [shape(NS, K)] + FACES + [shape(ROWS, PAY, K)],
        WORK,
        2 * 10**9,
        HB,
    )(order, matrix, bgt, bgc, came, own, other)

    state, residuals = (), [residual]
    for iteration in range(ITERS):
        which = (1, 3) if iteration + 1 == ITERS else (0, 1, 2, 3)
        moves = (("row", 1), ("row", -1), ("col", 1), ("col", -1))
        near = [cyclic(faces[face ^ 1], *moves[face]) for face in which]
        mine = [faces[face] for face in which]
        (local,) = call(
            functools.partial(image_kernel, which),
            [SM] + [HB] * (2 * len(which)),
            [shape(len(which), M, K)],
            [pltpu.VMEM((len(which), M, K), f32)] * 2 + [pltpu.SemaphoreType.DMA((16,))],
            COST,
            HB,
        )(masks, *mine, *near)
        came, local = coarse_phase(pay, parts, core, local)
        if iteration + 1 == ITERS:
            break
        first = iteration == 0
        given = (order, matrix, bgt, bgc, came, residuals[-1], local, *state)
        residual, moved, past, *faces, pay = call(
            functools.partial(step_kernel, first),
            [SM] + [HB] * (len(given) - 1),
            [shape(NS, K), shape(NS, K), shape(SLOT, K)] + FACES + [shape(ROWS, PAY, K)],
            WORK + MORE,
            2 * 10**9,
            HB,
        )(*given)
        state = (past, moved, local)
        residuals.append(residual)

    done, residual = call(
        end_kernel,
        [HB] * 8,
        [shape(2, K, M)] * 2,
        LAST,
        10**8,
        HB,
    )(bgc, came, residuals[2], residuals[0], residuals[1], local, past, moved)
    return (done[None, None], residual[None, None])


def solution(mesh):
    placed = (
        P("row", "col", None, None),
        P("row", "col", None, None),
        P("row", "col"),
        P("row", "col", None),
        P(None, "row", None, None, None, "col"),
        P("row", "col", None, None, None),
    )
    return jax.shard_map(
        per_device,
        mesh=mesh,
        in_specs=placed,
        out_specs=(P("row", "col", None, None, None), P("row", "col", None, None, None)),
        check_vma=False,
    )
```

```python
import functools

import jax
import jax.numpy as jnp
from jax import lax
from jax.experimental import pallas as pl
from jax.experimental.pallas import tpu as pltpu
from jax.sharding import PartitionSpec as P

M = 512
NS = 2048
BLK = 128
NB = 16
K = 128
ROWS = 8
COLS = 32
MODES = 6
ITERS = 3
SLOT = 8
SLOTS = 5
PAY = 40
ROWS16 = 48
TERMS = ((0, 0), (0, 1), (1, 0))
TALL = 1024
PART = 512
CHIPS = 16
HALF = COLS // 2
COST = 2 * 10**10

f32 = jnp.float32
bf16 = jnp.bfloat16
VM = pl.BlockSpec(memory_space=pltpu.VMEM)
SM = pl.BlockSpec(memory_space=pltpu.SMEM)
HB = pl.BlockSpec(memory_space=pltpu.HBM)
LIMIT = pltpu.CompilerParams(vmem_limit_bytes=56 * 1024 * 1024)
SMALL = pltpu.CompilerParams(vmem_limit_bytes=8 * 1024 * 1024)


def cyclic(value, axis, steps):
    count = lax.axis_size(axis)
    return lax.ppermute(value, axis, [(s, (s + steps) % count) for s in range(count)])


def shifted(value, axis, steps):
    count = lax.axis_size(axis)
    initial, last = (max(0, -steps), min(count, count - steps))
    return lax.ppermute(value, axis, [(s, s + steps) for s in range(initial, last)])


def swapped(value, partner):
    return lax.ppermute(value, "col", [(s, partner(s)) for s in range(COLS)])


def parts_of(value, count):
    pieces = []
    for _ in range(count):
        piece = value.astype(bf16)
        pieces.append(piece)
        value = value - piece.astype(f32)
    return pieces


class Copies:
    def __init__(self, sems):
        self.sems, self.used, self.open = sems, 0, []

    def start(self, source, target):
        copy = pltpu.make_async_copy(source, target, self.sems.at[self.used])
        copy.start()
        self.used += 1
        return copy

    def out(self, source, target):
        self.open.append(self.start(source, target))

    def close(self):
        for copy in self.open:
            copy.wait()


def wait(copies):
    for copy in copies:
        copy.wait()


def own_modes(full, own, masks):
    for block in range(NB):
        face = block // (M // BLK)
        value = own[block] * masks[face] if face % 2 == 0 else own[block]
        full[0:SLOT, BLK * block : BLK * (block + 1)] = value


def start_kernel(
    masks, own, near_s, near_e, side, turned, pay,
    own_v, near_v, side_v, turned_v, full, halves, pay_v, sems,
):
    copies = Copies(sems)
    ready = [copies.start(own, own_v), copies.start(near_s, near_v.at[0]), copies.start(near_e, near_v.at[1])]
    faces = [copies.start(side.at[index], side_v.at[index]) for index in range(2)]
    full[...] = jnp.zeros_like(full)
    for index in range(2):
        wait(faces[index : index + 1])
        for block in range(M // BLK):
            rows = slice(M * index + BLK * block, M * index + BLK * (block + 1))
            value = side_v[index, :, BLK * block : BLK * (block + 1)].T
            turned_v[index, BLK * block : BLK * (block + 1), :] = value
            high, low = parts_of(value, 2)
            halves[rows, :K] = high
            halves[rows, K:] = low
        copies.out(turned_v.at[index], turned.at[index])
    wait(ready)
    for index in range(2):
        rows = slice(SLOT * 2 * (index + 1), SLOT * (2 * index + 3))
        for block in range(M // BLK):
            lanes = slice(M * index + BLK * block, M * index + BLK * (block + 1))
            full[0:SLOT, lanes] = own_v[M // BLK * (2 * index + 1) + block]
            full[rows, lanes] = near_v[index, block] * -masks[2 * index + 1]
    pieces = jnp.concatenate(parts_of(full[...], 2), axis=0)
    d = jnp.dot(pieces, halves[...], preferred_element_type=f32)
    pay_v[...] = (d[:ROWS16, :K] + d[:ROWS16, K:] + d[ROWS16:, :K] + d[ROWS16:, K:])[0:PAY]
    for index in range(ROWS):
        copies.out(pay_v, pay.at[index])
    copies.close()


def modes_kernel(
    order, masks, own, down, up, right, left, from_n, from_w, bgt, bgc, other,
    own_v, down_v, up_v, right_v, left_v, full, turned, bgt_v, bgc_v, near_v, other_v, sems,
):
    copies = Copies(sems)
    ready = [copies.start(own, own_v)]
    for source, target in ((up, up_v), (left, left_v)):
        ready.append(copies.start(source, target))
    ready.append(copies.start(down.at[pl.ds(HALF, 4)], down_v))
    ready.append(copies.start(right.at[pl.ds(3 * HALF, 4)], right_v))
    sides = [copies.start(from_n, near_v.at[0]), copies.start(from_w, near_v.at[1])]
    full[...] = jnp.zeros_like(full)
    wait(ready)
    own_modes(full, own_v, masks)
    for slot, near in enumerate((down_v, up_v, right_v, left_v)):
        rows = slice(SLOT * (slot + 1), SLOT * (slot + 2))
        for block in range(M // BLK):
            lanes = slice(M * slot + BLK * block, M * slot + BLK * (block + 1))
            full[rows, lanes] = near[block] * -masks[slot]
    pieces = parts_of(full[...], 2)
    for index, (which, _) in enumerate(TERMS):
        turned[40 * index : 40 * (index + 1), :] = pieces[which][0:40].astype(f32)
    turned[120:128, :] = jnp.zeros((8, NS), f32)
    for block in range(NB):
        piece = turned[:, BLK * block : BLK * (block + 1)].T
        bgc_v[BLK * block : BLK * (block + 1), :] = piece.astype(bf16)
    copies.out(bgc_v, bgc)
    for block in range(NB):
        at = pl.multiple_of(order[block] * BLK, BLK)
        for index, piece in enumerate(parts_of(full[:, pl.ds(at, BLK)], 2)):
            bgt_v[ROWS16 * index : ROWS16 * (index + 1), BLK * block : BLK * (block + 1)] = piece
    copies.out(bgt_v, bgt)
    for index in range(2):
        wait(sides[index : index + 1])
        for block in range(M // BLK):
            inside = slice(BLK * block, BLK * (block + 1))
            other_v[index, inside, :] = near_v[index, :, inside].T * -masks[2 * index]
        copies.out(other_v.at[index], other.at[index])
    copies.close()


def table_kernel(
    core, mine, down, up, right, left, far, parts,
    mine_v, down_v, up_v, right_v, left_v, far_v, table, parts_v, sems,
):
    copies = Copies(sems)
    pairs = ((mine, mine_v), (down, down_v), (up, up_v), (right, right_v), (left, left_v), (far, far_v))
    wait([copies.start(source, target) for source, target in pairs])
    first = core[0] == 0
    half = lax.broadcasted_iota(jnp.int32, (SLOT, BLK), 1) < SLOT * ROWS

    @pl.loop(0, CHIPS)
    def _(target):
        at = 2 * target + core[0]
        picks = ((0, at), (1, at), (2, at), (0, jnp.maximum(at - 1, 0)), (0, jnp.minimum(at + 1, COLS - 1)))
        for slot, (line, column) in enumerate(picks):
            two = lax.div(column, 2)
            w, e, f = (ref[HALF * line + two] for ref in (right_v, left_v, far_v))
            m = (mine_v[two], down_v[two], up_v[two])[line]
            on_left = (core[0] == 0) == (slot < 3)
            pairs = ((jnp.where(first, w, f), jnp.where(first, m, w)), (jnp.where(first, e, m), jnp.where(first, f, e)))
            turned = []
            for a, b in pairs:
                across = pltpu.roll(jnp.where(on_left, b, a), SLOT * ROWS, 1)
                turned.append(jnp.where(half, jnp.where(on_left, a, across), jnp.where(on_left, across, b)))
            rows = pl.ds(pl.multiple_of((target * SLOTS + slot) * SLOT, SLOT), SLOT)
            table[rows, :K] = turned[0]
            table[rows, K:] = turned[1]

    for index, piece in enumerate(parts_of(table[...], 2)):
        parts_v[index] = piece
        copies.out(parts_v.at[index], parts.at[index])
    copies.close()


def coarse_kernel(core, parts, own_v, other_v, out, parts_v, entries, out_v, sems):
    copies = Copies(sems)
    table = [copies.start(parts.at[index], parts_v.at[index]) for index in range(2)]
    first = core[0] == 0

    def tile(which, line, slot):
        here = slice(SLOT * slot, SLOT * (slot + 1))
        a, b = own_v[line, here, :], other_v[line, here, :]
        return jnp.where(first, a, b) if which == 0 else jnp.where(first, b, a)

    total = jnp.zeros((2 * SLOT, K), f32)
    for line in range(ROWS):
        for which in range(2):
            value = tile(which, line, 0)
            if line > 0:
                value = value + tile(which, line - 1, 2)
            if line < ROWS - 1:
                value = value + tile(which, line + 1, 1)
            value = value + tile(1 - which, line, 3 + which)
            at = SLOT * (ROWS * (which + 1) + line)
            entries[at : at + SLOT, :] = value
        entries[SLOT * line : SLOT * (line + 1), :] = tile(0, line, 3)
        at = SLOT * (ROWS * 3 + line)
        entries[at : at + SLOT, :] = tile(1, line, 4)
        total = total + own_v[line, : 2 * SLOT, :] + other_v[line, : 2 * SLOT, :]
    both = jnp.concatenate(parts_of(entries[...], 2), axis=1)
    wait(table)
    d = jnp.dot(parts_v[0], both, preferred_element_type=f32)
    e = jnp.dot(parts_v[1], both, preferred_element_type=f32)
    value = e[:, K:] + e[:, :K] + d[:, K:] + d[:, :K]
    for target in range(CHIPS):
        out_v[target] = value[SLOTS * SLOT * target : SLOTS * SLOT * (target + 1)]
        out_v[target, 6:8, :] = total[6:8]
        out_v[target, 14:15, :] = total[14:15]
    copies.out(out_v, out)
    copies.close()


def take_values(came, stack):
    value = came[0]
    for index in range(1, CHIPS):
        value = value + came[index]
    spare = lax.broadcasted_iota(jnp.int32, (SLOT * SLOTS, K), 0) % SLOT >= MODES
    pieces = parts_of(jnp.where(spare, 0.0, value), 2)
    for index, (_, right) in enumerate(TERMS):
        stack[40 * index : 40 * (index + 1), :] = pieces[right].astype(f32)
    stack[120:128, :] = jnp.zeros((8, K), f32)
    return stack[...].astype(bf16), (value[6:7], value[7:8], value[14:15])


def folded(value):
    return jnp.sum(value.reshape(-1, SLOT, K), axis=0)


def schur_product(order, copies, matrix, turn, bgt, residual, halves, product):
    wait(turn)

    def tall(step, carry):
        value, energy = carry
        matrix.wait(step)
        rows = matrix.held[pl.ds(pl.multiple_of(step * TALL, TALL), TALL), :]
        both = jnp.dot(rows, halves[...], preferred_element_type=f32)
        both = both[:, :K] + both[:, K:]
        d = jnp.dot(
            bgt[:, pl.ds(pl.multiple_of(step * TALL, TALL), TALL)],
            jnp.concatenate(parts_of(both, 2), axis=1),
            preferred_element_type=f32,
        )
        value = value + d[:ROWS16, :K] + d[:ROWS16, K:] + d[ROWS16:, :K] + d[ROWS16:, K:]
        for piece in range(TALL // BLK):
            at = pl.multiple_of(order[step * (TALL // BLK) + piece] * BLK, BLK)
            y = both[BLK * piece : BLK * (piece + 1)]
            product[pl.ds(at, BLK), :] = y
            energy = energy + folded(residual[pl.ds(at, BLK), :] * y)
        return value, energy

    return lax.fori_loop(0, NS // TALL, tall, (jnp.zeros((ROWS16, K), f32), jnp.zeros((SLOT, K), f32)))


class Matrix:
    def __init__(self, source, held, sems):
        self.source, self.held, self.sems = source, held, sems

    def copy(self, part):
        rows = pl.ds(PART * part if isinstance(part, int) else pl.multiple_of(part * PART, PART), PART)
        return pltpu.make_async_copy(self.source.at[rows], self.held.at[rows], self.sems.at[part])

    def start(self, part):
        self.copy(part).start()

    def wait(self, step):
        for part in range(TALL // PART):
            self.copy(step * (TALL // PART) + part).wait()


def put_halves(value, halves, at):
    high, low = parts_of(value, 2)
    halves[pl.ds(pl.multiple_of(at * BLK, BLK), BLK), :K] = high
    halves[pl.ds(pl.multiple_of(at * BLK, BLK), BLK), K:] = low


def invert(order, inverse):
    for block in range(NB):
        inverse[order[block]] = block


def close_product(value, norm, energy, cross, product, pay, faces, copies, pay_held):
    for face in range(4):
        copies.out(product.at[pl.ds(M * face, M)], faces[face])
    pay_held[...] = value[0:PAY]
    pay_held[6:7, :] = jnp.sum(norm, axis=0, keepdims=True)
    pay_held[7:8, :] = jnp.sum(energy, axis=0, keepdims=True)
    pay_held[14:15, :] = jnp.sum(cross, axis=0, keepdims=True)
    for index in range(ROWS):
        copies.out(pay_held, pay.at[index])
    copies.close()


def begin_kernel(
    order, matrix, bgt, bgc, came, own, other, residual, yn, ys, yw, ye, pay,
    inverse, held, bgt_v, bgc_v, came_v, r_v, halves, product, spread, stack, pay_v, sems, tall_sems,
):
    copies, matrix = Copies(sems), Matrix(matrix, held, tall_sems)
    head = [copies.start(came, came_v), copies.start(bgc, bgc_v)]
    body = [copies.start((other, own)[face % 2].at[face // 2], r_v.at[pl.ds(M * face, M)]) for face in range(4)]
    matrix.start(0)
    matrix.start(1)
    turn = [copies.start(bgt, bgt_v)]
    invert(order, inverse)
    wait(head)
    matrix.start(2)
    matrix.start(3)
    stacked, _ = take_values(came_v, stack)
    norm = jnp.zeros((SLOT, K), f32)
    for face in range(4):
        inner = slice(M * face, M * (face + 1))
        spread[0:M, :] = jnp.dot(bgc_v[inner, :], stacked, preferred_element_type=f32)
        wait(body[face : face + 1])

        def block(index, norm, face=face):
            rows = pl.ds(pl.multiple_of(M * face + BLK * index, BLK), BLK)
            r = r_v[rows, :] - spread[pl.ds(pl.multiple_of(BLK * index, BLK), BLK), :]
            r_v[rows, :] = r
            put_halves(r, halves, inverse[M // BLK * face + index])
            return norm + folded(r * r) if face % 2 else norm

        norm = lax.fori_loop(0, M // BLK, block, norm)
        copies.out(r_v.at[inner], residual.at[inner])
    value, energy = schur_product(order, copies, matrix, turn, bgt_v, r_v, halves, product)
    close_product(value, norm, energy, jnp.zeros_like(norm), product, pay, (yn, ys, yw, ye), copies, pay_v)


def image_kernel(which, *refs):
    masks, refs = refs[0], refs[1:]
    count = len(which)
    faces, near, image, (y_v, near_v, sems) = refs[:count], refs[count : 2 * count], refs[2 * count], refs[2 * count + 1 :]
    copies = Copies(sems)
    ready = []
    for index in range(count):
        ready.append([copies.start(faces[index], y_v.at[index]), copies.start(near[index], near_v.at[index])])
    for index, face in enumerate(which):
        wait(ready[index])
        if face % 2:
            y_v[index] = y_v[index] - masks[face] * near_v[index]
        else:
            y_v[index] = masks[face] * (y_v[index] - near_v[index])
        copies.out(y_v.at[index], image.at[index])
    copies.close()


def scalars(first, sums, past):
    norm, energy, cross = sums
    if first:
        return norm, energy, None, norm / energy
    ratio = norm / past[0:1, :]
    curvature = energy + 2.0 * ratio * cross + ratio * ratio * past[1:2, :]
    return norm, curvature, ratio, norm / curvature


def step_kernel(first, *refs):
    order, matrix, bgt, bgc, came, residual, local = refs[:7]
    refs = refs[7:]
    if not first:
        past, moved, image = refs[:3]
        refs = refs[3:]
    new_residual, new_moved, new_past = refs[:3]
    new_faces, pay, refs = refs[3:7], refs[7], refs[8:]
    (inverse, held, bgt_v, bgc_v, came_v, r_v, halves, product, spread, stack, pay_v, sems, tall_sems,
     local_v, moved_v, image_v, past_v, new_past_v) = refs

    copies, matrix = Copies(sems), Matrix(matrix, held, tall_sems)
    head = [copies.start(came, came_v)]
    if not first:
        head.append(copies.start(past, past_v))
    head.append(copies.start(bgc, bgc_v))

    def fetch(pair):
        wide = pl.ds(2 * M * pair, 2 * M)
        part = [copies.start(residual.at[wide], r_v.at[wide])]
        part.append(copies.start(local.at[pl.ds(2 * pair, 2)], local_v.at[pl.ds(2 * pair, 2)]))
        if not first:
            part.append(copies.start(moved.at[wide], moved_v.at[wide]))
            part.append(copies.start(image.at[2 * pair + 1], image_v.at[pl.ds(M * pair, M)]))
        return part

    body = [fetch(0)]
    matrix.start(0)
    matrix.start(1)
    invert(order, inverse)

    wait(head)
    stacked, sums = take_values(came_v, stack)
    norm, curvature, ratio, step = scalars(first, sums, past_v)
    new_past_v[...] = jnp.zeros_like(new_past_v)
    new_past_v[0:1, :] = norm
    new_past_v[1:2, :] = curvature
    if first:
        new_past_v[2:3, :] = step
    else:
        new_past_v[2:3, :] = past_v[2:3, :] + step * ratio
        new_past_v[3:4, :] = step
        new_past_v[4:5, :] = ratio
    copies.out(new_past_v, new_past)
    carry = (jnp.zeros((SLOT, K), f32), jnp.zeros((SLOT, K), f32))
    for pair in range(2):
        wide = pl.ds(2 * M * pair, 2 * M)
        spread[...] = jnp.dot(bgc_v[2 * M * pair : 2 * M * (pair + 1), :], stacked, preferred_element_type=f32)
        wait(body[pair])
        if pair == 0:
            body.append(fetch(1))
            turn = [copies.start(bgt, bgt_v)]

        def block(index, carry, pair=pair):
            norm, cross = carry
            for kind in range(2):
                face = 2 * pair + kind
                rows = pl.ds(pl.multiple_of(M * face + BLK * index, BLK), BLK)
                q = local_v[face, pl.ds(pl.multiple_of(BLK * index, BLK), BLK), :]
                f = q
                if kind and not first:
                    f = q + ratio * image_v[pl.ds(pl.multiple_of(M * pair + BLK * index, BLK), BLK), :]
                q = q - spread[pl.ds(pl.multiple_of(M * kind + BLK * index, BLK), BLK), :]
                if not first:
                    q = q + ratio * moved_v[rows, :]
                moved_v[rows, :] = q
                r = r_v[rows, :] - step * q
                r_v[rows, :] = r
                put_halves(r, halves, inverse[M // BLK * face + index])
                if kind:
                    norm = norm + folded(r * r)
                    cross = cross + folded(r * f)
            return norm, cross

        carry = lax.fori_loop(0, M // BLK, block, carry)
        if pair == 0:
            matrix.start(2)
            matrix.start(3)
        for source, target in ((r_v, new_residual), (moved_v, new_moved)):
            copies.out(source.at[wide], target.at[wide])
    value, energy = schur_product(order, copies, matrix, turn, bgt_v, r_v, halves, product)
    close_product(value, carry[0], energy, carry[1], product, pay, new_faces, copies, pay_v)


def end_kernel(
    bgc, came, residual, first, second, local, past, moved, out_done, out_residual,
    stack, bgc_v, came_v, past_v, r_v, first_v, second_v, local_v, moved_v, x_v, s_v, sems,
):
    copies = Copies(sems)
    head = [copies.start(came, came_v), copies.start(past, past_v)]
    body = []
    for pair in range(2):
        rows, own = pl.ds(M * (2 * pair + 1), M), pl.ds(M * pair, M)
        part = [copies.start(bgc.at[rows], bgc_v.at[own]), copies.start(local.at[pair], local_v.at[own])]
        for source, target in ((residual, r_v), (moved, moved_v), (first, first_v), (second, second_v)):
            part.append(copies.start(source.at[rows], target.at[own]))
        body.append(part)
    wait(head)
    stacked, sums = take_values(came_v, stack)
    _, _, ratio, step = scalars(False, sums, past_v)
    along = step * ratio
    of_second = past_v[3:4, :] + along
    of_first = past_v[2:3, :] + along * past_v[4:5, :]
    for pair in range(2):
        wait(body[pair])
        for block in range(M // BLK):
            inside = slice(BLK * block, BLK * (block + 1))
            own = slice(M * pair + BLK * block, M * pair + BLK * (block + 1))
            q = local_v[own, :] - jnp.dot(bgc_v[own, :], stacked, preferred_element_type=f32)
            q = q + ratio * moved_v[own, :]
            r = r_v[own, :]
            s_v[pair, :, inside] = (r - step * q).T
            x_v[pair, :, inside] = (of_first * first_v[own, :] + of_second * second_v[own, :] + step * r).T
        copies.out(s_v.at[pair], out_residual.at[pair])
        copies.out(x_v.at[pair], out_done.at[pair])
    copies.close()


def shape(*dims, kind=f32):
    return jax.ShapeDtypeStruct(dims, kind)


WORK = [
    pltpu.SMEM((NB,), jnp.int32),
    pltpu.VMEM((NS, NS), bf16),
    pltpu.VMEM((2 * ROWS16, NS), bf16),
    pltpu.VMEM((NS, K), bf16),
    pltpu.VMEM((CHIPS, SLOTS * SLOT, K), f32),
    pltpu.VMEM((NS, K), f32),
    pltpu.VMEM((NS, 2 * K), bf16),
    pltpu.VMEM((NS, K), f32),
    pltpu.VMEM((2 * M, K), f32),
    pltpu.VMEM((K, K), f32),
    pltpu.VMEM((PAY, K), f32),
    pltpu.SemaphoreType.DMA((64,)),
    pltpu.SemaphoreType.DMA((NS // PART,)),
]
MORE = [pltpu.VMEM((4, M, K), f32), pltpu.VMEM((NS, K), f32), pltpu.VMEM((2 * M, K), f32)]
MORE += [pltpu.VMEM((SLOT, K), f32)] * 2
LAST = (
    [pltpu.VMEM((K, K), f32), pltpu.VMEM((2 * M, K), bf16), pltpu.VMEM((CHIPS, SLOTS * SLOT, K), f32)]
    + [pltpu.VMEM((SLOT, K), f32)]
    + [pltpu.VMEM((2 * M, K), f32)] * 5
    + [pltpu.VMEM((2, K, M), f32)] * 2
    + [pltpu.SemaphoreType.DMA((32,))]
)
FACES = [shape(M, K)] * 4


def call(kernel, specs, outs, scratch, flops, place, limit=LIMIT):
    return pl.pallas_call(
        kernel,
        in_specs=specs,
        out_specs=[place] * len(outs),
        out_shape=outs,
        scratch_shapes=scratch,
        compiler_params=limit,
        cost_estimate=pl.CostEstimate(flops=flops, bytes_accessed=1 << 20, transcendentals=0),
    )


def coarse_phase(pay, parts, core, *beside):
    own = lax.all_to_all(pay, "row", 0, 0, tiled=True)
    own, parts, *beside = lax.optimization_barrier((own, parts, *beside))
    other = swapped(own, lambda c: c ^ 1)
    (terms,) = call(
        coarse_kernel,
        [SM, HB, VM, VM],
        [shape(CHIPS, SLOTS * SLOT, K)],
        [
            pltpu.VMEM((2, CHIPS * SLOTS * SLOT, 2 * K), bf16),
            pltpu.VMEM((2 * K, K), f32),
            pltpu.VMEM((CHIPS, SLOTS * SLOT, K), f32),
            pltpu.SemaphoreType.DMA((8,)),
        ],
        10**8,
        HB,
        SMALL,
    )(core, parts, own, other)
    groups = [[2 * chip + which for chip in range(CHIPS)] for which in range(2)]
    return lax.all_to_all(terms, "col", 0, 0, axis_index_groups=groups, tiled=True), *beside


def per_device(schur_blocks, rigid_modes, floating, block_order, coarse_inverse, right_side):
    order = block_order[0, 0]
    row, col = lax.axis_index("row"), lax.axis_index("col")
    core = (col % 2).astype(jnp.int32).reshape(1)
    masks = jnp.stack([row > 0, row < ROWS - 1, col > 0, col < COLS - 1]).astype(f32)
    side = right_side[0, 0]

    modes = (rigid_modes[0, 0] * floating[0, 0].astype(f32)).reshape(MODES, NB, BLK)
    modes = jnp.pad(jnp.transpose(modes, (1, 0, 2)), ((0, 0), (0, SLOT - MODES), (0, 0)))
    near_s = cyclic(modes[0:4], "row", -1)
    near_e = cyclic(modes[8:12], "col", -1)
    own, pay = call(
        start_kernel,
        [SM] + [HB] * 4,
        [shape(2, M, K), shape(ROWS, PAY, K)],
        [
            pltpu.VMEM((NB, SLOT, BLK), f32),
            pltpu.VMEM((2, 4, SLOT, BLK), f32),
            pltpu.VMEM((2, K, M), f32),
            pltpu.VMEM((2, M, K), f32),
            pltpu.VMEM((ROWS16, 2 * M), f32),
            pltpu.VMEM((2 * M, 2 * K), bf16),
            pltpu.VMEM((PAY, K), f32),
            pltpu.SemaphoreType.DMA((16,)),
        ],
        10**8,
        HB,
    )(masks, modes, near_s, near_e, side)
    from_n = cyclic(side[0], "row", 1)
    from_w = cyclic(side[1], "col", 1)
    mine = jnp.transpose(coarse_inverse[:, 0, :, :, :, 0], (1, 0, 3, 2))
    mine = jnp.pad(mine, ((0, 0), (0, SLOT - MODES), (0, 0), (0, SLOT - MODES))).reshape(HALF, 2, SLOT, SLOT * ROWS)
    mine = jnp.concatenate([mine[:, 0], mine[:, 1]], axis=2)
    down = cyclic(jnp.concatenate([mine, modes[4:8]], axis=0), "row", 1)
    up = cyclic(mine, "row", -1)
    down, up, pay = lax.optimization_barrier((down, up, pay))
    lines = jnp.concatenate([mine, down[:HALF], up], axis=0)
    right = cyclic(jnp.concatenate([lines, modes[12:16]], axis=0), "col", 1)
    left = cyclic(lines, "col", -1)
    right, left, from_n, from_w = lax.optimization_barrier((right, left, from_n, from_w))
    far = swapped(jnp.where(core[0] == 0, right[: 3 * HALF], left), lambda c: c ^ 1)
    (parts,) = call(
        table_kernel,
        [SM] + [HB] * 6,
        [shape(2, CHIPS * SLOTS * SLOT, 2 * K, kind=bf16)],
        [pltpu.VMEM((tiles, SLOT, BLK), f32) for tiles in (HALF, HALF + 4, HALF, 3 * HALF + 4, 3 * HALF, 3 * HALF)]
        + [
            pltpu.VMEM((CHIPS * SLOTS * SLOT, 2 * K), f32),
            pltpu.VMEM((2, CHIPS * SLOTS * SLOT, 2 * K), bf16),
            pltpu.SemaphoreType.DMA((16,)),
        ],
        10**6,
        HB,
    )(core, mine, down, up, right, left, far)
    bgt, bgc, other = call(
        modes_kernel,
        [SM] * 2 + [HB] * 7,
        [shape(2 * ROWS16, NS, kind=bf16), shape(NS, K, kind=bf16), shape(2, M, K)],
        [pltpu.VMEM((tiles, SLOT, BLK), f32) for tiles in (NB, 4, 4, 4, 4)]
        + [
            pltpu.VMEM((ROWS16, NS), f32),
            pltpu.VMEM((K, NS), f32),
            pltpu.VMEM((2 * ROWS16, NS), bf16),
            pltpu.VMEM((NS, K), bf16),
            pltpu.VMEM((2, K, M), f32),
            pltpu.VMEM((2, M, K), f32),
            pltpu.SemaphoreType.DMA((16,)),
        ],
        COST,
        HB,
    )(order, masks, modes, down, near_s, right, near_e, from_n, from_w)
    (came,) = coarse_phase(pay, parts, core)

    matrix = schur_blocks[0, 0]
    residual, *faces, pay = call(
        begin_kernel,
        [SM] + [HB] * 6,
        [shape(NS, K)] + FACES + [shape(ROWS, PAY, K)],
        WORK,
        2 * 10**9,
        HB,
    )(order, matrix, bgt, bgc, came, own, other)

    state, residuals = (), [residual]
    for iteration in range(ITERS):
        which = (1, 3) if iteration + 1 == ITERS else (0, 1, 2, 3)
        moves = (("row", 1), ("row", -1), ("col", 1), ("col", -1))
        near = [cyclic(faces[face ^ 1], *moves[face]) for face in which]
        mine = [faces[face] for face in which]
        (local,) = call(
            functools.partial(image_kernel, which),
            [SM] + [HB] * (2 * len(which)),
            [shape(len(which), M, K)],
            [pltpu.VMEM((len(which), M, K), f32)] * 2 + [pltpu.SemaphoreType.DMA((16,))],
            COST,
            HB,
        )(masks, *mine, *near)
        came, local = coarse_phase(pay, parts, core, local)
        if iteration + 1 == ITERS:
            break
        first = iteration == 0
        given = (order, matrix, bgt, bgc, came, residuals[-1], local, *state)
        residual, moved, past, *faces, pay = call(
            functools.partial(step_kernel, first),
            [SM] + [HB] * (len(given) - 1),
            [shape(NS, K), shape(NS, K), shape(SLOT, K)] + FACES + [shape(ROWS, PAY, K)],
            WORK + MORE,
            2 * 10**9,
            HB,
        )(*given)
        state = (past, moved, local)
        residuals.append(residual)

    done, residual = call(
        end_kernel,
        [HB] * 8,
        [shape(2, K, M)] * 2,
        LAST,
        10**8,
        HB,
    )(bgc, came, residuals[2], residuals[0], residuals[1], local, past, moved)
    return (done[None, None], residual[None, None])


def solution(mesh):
    placed = (
        P("row", "col", None, None),
        P("row", "col", None, None),
        P("row", "col"),
        P("row", "col", None),
        P(None, "row", None, None, None, "col"),
        P("row", "col", None, None, None),
    )
    return jax.shard_map(
        per_device,
        mesh=mesh,
        in_specs=placed,
        out_specs=(P("row", "col", None, None, None), P("row", "col", None, None, None)),
        check_vma=False,
    )
```

```python
import functools

import jax
import jax.numpy as jnp
from jax import lax
from jax.experimental import pallas as pl
from jax.experimental.pallas import tpu as pltpu
from jax.sharding import PartitionSpec as P

M = 512
NS = 2048
BLK = 128
NB = 16
K = 128
ROWS = 8
COLS = 32
MODES = 6
ITERS = 3
SLOT = 8
SLOTS = 5
PAY = 40
ROWS16 = 48
TERMS = ((0, 0), (0, 1), (1, 0), (1, 1), (0, 2), (2, 0))
TALL = 1024
PART = 512
CHIPS = 16
HALF = COLS // 2
COST = 2 * 10**10

f32 = jnp.float32
bf16 = jnp.bfloat16
VM = pl.BlockSpec(memory_space=pltpu.VMEM)
SM = pl.BlockSpec(memory_space=pltpu.SMEM)
HB = pl.BlockSpec(memory_space=pltpu.HBM)
LIMIT = pltpu.CompilerParams(vmem_limit_bytes=56 * 1024 * 1024)
SMALL = pltpu.CompilerParams(vmem_limit_bytes=8 * 1024 * 1024)


def cyclic(value, axis, steps):
    count = lax.axis_size(axis)
    return lax.ppermute(value, axis, [(s, (s + steps) % count) for s in range(count)])


def shifted(value, axis, steps):
    count = lax.axis_size(axis)
    initial, last = (max(0, -steps), min(count, count - steps))
    return lax.ppermute(value, axis, [(s, s + steps) for s in range(initial, last)])


def swapped(value, partner):
    return lax.ppermute(value, "col", [(s, partner(s)) for s in range(COLS)])


def parts_of(value, count):
    pieces = []
    for _ in range(count):
        piece = value.astype(bf16)
        pieces.append(piece)
        value = value - piece.astype(f32)
    return pieces


class Copies:
    def __init__(self, sems):
        self.sems, self.used, self.open = sems, 0, []

    def start(self, source, target):
        copy = pltpu.make_async_copy(source, target, self.sems.at[self.used])
        copy.start()
        self.used += 1
        return copy

    def out(self, source, target):
        self.open.append(self.start(source, target))

    def close(self):
        for copy in self.open:
            copy.wait()


def wait(copies):
    for copy in copies:
        copy.wait()


def own_modes(full, own, masks):
    for block in range(NB):
        face = block // (M // BLK)
        value = own[block] * masks[face] if face % 2 == 0 else own[block]
        full[0:SLOT, BLK * block : BLK * (block + 1)] = value


def start_kernel(
    masks, own, near_s, near_e, side, turned, pay,
    own_v, near_v, side_v, turned_v, full, halves, pay_v, sems,
):
    copies = Copies(sems)
    ready = [copies.start(own, own_v), copies.start(near_s, near_v.at[0]), copies.start(near_e, near_v.at[1])]
    faces = [copies.start(side.at[index], side_v.at[index]) for index in range(2)]
    full[...] = jnp.zeros_like(full)
    for index in range(2):
        wait(faces[index : index + 1])
        for block in range(M // BLK):
            rows = slice(M * index + BLK * block, M * index + BLK * (block + 1))
            value = side_v[index, :, BLK * block : BLK * (block + 1)].T
            turned_v[index, BLK * block : BLK * (block + 1), :] = value
            high, low = parts_of(value, 2)
            halves[rows, :K] = high
            halves[rows, K:] = low
        copies.out(turned_v.at[index], turned.at[index])
    wait(ready)
    for index in range(2):
        rows = slice(SLOT * 2 * (index + 1), SLOT * (2 * index + 3))
        for block in range(M // BLK):
            lanes = slice(M * index + BLK * block, M * index + BLK * (block + 1))
            full[0:SLOT, lanes] = own_v[M // BLK * (2 * index + 1) + block]
            full[rows, lanes] = near_v[index, block] * -masks[2 * index + 1]
    pieces = jnp.concatenate(parts_of(full[...], 2), axis=0)
    d = jnp.dot(pieces, halves[...], preferred_element_type=f32)
    pay_v[...] = (d[:ROWS16, :K] + d[:ROWS16, K:] + d[ROWS16:, :K] + d[ROWS16:, K:])[0:PAY]
    for index in range(ROWS):
        copies.out(pay_v, pay.at[index])
    copies.close()


def modes_kernel(
    order, masks, own, down, up, right, left, from_n, from_w, bgt, bgc, other,
    own_v, down_v, up_v, right_v, left_v, full, turned, bgt_v, bgc_v, near_v, other_v, sems,
):
    copies = Copies(sems)
    ready = [copies.start(own, own_v)]
    for source, target in ((up, up_v), (left, left_v)):
        ready.append(copies.start(source, target))
    ready.append(copies.start(down.at[pl.ds(HALF, 4)], down_v))
    ready.append(copies.start(right.at[pl.ds(3 * HALF, 4)], right_v))
    sides = [copies.start(from_n, near_v.at[0]), copies.start(from_w, near_v.at[1])]
    full[...] = jnp.zeros_like(full)
    wait(ready)
    own_modes(full, own_v, masks)
    for slot, near in enumerate((down_v, up_v, right_v, left_v)):
        rows = slice(SLOT * (slot + 1), SLOT * (slot + 2))
        for block in range(M // BLK):
            lanes = slice(M * slot + BLK * block, M * slot + BLK * (block + 1))
            full[rows, lanes] = near[block] * -masks[slot]
    pieces = parts_of(full[...], 3)
    for index, (which, _) in enumerate(TERMS):
        turned[40 * index : 40 * (index + 1), :] = pieces[which][0:40].astype(f32)
    turned[240:256, :] = jnp.zeros((16, NS), f32)
    for block in range(NB):
        for half in range(2):
            piece = turned[BLK * half : BLK * (half + 1), BLK * block : BLK * (block + 1)].T
            bgc_v[BLK * block : BLK * (block + 1), BLK * half : BLK * (half + 1)] = piece.astype(bf16)
    copies.out(bgc_v, bgc)
    for block in range(NB):
        at = pl.multiple_of(order[block] * BLK, BLK)
        for index, piece in enumerate(parts_of(full[:, pl.ds(at, BLK)], 2)):
            bgt_v[ROWS16 * index : ROWS16 * (index + 1), BLK * block : BLK * (block + 1)] = piece
    copies.out(bgt_v, bgt)
    for index in range(2):
        wait(sides[index : index + 1])
        for block in range(M // BLK):
            inside = slice(BLK * block, BLK * (block + 1))
            other_v[index, inside, :] = near_v[index, :, inside].T * -masks[2 * index]
        copies.out(other_v.at[index], other.at[index])
    copies.close()


def table_kernel(
    core, mine, down, up, right, left, far, parts,
    mine_v, down_v, up_v, right_v, left_v, far_v, table, parts_v, sems,
):
    copies = Copies(sems)
    pairs = ((mine, mine_v), (down, down_v), (up, up_v), (right, right_v), (left, left_v), (far, far_v))
    wait([copies.start(source, target) for source, target in pairs])
    first = core[0] == 0
    half = lax.broadcasted_iota(jnp.int32, (SLOT, BLK), 1) < SLOT * ROWS

    @pl.loop(0, CHIPS)
    def _(target):
        at = 2 * target + core[0]
        picks = ((0, at), (1, at), (2, at), (0, jnp.maximum(at - 1, 0)), (0, jnp.minimum(at + 1, COLS - 1)))
        for slot, (line, column) in enumerate(picks):
            two = lax.div(column, 2)
            w, e, f = (ref[HALF * line + two] for ref in (right_v, left_v, far_v))
            m = (mine_v[two], down_v[two], up_v[two])[line]
            on_left = (core[0] == 0) == (slot < 3)
            pairs = ((jnp.where(first, w, f), jnp.where(first, m, w)), (jnp.where(first, e, m), jnp.where(first, f, e)))
            turned = []
            for a, b in pairs:
                across = pltpu.roll(jnp.where(on_left, b, a), SLOT * ROWS, 1)
                turned.append(jnp.where(half, jnp.where(on_left, a, across), jnp.where(on_left, across, b)))
            rows = pl.ds(pl.multiple_of((target * SLOTS + slot) * SLOT, SLOT), SLOT)
            table[rows, :K] = turned[0]
            table[rows, K:] = turned[1]

    for index, piece in enumerate(parts_of(table[...], 2)):
        parts_v[index] = piece
        copies.out(parts_v.at[index], parts.at[index])
    copies.close()


def coarse_kernel(core, parts, own_v, other_v, out, parts_v, entries, out_v, sems):
    copies = Copies(sems)
    table = [copies.start(parts.at[index], parts_v.at[index]) for index in range(2)]
    first = core[0] == 0

    def tile(which, line, slot):
        here = slice(SLOT * slot, SLOT * (slot + 1))
        a, b = own_v[line, here, :], other_v[line, here, :]
        return jnp.where(first, a, b) if which == 0 else jnp.where(first, b, a)

    total = jnp.zeros((2 * SLOT, K), f32)
    for line in range(ROWS):
        for which in range(2):
            value = tile(which, line, 0)
            if line > 0:
                value = value + tile(which, line - 1, 2)
            if line < ROWS - 1:
                value = value + tile(which, line + 1, 1)
            value = value + tile(1 - which, line, 3 + which)
            at = SLOT * (ROWS * (which + 1) + line)
            entries[at : at + SLOT, :] = value
        entries[SLOT * line : SLOT * (line + 1), :] = tile(0, line, 3)
        at = SLOT * (ROWS * 3 + line)
        entries[at : at + SLOT, :] = tile(1, line, 4)
        total = total + own_v[line, : 2 * SLOT, :] + other_v[line, : 2 * SLOT, :]
    both = jnp.concatenate(parts_of(entries[...], 2), axis=1)
    wait(table)
    d = jnp.dot(parts_v[0], both, preferred_element_type=f32)
    e = jnp.dot(parts_v[1], both, preferred_element_type=f32)
    value = e[:, K:] + e[:, :K] + d[:, K:] + d[:, :K]
    for target in range(CHIPS):
        out_v[target] = value[SLOTS * SLOT * target : SLOTS * SLOT * (target + 1)]
        out_v[target, 6:8, :] = total[6:8]
        out_v[target, 14:15, :] = total[14:15]
    copies.out(out_v, out)
    copies.close()


def take_values(came, stack):
    value = came[0]
    for index in range(1, CHIPS):
        value = value + came[index]
    spare = lax.broadcasted_iota(jnp.int32, (SLOT * SLOTS, K), 0) % SLOT >= MODES
    pieces = parts_of(jnp.where(spare, 0.0, value), 3)
    for index, (_, right) in enumerate(TERMS):
        stack[40 * index : 40 * (index + 1), :] = pieces[right].astype(f32)
    stack[240:256, :] = jnp.zeros((16, K), f32)
    return stack[...].astype(bf16), (value[6:7], value[7:8], value[14:15])


def folded(value):
    return jnp.sum(value.reshape(-1, SLOT, K), axis=0)


def schur_product(order, copies, matrix, turn, bgt, residual, halves, product):
    wait(turn)

    def tall(step, carry):
        value, energy = carry
        matrix.wait(step)
        rows = matrix.held[pl.ds(pl.multiple_of(step * TALL, TALL), TALL), :]
        both = jnp.dot(rows, halves[...], preferred_element_type=f32)
        both = both[:, :K] + both[:, K:]
        d = jnp.dot(
            bgt[:, pl.ds(pl.multiple_of(step * TALL, TALL), TALL)],
            jnp.concatenate(parts_of(both, 2), axis=1),
            preferred_element_type=f32,
        )
        value = value + d[:ROWS16, :K] + d[:ROWS16, K:] + d[ROWS16:, :K] + d[ROWS16:, K:]
        for piece in range(TALL // BLK):
            at = pl.multiple_of(order[step * (TALL // BLK) + piece] * BLK, BLK)
            y = both[BLK * piece : BLK * (piece + 1)]
            product[pl.ds(at, BLK), :] = y
            energy = energy + folded(residual[pl.ds(at, BLK), :] * y)
        return value, energy

    return lax.fori_loop(0, NS // TALL, tall, (jnp.zeros((ROWS16, K), f32), jnp.zeros((SLOT, K), f32)))


class Matrix:
    def __init__(self, source, held, sems):
        self.source, self.held, self.sems = source, held, sems

    def copy(self, part):
        rows = pl.ds(PART * part if isinstance(part, int) else pl.multiple_of(part * PART, PART), PART)
        return pltpu.make_async_copy(self.source.at[rows], self.held.at[rows], self.sems.at[part])

    def start(self, part):
        self.copy(part).start()

    def wait(self, step):
        for part in range(TALL // PART):
            self.copy(step * (TALL // PART) + part).wait()


def put_halves(value, halves, at):
    high, low = parts_of(value, 2)
    halves[pl.ds(pl.multiple_of(at * BLK, BLK), BLK), :K] = high
    halves[pl.ds(pl.multiple_of(at * BLK, BLK), BLK), K:] = low


def invert(order, inverse):
    for block in range(NB):
        inverse[order[block]] = block


def close_product(value, norm, energy, cross, product, pay, faces, copies, pay_held):
    for face in range(4):
        copies.out(product.at[pl.ds(M * face, M)], faces[face])
    pay_held[...] = value[0:PAY]
    pay_held[6:7, :] = jnp.sum(norm, axis=0, keepdims=True)
    pay_held[7:8, :] = jnp.sum(energy, axis=0, keepdims=True)
    pay_held[14:15, :] = jnp.sum(cross, axis=0, keepdims=True)
    for index in range(ROWS):
        copies.out(pay_held, pay.at[index])
    copies.close()


def begin_kernel(
    order, matrix, bgt, bgc, came, own, other, residual, yn, ys, yw, ye, pay,
    inverse, held, bgt_v, bgc_v, came_v, r_v, halves, product, spread, stack, pay_v, sems, tall_sems,
):
    copies, matrix = Copies(sems), Matrix(matrix, held, tall_sems)
    head = [copies.start(came, came_v), copies.start(bgc, bgc_v)]
    body = [copies.start((other, own)[face % 2].at[face // 2], r_v.at[pl.ds(M * face, M)]) for face in range(4)]
    matrix.start(0)
    matrix.start(1)
    turn = [copies.start(bgt, bgt_v)]
    invert(order, inverse)
    wait(head)
    matrix.start(2)
    matrix.start(3)
    stacked, _ = take_values(came_v, stack)
    norm = jnp.zeros((SLOT, K), f32)
    for face in range(4):
        inner = slice(M * face, M * (face + 1))
        spread[0:M, :] = jnp.dot(bgc_v[inner, :], stacked, preferred_element_type=f32)
        wait(body[face : face + 1])

        def block(index, norm, face=face):
            rows = pl.ds(pl.multiple_of(M * face + BLK * index, BLK), BLK)
            r = r_v[rows, :] - spread[pl.ds(pl.multiple_of(BLK * index, BLK), BLK), :]
            r_v[rows, :] = r
            put_halves(r, halves, inverse[M // BLK * face + index])
            return norm + folded(r * r) if face % 2 else norm

        norm = lax.fori_loop(0, M // BLK, block, norm)
        copies.out(r_v.at[inner], residual.at[inner])
    value, energy = schur_product(order, copies, matrix, turn, bgt_v, r_v, halves, product)
    close_product(value, norm, energy, jnp.zeros_like(norm), product, pay, (yn, ys, yw, ye), copies, pay_v)


def image_kernel(which, *refs):
    masks, refs = refs[0], refs[1:]
    count = len(which)
    faces, near, image, (y_v, near_v, sems) = refs[:count], refs[count : 2 * count], refs[2 * count], refs[2 * count + 1 :]
    copies = Copies(sems)
    ready = []
    for index in range(count):
        ready.append([copies.start(faces[index], y_v.at[index]), copies.start(near[index], near_v.at[index])])
    for index, face in enumerate(which):
        wait(ready[index])
        if face % 2:
            y_v[index] = y_v[index] - masks[face] * near_v[index]
        else:
            y_v[index] = masks[face] * (y_v[index] - near_v[index])
        copies.out(y_v.at[index], image.at[index])
    copies.close()


def scalars(first, sums, past):
    norm, energy, cross = sums
    if first:
        return norm, energy, None, norm / energy
    ratio = norm / past[0:1, :]
    curvature = energy + 2.0 * ratio * cross + ratio * ratio * past[1:2, :]
    return norm, curvature, ratio, norm / curvature


def step_kernel(first, *refs):
    order, matrix, bgt, bgc, came, residual, local = refs[:7]
    refs = refs[7:]
    if not first:
        past, moved, image = refs[:3]
        refs = refs[3:]
    new_residual, new_moved, new_past = refs[:3]
    new_faces, pay, refs = refs[3:7], refs[7], refs[8:]
    (inverse, held, bgt_v, bgc_v, came_v, r_v, halves, product, spread, stack, pay_v, sems, tall_sems,
     local_v, moved_v, image_v, past_v, new_past_v) = refs

    copies, matrix = Copies(sems), Matrix(matrix, held, tall_sems)
    head = [copies.start(came, came_v)]
    if not first:
        head.append(copies.start(past, past_v))
    head.append(copies.start(bgc, bgc_v))

    def fetch(pair):
        wide = pl.ds(2 * M * pair, 2 * M)
        part = [copies.start(residual.at[wide], r_v.at[wide])]
        part.append(copies.start(local.at[pl.ds(2 * pair, 2)], local_v.at[pl.ds(2 * pair, 2)]))
        if not first:
            part.append(copies.start(moved.at[wide], moved_v.at[wide]))
            part.append(copies.start(image.at[2 * pair + 1], image_v.at[pl.ds(M * pair, M)]))
        return part

    body = [fetch(0)]
    matrix.start(0)
    matrix.start(1)
    invert(order, inverse)

    wait(head)
    stacked, sums = take_values(came_v, stack)
    norm, curvature, ratio, step = scalars(first, sums, past_v)
    new_past_v[...] = jnp.zeros_like(new_past_v)
    new_past_v[0:1, :] = norm
    new_past_v[1:2, :] = curvature
    if first:
        new_past_v[2:3, :] = step
    else:
        new_past_v[2:3, :] = past_v[2:3, :] + step * ratio
        new_past_v[3:4, :] = step
        new_past_v[4:5, :] = ratio
    copies.out(new_past_v, new_past)
    carry = (jnp.zeros((SLOT, K), f32), jnp.zeros((SLOT, K), f32))
    for pair in range(2):
        wide = pl.ds(2 * M * pair, 2 * M)
        spread[...] = jnp.dot(bgc_v[2 * M * pair : 2 * M * (pair + 1), :], stacked, preferred_element_type=f32)
        wait(body[pair])
        if pair == 0:
            body.append(fetch(1))
            turn = [copies.start(bgt, bgt_v)]

        def block(index, carry, pair=pair):
            norm, cross = carry
            for kind in range(2):
                face = 2 * pair + kind
                rows = pl.ds(pl.multiple_of(M * face + BLK * index, BLK), BLK)
                q = local_v[face, pl.ds(pl.multiple_of(BLK * index, BLK), BLK), :]
                f = q
                if kind and not first:
                    f = q + ratio * image_v[pl.ds(pl.multiple_of(M * pair + BLK * index, BLK), BLK), :]
                q = q - spread[pl.ds(pl.multiple_of(M * kind + BLK * index, BLK), BLK), :]
                if not first:
                    q = q + ratio * moved_v[rows, :]
                moved_v[rows, :] = q
                r = r_v[rows, :] - step * q
                r_v[rows, :] = r
                put_halves(r, halves, inverse[M // BLK * face + index])
                if kind:
                    norm = norm + folded(r * r)
                    cross = cross + folded(r * f)
            return norm, cross

        carry = lax.fori_loop(0, M // BLK, block, carry)
        if pair == 0:
            matrix.start(2)
            matrix.start(3)
        for source, target in ((r_v, new_residual), (moved_v, new_moved)):
            copies.out(source.at[wide], target.at[wide])
    value, energy = schur_product(order, copies, matrix, turn, bgt_v, r_v, halves, product)
    close_product(value, carry[0], energy, carry[1], product, pay, new_faces, copies, pay_v)


def end_kernel(
    bgc, came, residual, first, second, local, past, moved, out_done, out_residual,
    stack, bgc_v, came_v, past_v, r_v, first_v, second_v, local_v, moved_v, x_v, s_v, sems,
):
    copies = Copies(sems)
    head = [copies.start(came, came_v), copies.start(past, past_v)]
    body = []
    for pair in range(2):
        rows, own = pl.ds(M * (2 * pair + 1), M), pl.ds(M * pair, M)
        part = [copies.start(bgc.at[rows], bgc_v.at[own]), copies.start(local.at[pair], local_v.at[own])]
        for source, target in ((residual, r_v), (moved, moved_v), (first, first_v), (second, second_v)):
            part.append(copies.start(source.at[rows], target.at[own]))
        body.append(part)
    wait(head)
    stacked, sums = take_values(came_v, stack)
    _, _, ratio, step = scalars(False, sums, past_v)
    along = step * ratio
    of_second = past_v[3:4, :] + along
    of_first = past_v[2:3, :] + along * past_v[4:5, :]
    for pair in range(2):
        wait(body[pair])
        for block in range(M // BLK):
            inside = slice(BLK * block, BLK * (block + 1))
            own = slice(M * pair + BLK * block, M * pair + BLK * (block + 1))
            q = local_v[own, :] - jnp.dot(bgc_v[own, :], stacked, preferred_element_type=f32)
            q = q + ratio * moved_v[own, :]
            r = r_v[own, :]
            s_v[pair, :, inside] = (r - step * q).T
            x_v[pair, :, inside] = (of_first * first_v[own, :] + of_second * second_v[own, :] + step * r).T
        copies.out(s_v.at[pair], out_residual.at[pair])
        copies.out(x_v.at[pair], out_done.at[pair])
    copies.close()


def shape(*dims, kind=f32):
    return jax.ShapeDtypeStruct(dims, kind)


WORK = [
    pltpu.SMEM((NB,), jnp.int32),
    pltpu.VMEM((NS, NS), bf16),
    pltpu.VMEM((2 * ROWS16, NS), bf16),
    pltpu.VMEM((NS, 2 * K), bf16),
    pltpu.VMEM((CHIPS, SLOTS * SLOT, K), f32),
    pltpu.VMEM((NS, K), f32),
    pltpu.VMEM((NS, 2 * K), bf16),
    pltpu.VMEM((NS, K), f32),
    pltpu.VMEM((2 * M, K), f32),
    pltpu.VMEM((256, K), f32),
    pltpu.VMEM((PAY, K), f32),
    pltpu.SemaphoreType.DMA((64,)),
    pltpu.SemaphoreType.DMA((NS // PART,)),
]
MORE = [pltpu.VMEM((4, M, K), f32), pltpu.VMEM((NS, K), f32), pltpu.VMEM((2 * M, K), f32)]
MORE += [pltpu.VMEM((SLOT, K), f32)] * 2
LAST = (
    [pltpu.VMEM((256, K), f32), pltpu.VMEM((2 * M, 2 * K), bf16), pltpu.VMEM((CHIPS, SLOTS * SLOT, K), f32)]
    + [pltpu.VMEM((SLOT, K), f32)]
    + [pltpu.VMEM((2 * M, K), f32)] * 5
    + [pltpu.VMEM((2, K, M), f32)] * 2
    + [pltpu.SemaphoreType.DMA((32,))]
)
FACES = [shape(M, K)] * 4


def call(kernel, specs, outs, scratch, flops, place, limit=LIMIT):
    return pl.pallas_call(
        kernel,
        in_specs=specs,
        out_specs=[place] * len(outs),
        out_shape=outs,
        scratch_shapes=scratch,
        compiler_params=limit,
        cost_estimate=pl.CostEstimate(flops=flops, bytes_accessed=1 << 20, transcendentals=0),
    )


def coarse_phase(pay, parts, core, *beside):
    own = lax.all_to_all(pay, "row", 0, 0, tiled=True)
    own, parts, *beside = lax.optimization_barrier((own, parts, *beside))
    other = swapped(own, lambda c: c ^ 1)
    (terms,) = call(
        coarse_kernel,
        [SM, HB, VM, VM],
        [shape(CHIPS, SLOTS * SLOT, K)],
        [
            pltpu.VMEM((2, CHIPS * SLOTS * SLOT, 2 * K), bf16),
            pltpu.VMEM((2 * K, K), f32),
            pltpu.VMEM((CHIPS, SLOTS * SLOT, K), f32),
            pltpu.SemaphoreType.DMA((8,)),
        ],
        10**8,
        HB,
        SMALL,
    )(core, parts, own, other)
    groups = [[2 * chip + which for chip in range(CHIPS)] for which in range(2)]
    return lax.all_to_all(terms, "col", 0, 0, axis_index_groups=groups, tiled=True), *beside


def per_device(schur_blocks, rigid_modes, floating, block_order, coarse_inverse, right_side):
    order = block_order[0, 0]
    row, col = lax.axis_index("row"), lax.axis_index("col")
    core = (col % 2).astype(jnp.int32).reshape(1)
    masks = jnp.stack([row > 0, row < ROWS - 1, col > 0, col < COLS - 1]).astype(f32)
    side = right_side[0, 0]

    modes = (rigid_modes[0, 0] * floating[0, 0].astype(f32)).reshape(MODES, NB, BLK)
    modes = jnp.pad(jnp.transpose(modes, (1, 0, 2)), ((0, 0), (0, SLOT - MODES), (0, 0)))
    near_s = cyclic(modes[0:4], "row", -1)
    near_e = cyclic(modes[8:12], "col", -1)
    own, pay = call(
        start_kernel,
        [SM] + [HB] * 4,
        [shape(2, M, K), shape(ROWS, PAY, K)],
        [
            pltpu.VMEM((NB, SLOT, BLK), f32),
            pltpu.VMEM((2, 4, SLOT, BLK), f32),
            pltpu.VMEM((2, K, M), f32),
            pltpu.VMEM((2, M, K), f32),
            pltpu.VMEM((ROWS16, 2 * M), f32),
            pltpu.VMEM((2 * M, 2 * K), bf16),
            pltpu.VMEM((PAY, K), f32),
            pltpu.SemaphoreType.DMA((16,)),
        ],
        10**8,
        HB,
    )(masks, modes, near_s, near_e, side)
    from_n = cyclic(side[0], "row", 1)
    from_w = cyclic(side[1], "col", 1)
    mine = jnp.transpose(coarse_inverse[:, 0, :, :, :, 0], (1, 0, 3, 2))
    mine = jnp.pad(mine, ((0, 0), (0, SLOT - MODES), (0, 0), (0, SLOT - MODES))).reshape(HALF, 2, SLOT, SLOT * ROWS)
    mine = jnp.concatenate([mine[:, 0], mine[:, 1]], axis=2)
    down = cyclic(jnp.concatenate([mine, modes[4:8]], axis=0), "row", 1)
    up = cyclic(mine, "row", -1)
    down, up, pay = lax.optimization_barrier((down, up, pay))
    lines = jnp.concatenate([mine, down[:HALF], up], axis=0)
    right = cyclic(jnp.concatenate([lines, modes[12:16]], axis=0), "col", 1)
    left = cyclic(lines, "col", -1)
    right, left, from_n, from_w = lax.optimization_barrier((right, left, from_n, from_w))
    far = swapped(jnp.where(core[0] == 0, right[: 3 * HALF], left), lambda c: c ^ 1)
    (parts,) = call(
        table_kernel,
        [SM] + [HB] * 6,
        [shape(2, CHIPS * SLOTS * SLOT, 2 * K, kind=bf16)],
        [pltpu.VMEM((tiles, SLOT, BLK), f32) for tiles in (HALF, HALF + 4, HALF, 3 * HALF + 4, 3 * HALF, 3 * HALF)]
        + [
            pltpu.VMEM((CHIPS * SLOTS * SLOT, 2 * K), f32),
            pltpu.VMEM((2, CHIPS * SLOTS * SLOT, 2 * K), bf16),
            pltpu.SemaphoreType.DMA((16,)),
        ],
        10**6,
        HB,
    )(core, mine, down, up, right, left, far)
    bgt, bgc, other = call(
        modes_kernel,
        [SM] * 2 + [HB] * 7,
        [shape(2 * ROWS16, NS, kind=bf16), shape(NS, 2 * K, kind=bf16), shape(2, M, K)],
        [pltpu.VMEM((tiles, SLOT, BLK), f32) for tiles in (NB, 4, 4, 4, 4)]
        + [
            pltpu.VMEM((ROWS16, NS), f32),
            pltpu.VMEM((256, NS), f32),
            pltpu.VMEM((2 * ROWS16, NS), bf16),
            pltpu.VMEM((NS, 2 * K), bf16),
            pltpu.VMEM((2, K, M), f32),
            pltpu.VMEM((2, M, K), f32),
            pltpu.SemaphoreType.DMA((16,)),
        ],
        COST,
        HB,
    )(order, masks, modes, down, near_s, right, near_e, from_n, from_w)
    (came,) = coarse_phase(pay, parts, core)

    matrix = schur_blocks[0, 0]
    residual, *faces, pay = call(
        begin_kernel,
        [SM] + [HB] * 6,
        [shape(NS, K)] + FACES + [shape(ROWS, PAY, K)],
        WORK,
        2 * 10**9,
        HB,
    )(order, matrix, bgt, bgc, came, own, other)

    state, residuals = (), [residual]
    for iteration in range(ITERS):
        which = (1, 3) if iteration + 1 == ITERS else (0, 1, 2, 3)
        moves = (("row", 1), ("row", -1), ("col", 1), ("col", -1))
        near = [cyclic(faces[face ^ 1], *moves[face]) for face in which]
        mine = [faces[face] for face in which]
        (local,) = call(
            functools.partial(image_kernel, which),
            [SM] + [HB] * (2 * len(which)),
            [shape(len(which), M, K)],
            [pltpu.VMEM((len(which), M, K), f32)] * 2 + [pltpu.SemaphoreType.DMA((16,))],
            COST,
            HB,
        )(masks, *mine, *near)
        came, local = coarse_phase(pay, parts, core, local)
        if iteration + 1 == ITERS:
            break
        first = iteration == 0
        given = (order, matrix, bgt, bgc, came, residuals[-1], local, *state)
        residual, moved, past, *faces, pay = call(
            functools.partial(step_kernel, first),
            [SM] + [HB] * (len(given) - 1),
            [shape(NS, K), shape(NS, K), shape(SLOT, K)] + FACES + [shape(ROWS, PAY, K)],
            WORK + MORE,
            2 * 10**9,
            HB,
        )(*given)
        state = (past, moved, local)
        residuals.append(residual)

    done, residual = call(
        end_kernel,
        [HB] * 8,
        [shape(2, K, M)] * 2,
        LAST,
        10**8,
        HB,
    )(bgc, came, residuals[2], residuals[0], residuals[1], local, past, moved)
    return (done[None, None], residual[None, None])


def solution(mesh):
    placed = (
        P("row", "col", None, None),
        P("row", "col", None, None),
        P("row", "col"),
        P("row", "col", None),
        P(None, "row", None, None, None, "col"),
        P("row", "col", None, None, None),
    )
    return jax.shard_map(
        per_device,
        mesh=mesh,
        in_specs=placed,
        out_specs=(P("row", "col", None, None, None), P("row", "col", None, None, None)),
        check_vma=False,
    )
```
